32 devices in a mesh: gx: 16 (over z, y, core), yz: 2 (over x).
Axes of the slice: x: 2, y: 2, z: 4, core: 2. Of those that a mesh axis runs over, the one named last changes fastest.
Arguments:
- log_conductivity: float32 [128, 128, 128], P('gx', 'yz'), may hold values from 4.5 to 7.5
- storage: float32 [128, 128, 128], P('gx', 'yz'), may hold values from 0.3 to 1.5
- head: float32 [128, 128, 128], P('gx', 'yz'), may hold values from -6 to 6
- well_east: int32 [32], replicated, may hold values from 0 to 127
- well_north: int32 [32], replicated, may hold values from 0 to 127
- well_depth: int32 [32], replicated, may hold values from 0 to 127
- pump_rates: float32 [32], replicated, may hold values from -3000 to 3000
- probe_east: int32 [1024], replicated, may hold values from 0 to 127
- probe_north: int32 [1024], replicated, may hold values from 0 to 127
- probe_depth: int32 [1024], replicated, may hold values from 0 to 127
- probe_heads: float32 [1024], replicated, may hold values from -6 to 6
Outputs:
- head_next: float32 [128, 128, 128], P('gx', 'yz')
- log_conductivity_gradient: float32 [128, 128, 128], P('gx', 'yz')
- misfits: float32 [1024], replicated
The draws below stay inside these ranges and needn't reach their ends.
All inputs are finite; a program needn't handle non-finite values.
Results may differ from the reference program's by a relative error of at most 0.0028.
Values sent between devices are 32-bit elements; how exact they have to be, the bound alone decides.
No kernel may reach another device: no remote copies, remote signals or barrier semaphores. Data moves between devices by JAX's collectives and lax.ppermute only.
A program may use at most 64 MiB of HBM per device.

```python
import math
import jax
import jax.numpy as jnp
from jax import lax

NZ = 128
NW = 32
NO = 1024
NX = 128
NY = 128


def with_ends(values, key, smallest, largest):
    shape = values.shape
    spot = [jax.random.randint(jax.random.fold_in(key, axis), (), 0, shape[axis]) for axis in range(len(shape))]
    values = values.at[tuple(spot)].set(smallest)
    longest = shape.index(max(shape))
    spot[longest] = (spot[longest] + 1) % shape[longest]
    return values.at[tuple(spot)].set(largest)


def steps_of(own_key, shape, shards, smallest, high):
    loudness, own = 1.0, jax.random.fold_in(own_key, 6)
    for dim, parts in shards:
        draws = jnp.exp(jax.random.uniform(jax.random.fold_in(own, dim), (parts,), jnp.float32, smallest / len(shards), high / len(shards)))
        loudness = loudness * jnp.repeat(draws, shape[dim] // parts).reshape([-1 if axis == dim else 1 for axis in range(len(shape))])
    return loudness


def bell_draw(own_key, extent, width, bound, cuts=(), kind=jnp.bfloat16):
    values = jax.random.normal(own_key, extent, jnp.float32) * width
    if len(cuts) > 0:
        values = steps_of(own_key, extent, cuts, -0.22, 0.18) * values
    return jnp.clip(values, min=-bound, max=bound).astype(kind)


def setup_inputs(seed: int = 0) -> dict:
    streams_of = jax.random.split(jax.random.key(seed), 12)
    log_conductivity = jnp.clip(4.5 + 3.0 * jax.random.uniform(streams_of[0], (NX, NY, NZ), jnp.float32) ** steps_of(streams_of[0], (NX, NY, NZ), ((0, 16), (1, 2)), -0.2, 0.2), 4.5, 7.5)
    storage = jnp.clip(jnp.exp(math.log(1.5) - 1.60943787 * jax.random.uniform(streams_of[1], (NX, NY, NZ), jnp.float32) ** steps_of(streams_of[1], (NX, NY, NZ), ((0, 16), (1, 2)), -0.2, 0.2)), 0.3, 1.5)
    head = bell_draw(streams_of[2], (NX, NY, NZ), 1.0, 6.0, ((0, 16), (1, 2)), jnp.float32)
    well_east = with_ends(jax.random.randint(streams_of[3], (NW,), 0, NX), jax.random.fold_in(streams_of[3], 1), 0, NX - 1).astype(jnp.int32)
    well_north = with_ends(jax.random.randint(streams_of[4], (NW,), 0, NY), jax.random.fold_in(streams_of[4], 1), 0, NY - 1).astype(jnp.int32)
    well_depth = with_ends(jax.random.randint(streams_of[5], (NW,), 0, NZ), jax.random.fold_in(streams_of[5], 1), 0, NZ - 1).astype(jnp.int32)
    pump_rates = jnp.clip(jax.random.uniform(streams_of[6], (NW,), jnp.float32, -3000.0, 3000.0), -3000.0, 3000.0)
    probe_east = with_ends(jax.random.randint(streams_of[7], (NO,), 0, NX), jax.random.fold_in(streams_of[7], 1), 0, NX - 1).astype(jnp.int32)
    probe_north = with_ends(jax.random.randint(streams_of[8], (NO,), 0, NY), jax.random.fold_in(streams_of[8], 1), 0, NY - 1).astype(jnp.int32)
    probe_depth = with_ends(jax.random.randint(streams_of[9], (NO,), 0, NZ), jax.random.fold_in(streams_of[9], 1), 0, NZ - 1).astype(jnp.int32)
    probe_heads = bell_draw(streams_of[10], (NO,), 1.0, 6.0, (), jnp.float32)
    return dict(log_conductivity=log_conductivity, storage=storage, head=head, well_east=well_east, well_north=well_north, well_depth=well_depth, pump_rates=pump_rates, probe_east=probe_east, probe_north=probe_north, probe_depth=probe_depth, probe_heads=probe_heads)


misfit_weight = 100.0


def harmonic(left_cond, right_cond):
    return 2.0 * left_cond * right_cond / (left_cond + right_cond)


def pad_zeros(values, along):
    widths = [(0, 0)] * values.ndim
    widths[along] = (1, 1)
    return jnp.pad(values, widths)


def face_bands(padded, along):
    count = padded.shape[along] - 2
    faces = harmonic(lax.slice_in_dim(padded, 0, count + 1, axis=along),
                     lax.slice_in_dim(padded, 1, count + 2, axis=along))
    return (lax.slice_in_dim(faces, 0, count, axis=along),
            lax.slice_in_dim(faces, 1, count + 1, axis=along))


def face_sum(padded_cond, padded_adjoint, padded_head, along):
    count = padded_cond.shape[along] - 2
    left_cond = lax.slice_in_dim(padded_cond, 0, count + 1, axis=along)
    right_cond = lax.slice_in_dim(padded_cond, 1, count + 2, axis=along)
    left_adj = lax.slice_in_dim(padded_adjoint, 0, count + 1, axis=along)
    right_adj = lax.slice_in_dim(padded_adjoint, 1, count + 2, axis=along)
    left_head = lax.slice_in_dim(padded_head, 0, count + 1, axis=along)
    right_head = lax.slice_in_dim(padded_head, 1, count + 2, axis=along)
    product = -(left_adj - right_adj) * (left_head - right_head)
    total = left_cond + right_cond
    square = total * total
    to_left = product * 2.0 * right_cond * right_cond / square
    to_right = product * 2.0 * left_cond * left_cond / square
    return (lax.slice_in_dim(to_left, 1, count + 1, axis=along)
            + lax.slice_in_dim(to_right, 0, count, axis=along))


def thomas(lower_band, main_band, upper_band, right_side, along):
    below = jnp.moveaxis(lower_band, along, 0)
    middle = jnp.moveaxis(main_band, along, 0)
    above = jnp.moveaxis(upper_band, along, 0)
    source = jnp.moveaxis(right_side, along, 0)

    def forward(carry, row):
        ratio_prev, value_prev = carry
        row_below, row_middle, row_above, row_source = row
        pivot = row_middle - row_below * ratio_prev
        ratio = row_above / pivot
        value = (row_source - row_below * value_prev) / pivot
        return (ratio, value), (ratio, value)

    nothing = jnp.zeros_like(source[0])
    final_carry, (ratios, values) = lax.scan(forward, (nothing, nothing), (below, middle, above, source))

    def backward(after, row):
        ratio, value = row
        result = value - ratio * after
        return result, result

    last_value, solved = lax.scan(backward, nothing, (ratios, values), reverse=True)
    return jnp.moveaxis(solved, 0, along)


def reference(log_conductivity, storage, head, well_east, well_north, well_depth, pump_rates,
              probe_east, probe_north, probe_depth, probe_heads):
    conduct = jnp.exp(log_conductivity)

    def solve_lines(source, along):
        lower_face, upper_face = face_bands(pad_zeros(conduct, along), along)
        return thomas(-lower_face, storage + lower_face + upper_face, -upper_face, source, along)

    sources = jnp.zeros_like(head).at[well_east, well_north, well_depth].add(pump_rates)
    head_first = solve_lines(storage * head + sources, 0)
    head_second = solve_lines(storage * head_first, 1)
    head_next = solve_lines(storage * head_second, 2)
    misfits = head_next[probe_east, probe_north, probe_depth] - probe_heads
    adjoint_source = jnp.zeros_like(head).at[probe_east, probe_north, probe_depth].add(misfit_weight * misfits)
    adjoint_third = solve_lines(adjoint_source, 2)
    adjoint_second = solve_lines(storage * adjoint_third, 1)
    adjoint_first = solve_lines(storage * adjoint_second, 0)
    terms = face_sum(pad_zeros(conduct, 0), pad_zeros(adjoint_first, 0), pad_zeros(head_first, 0), 0)
    terms = terms + face_sum(pad_zeros(conduct, 1), pad_zeros(adjoint_second, 1), pad_zeros(head_second, 1), 1)
    terms = terms + face_sum(pad_zeros(conduct, 2), pad_zeros(adjoint_third, 2), pad_zeros(head_next, 2), 2)
    return head_next, conduct * terms, misfits
```

```python
import jax
import jax.numpy as jnp
from jax import lax
from jax.experimental import pallas as pl
from jax.experimental.pallas import tpu as pltpu
from jax.sharding import PartitionSpec as P


misfit_weight = 100.0
lanes = 128
chunk = 8


def harmonic(left_cond, right_cond):
    return 2.0 * left_cond * right_cond / (left_cond + right_cond)


def eliminate(entry, links, grounds, loads):
    near_ground = near_load = far_ground = far_load = None
    steps = []
    for link, ground, load in zip(links, grounds, loads):
        if far_ground is not None:
            ground, load = ground + far_ground, load + far_load
        inverse = 1.0 / (entry + link + ground)
        to_near, to_far = entry * inverse, link * inverse
        far_ground, far_load = to_far * ground, to_far * load
        if near_ground is None:
            near_ground, near_load = to_near * ground, to_near * load
        else:
            near_ground, near_load = near_ground + to_near * ground, near_load + to_near * load
        steps.append((inverse, to_near, to_far, inverse * load))
        entry = to_near * link
    return (entry, near_ground, far_ground, near_load, far_load), steps


def eliminate_loads(factors, loads):
    near_load = far_load = None
    scaled = []
    for (inverse, to_near, to_far), load in zip(factors, loads):
        if far_load is not None:
            load = load + far_load
        far_load = to_far * load
        near_load = to_near * load if near_load is None else near_load + to_near * load
        scaled.append(inverse * load)
    return near_load, far_load, scaled


def expand(steps, near, far):
    values = []
    for _, to_near, to_far, scaled in reversed(steps):
        far = scaled + to_near * near + to_far * far
        values.append(far)
    return values[::-1]


def combine(blocks):
    pairs = list(zip(blocks[:-1], blocks[1:]))
    (entry, near_ground, far_ground, near_load, far_load), steps = eliminate(
        blocks[0][0],
        [after[0] for _, after in pairs],
        [before[2] + after[1] for before, after in pairs],
        [before[4] + after[3] for before, after in pairs],
    )
    joined = (
        entry,
        blocks[0][1] + near_ground,
        blocks[-1][2] + far_ground,
        blocks[0][3] + near_load,
        blocks[-1][4] + far_load,
    )
    return joined, steps


def combine_loads(blocks, factors):
    near_load, far_load, scaled = eliminate_loads(
        factors, [before[1] + after[0] for before, after in zip(blocks[:-1], blocks[1:])]
    )
    return (blocks[0][0] + near_load, blocks[-1][1] + far_load), scaled


def with_scaled(factors, scaled):
    return [factor + (value,) for factor, value in zip(factors, scaled)]


def factors_of(ref):
    return [(ref[i, 0], ref[i, 1], ref[i, 2]) for i in range(ref.shape[0])]


def steps_of(ref):
    return [(None, ref[i, 1], ref[i, 2], ref[i, 3]) for i in range(ref.shape[0])]


def keep_steps(ref, steps):
    for i, step in enumerate(steps):
        for j, value in enumerate(step):
            ref[i, j] = value


def face_gradient(left_cond, right_cond, adjoint_drop, head_drop):
    total = 1.0 / (left_cond + right_cond)
    flow = -(adjoint_drop * head_drop) * (2.0 * left_cond * right_cond * total) * total
    return flow * right_cond, flow * left_cond


def exact_parts(values):
    parts = []
    for _ in range(3):
        part = values.astype(jnp.bfloat16)
        parts.append(part)
        values = values - part.astype(jnp.float32)
    return parts


def run(body, outs, ins, scratch=(), smem=(), flops=1000000, limit=48):
    shapes = [jax.ShapeDtypeStruct(shape, jnp.float32) for shape in outs]
    size = 4 * (sum(x.size for x in ins) + sum(x.size for x in shapes))
    return pl.pallas_call(
        body,
        out_shape=shapes,
        in_specs=[pl.BlockSpec(memory_space=pltpu.VMEM)] * len(ins),
        out_specs=[pl.BlockSpec(memory_space=pltpu.VMEM)] * len(outs),
        scratch_shapes=[pltpu.VMEM(shape, kind) for shape, kind in scratch],
        compiler_params=pltpu.CompilerParams(vmem_limit_bytes=limit * 1024 * 1024),
        cost_estimate=pl.CostEstimate(flops=flops, bytes_accessed=size, transcendentals=0),
    )(*ins)


f32 = jnp.float32


def place(scratch, arrivals, stride):
    count = len(arrivals)
    position = lax.rem(lax.axis_index("gx") // stride, count)
    for turn, arrival in enumerate(arrivals):
        scratch[position ^ turn] = arrival[...]
    return position


def exchange(value, axis, stride, count):
    size = lax.axis_size(axis)
    return [value] + [
        lax.ppermute(value, axis, [(i, i ^ (turn * stride)) for i in range(size)])
        for turn in range(1, count)
    ]


def own_edges(scratch, position, near, faces, far):
    for i, value in enumerate([near] + faces + [far]):
        scratch[i] = value
    return scratch[position], scratch[position + 1]


def x_ends(cond):
    me, count = lax.axis_index("gx"), lax.axis_size("gx")
    depth = cond.shape[0]
    near = jnp.where(me == 0, 0.0, 2.0) * cond[0]
    far = jnp.where(me == count - 1, 0.0, 2.0) * cond[depth - 1]
    return near, far


def x_reduce(log_cond, storage, head, east, north, depth, rates,
             cond, steps_ref, own, send, five):
    cells, rows, _ = cond.shape
    me, group = lax.axis_index("gx"), lax.axis_index("yz")
    wells = rates.shape[1]
    cond[...] = jnp.exp(log_cond[...])
    local_east = east[...] - me * cells
    local_north = north[...] - group * rows
    inside = (
        (local_east >= 0) & (local_east < cells) & (local_north >= 0) & (local_north < rows)
    )
    spot = jnp.where(inside, local_east * rows + local_north, -1)
    at_row = jnp.where(
        lax.broadcasted_iota(jnp.int32, (cells * rows, wells), 0) == spot, 1.0, 0.0
    ).astype(jnp.bfloat16)
    at_depth = lax.broadcasted_iota(jnp.int32, (lanes, wells), 0) == depth[...]
    sources = sum(
        lax.dot_general(
            at_row, part, (((1,), (1,)), ((), ())), preferred_element_type=f32
        )
        for part in exact_parts(jnp.where(at_depth, rates[...], 0.0))
    ).reshape(cells, rows, lanes)
    near, far = x_ends(cond)
    links = [harmonic(cond[i], cond[i + 1]) for i in range(cells - 1)] + [far]
    block, steps = eliminate(
        near,
        links,
        [storage[i] for i in range(cells)],
        [storage[i] * head[i] + sources[i] for i in range(cells)],
    )
    keep_steps(steps_ref, steps)
    for i, value in enumerate(block):
        five[i] = value
    half = rows // 2
    mine = lax.rem(me, 2)
    own[...] = five[:, pl.ds(pl.multiple_of(mine * half, half), half), :]
    send[...] = five[:, pl.ds(pl.multiple_of((1 - mine) * half, half), half), :]


def make_join(stride, count):
    def join(*refs):
        arrivals, (joined_ref, steps_ref, scratch) = refs[:count], refs[count:]
        place(scratch, arrivals, stride)
        joined, steps = combine(
            [[scratch[i, j] for j in range(5)] for i in range(count)]
        )
        for i, value in enumerate(joined):
            joined_ref[i] = value
        keep_steps(steps_ref, steps)

    return join


def hand_back(edges, middle, own, send):
    near, far = edges
    first = lax.rem(lax.axis_index("gx"), 2) == 0
    own[0] = jnp.where(first, near, middle)
    own[1] = jnp.where(first, middle, far)
    send[0] = jnp.where(first, middle, near)
    send[1] = jnp.where(first, far, middle)


def make_top(stride, count, inner):
    def top(*refs):
        arrivals = refs[:count]
        group_steps, pair_steps, own, send, steps_ref, scratch, edges_top, edges_group = refs[count:]
        position = place(scratch, arrivals, stride)
        nothing = jnp.zeros(own.shape[1:], f32)
        _, steps = combine([[scratch[i, j] for j in range(5)] for i in range(count)])
        keep_steps(steps_ref, steps)
        edges = own_edges(edges_top, position, nothing, expand(steps, nothing, nothing), nothing)
        position = lax.rem(lax.axis_index("gx") // 2, inner)
        edges = own_edges(
            edges_group, position, edges[0], expand(steps_of(group_steps), *edges), edges[1]
        )
        hand_back(edges, expand(steps_of(pair_steps), *edges)[0], own, send)

    return top


def both_halves(own, other, scratch):
    half = own.shape[1]
    mine = lax.rem(lax.axis_index("gx"), 2)
    scratch[:, pl.ds(pl.multiple_of(mine * half, half), half), :] = own[...]
    scratch[:, pl.ds(pl.multiple_of((1 - mine) * half, half), half), :] = other[...]


def y_cells(ref, spot):
    chunks = ref.shape[1] // chunk
    return ref[:, pl.ds(spot, chunks, stride=chunk), :]


def y_links(cond):
    me, count = lax.axis_index("yz"), lax.axis_size("yz")
    cells = [y_cells(cond, spot) for spot in range(chunk)]
    place_of = lax.broadcasted_iota(jnp.int32, cells[0].shape, 1)
    chunks = cells[0].shape[1]
    near = jnp.where((place_of == 0) & (me == 0), 0.0, 2.0 * cells[0])
    far = jnp.where((place_of == chunks - 1) & (me == count - 1), 0.0, 2.0 * cells[-1])
    return cells, near, far


def by_chunk(value, scratch):
    slab, chunks, _ = value.shape
    scratch[...] = value.reshape(slab * chunks, lanes)
    return [scratch[pl.ds(i, slab, stride=chunks), :] for i in range(chunks)]


def from_chunk(values, scratch):
    slab, chunks = values[0].shape[0], len(values)
    for i, value in enumerate(values):
        scratch[pl.ds(i, slab, stride=chunks), :] = value
    return scratch[...].reshape(slab, chunks, lanes)


def y_reduce(own, other, x_steps, cond, storage,
             head_first, x_edges, cell_steps, chunk_steps, message, turned):
    cells = head_first.shape[0]
    both_halves(own, other, x_edges)
    far = x_edges[1]
    for i in reversed(range(cells)):
        far = x_steps[i, 3] + x_steps[i, 1] * x_edges[0] + x_steps[i, 2] * far
        head_first[i] = far
    conds, near, far = y_links(cond)
    links = [harmonic(conds[i], conds[i + 1]) for i in range(chunk - 1)] + [far]
    stores = [y_cells(storage, spot) for spot in range(chunk)]
    loads = [stores[spot] * y_cells(head_first, spot) for spot in range(chunk)]
    block, steps = eliminate(near, links, stores, loads)
    keep_steps(cell_steps, steps)
    parts = [by_chunk(value, turned.at[i]) for i, value in enumerate(block)]
    joined, steps = combine(list(zip(*parts)))
    keep_steps(chunk_steps, steps)
    for i, value in enumerate(joined):
        message[i] = value


def make_z(count, cuts):
    def z_solve(*refs):
        arrivals = refs[:count]
        (cell_steps, chunk_steps, cond, storage, east, north, depth, observed,
         y_factors, head_second, y_edges, head_third, z_terms, message, scaled_cells, scaled_chunks,
         scratch, edges, turned, ahead, behind, inverses, grounds, loads, second, third) = refs[count:]
        me = lax.axis_index("yz")
        for turn, arrival in enumerate(arrivals):
            scratch[me ^ turn] = arrival[...]
        nothing = jnp.zeros(arrivals[0].shape[1:], f32)
        _, steps = combine([[scratch[i, j] for j in range(5)] for i in range(count)])
        keep_steps(y_factors, steps)
        near, far = own_edges(edges, me, nothing, expand(steps, nothing, nothing), nothing)
        faces = [near] + expand(steps_of(chunk_steps), near, far) + [far]
        near = from_chunk(faces[:-1], turned.at[0])
        far = from_chunk(faces[1:], turned.at[1])
        y_edges[0] = near
        y_edges[1] = far
        for spot in reversed(range(chunk)):
            far = cell_steps[spot, 3] + cell_steps[spot, 1] * near + cell_steps[spot, 2] * far
            head_second[spot] = far
            second[:, pl.ds(spot, second.shape[1] // chunk, stride=chunk), :] = far

        slab, rows, _ = cond.shape
        total = slab * rows
        piece = total // cuts
        lane = lax.broadcasted_iota(jnp.int32, (piece, lanes), 1)

        def cut(ref, i):
            per = slab // cuts
            return ref[i * per:(i + 1) * per].reshape(piece, lanes)

        for i in range(cuts):
            here = cut(cond, i)
            ahead[0, i] = jnp.where(
                lane == lanes - 1, 0.0, harmonic(here, pltpu.roll(here, lanes - 1, 1))
            )
            grounds[i] = cut(storage, i)
            loads[i] = cut(storage, i) * cut(second, i)
        levels = lanes.bit_length() - 1
        for level in range(levels):
            shift = 1 << level
            for i in range(cuts):
                link, ground, load = ahead[level, i], grounds[i], loads[i]
                link_back = pltpu.roll(link, shift, 1)
                inverse = 1.0 / (link + link_back + ground)
                behind[level, i] = link_back
                inverses[level, i] = inverse
                held = inverse * ground
                passed = inverse * load
                grounds[i] = (
                    ground
                    + link * pltpu.roll(held, lanes - shift, 1)
                    + link_back * pltpu.roll(held, shift, 1)
                )
                loads[i] = (
                    load
                    + link * pltpu.roll(passed, lanes - shift, 1)
                    + link_back * pltpu.roll(passed, shift, 1)
                )
                if level < levels - 1:
                    ahead[level + 1, i] = link * pltpu.roll(inverse * link, lanes - shift, 1)
        for i in range(cuts):
            grounds[i] = 1.0 / grounds[i]
            third[pl.ds(i * piece, piece), :] = loads[i] * grounds[i]
        head_third[...] = third[...].reshape(slab, rows, lanes)

        local_east = east[...] - lax.axis_index("gx") * slab
        local_north = north[...] - me * rows
        inside = (
            (local_east >= 0) & (local_east < slab) & (local_north >= 0) & (local_north < rows)
        )
        points = inside.shape[1]
        spot = jnp.where(inside, local_east * rows + local_north, -1)
        at_row = jnp.where(
            lax.broadcasted_iota(jnp.int32, (total, points), 0) == spot, 1.0, 0.0
        ).astype(jnp.bfloat16)
        at_depth = lax.broadcasted_iota(jnp.int32, (lanes, points), 0) == depth[...]
        found = sum(
            lax.dot_general(
                part, at_row, (((0,), (0,)), ((), ())), preferred_element_type=f32
            )
            for part in exact_parts(third[...])
        )
        found = jnp.sum(jnp.where(at_depth, found, 0.0), axis=0, keepdims=True)
        misfit = jnp.where(inside, found - observed[...], 0.0)
        for i in range(points // lanes):
            message[2, i:i + 1, :] = misfit[:, i * lanes:(i + 1) * lanes]
        parts = [
            jnp.where(at_depth, part.astype(f32), 0.0).astype(jnp.bfloat16)
            for part in exact_parts(misfit_weight * misfit)
        ]
        source = sum(
            lax.dot_general(
                at_row, part, (((1,), (1,)), ((), ())), preferred_element_type=f32
            )
            for part in parts
        )
        for i in range(cuts):
            loads[i] = source[i * piece:(i + 1) * piece]
        for level in range(levels):
            shift = 1 << level
            for i in range(cuts):
                load = loads[i]
                passed = inverses[level, i] * load
                loads[i] = (
                    load
                    + ahead[level, i] * pltpu.roll(passed, lanes - shift, 1)
                    + behind[level, i] * pltpu.roll(passed, shift, 1)
                )
        per = slab // cuts
        for i in range(cuts):
            adjoint = loads[i] * grounds[i]
            here = cut(cond, i)
            head = third[pl.ds(i * piece, piece), :]
            to_left, to_right = face_gradient(
                here,
                pltpu.roll(here, lanes - 1, 1),
                adjoint - pltpu.roll(adjoint, lanes - 1, 1),
                head - pltpu.roll(head, lanes - 1, 1),
            )
            to_left = jnp.where(lane == lanes - 1, 0.0, to_left)
            to_right = jnp.where(lane == lanes - 1, 0.0, to_right)
            z_terms[i * per:(i + 1) * per] = (
                (to_left + pltpu.roll(to_right, 1, 1)).reshape(per, rows, lanes)
            )
            second[i * per:(i + 1) * per] = (cut(storage, i) * adjoint).reshape(per, rows, lanes)

        near, far, scaled = eliminate_loads(
            factors_of(cell_steps), [y_cells(second, i) for i in range(chunk)]
        )
        for i, value in enumerate(scaled):
            scaled_cells[i] = value
        blocks = list(zip(by_chunk(near, turned.at[0]), by_chunk(far, turned.at[1])))
        joined, scaled = combine_loads(blocks, factors_of(chunk_steps))
        for i, value in enumerate(scaled):
            scaled_chunks[i] = value
        message[0] = joined[0]
        message[1] = joined[1]

    return z_solve


def make_y_back(count):
    def y_back(*refs):
        arrivals = refs[:count]
        (y_factors, cell_steps, chunk_steps, scaled_cells, scaled_chunks, head_second, y_edges,
         cond, storage, z_terms, x_steps,
         terms, scaled_x, own, send, scratch, edges, turned, second, pair) = refs[count:]
        me = lax.axis_index("yz")
        misfit = arrivals[0][2]
        for turn, arrival in enumerate(arrivals):
            scratch[me ^ turn] = arrival[:2]
            if turn:
                misfit = misfit + arrival[2]
        nothing = jnp.zeros(arrivals[0].shape[1:], f32)
        factors = factors_of(y_factors)
        _, scaled = combine_loads([[scratch[i, 0], scratch[i, 1]] for i in range(count)], factors)
        faces = expand(with_scaled(factors, scaled), nothing, nothing)
        near, far = own_edges(edges, me, nothing, faces, nothing)
        factors = factors_of(chunk_steps)
        steps = with_scaled(factors, [scaled_chunks[i] for i in range(len(factors))])
        faces = [near] + expand(steps, near, far) + [far]
        near = from_chunk(faces[:-1], turned.at[0])
        far = from_chunk(faces[1:], turned.at[1])
        conds, near_link, far_link = y_links(cond)
        after = far
        adjoint = [None] * chunk
        for spot in reversed(range(chunk)):
            after = scaled_cells[spot] + cell_steps[spot, 1] * near + cell_steps[spot, 2] * after
            adjoint[spot] = after
            second[:, pl.ds(spot, second.shape[1] // chunk, stride=chunk), :] = after
        from_left = -near_link * (adjoint[0] - near) * (head_second[0] - y_edges[0])
        for spot in range(chunk):
            if spot < chunk - 1:
                to_left, to_right = face_gradient(
                    conds[spot], conds[spot + 1],
                    adjoint[spot] - adjoint[spot + 1],
                    head_second[spot] - head_second[spot + 1],
                )
                value = from_left + to_left
                from_left = to_right
            else:
                value = from_left - far_link * (adjoint[spot] - far) * (head_second[spot] - y_edges[1])
            spots = (slice(None), pl.ds(spot, second.shape[1] // chunk, stride=chunk), slice(None))
            terms[spots] = value + z_terms[spots]

        near, far, scaled = eliminate_loads(
            factors_of(x_steps), [storage[i] * second[i] for i in range(second.shape[0])]
        )
        for i, value in enumerate(scaled):
            scaled_x[i] = value
        pair[0] = near
        pair[1] = far
        half = pair.shape[1] // 2
        mine = lax.rem(lax.axis_index("gx"), 2)
        for ref, side in ((own, mine), (send, 1 - mine)):
            for i in range(2):
                ref[i * half:(i + 1) * half] = pair[i, pl.ds(pl.multiple_of(side * half, half), half), :]
            ref[2 * half:] = misfit

    return y_back


def loads_in(arrivals, scratch, stride):
    rows = scratch.shape[2]
    count = len(arrivals)
    position = lax.rem(lax.axis_index("gx") // stride, count)
    misfit = None
    for turn, arrival in enumerate(arrivals):
        scratch[position ^ turn, 0] = arrival[:rows]
        scratch[position ^ turn, 1] = arrival[rows:2 * rows]
        part = arrival[2 * rows:]
        misfit = part if misfit is None else misfit + part
    return [[scratch[i, 0], scratch[i, 1]] for i in range(count)], misfit, position


def make_join_loads(stride, count):
    def join(*refs):
        arrivals, (steps_ref, message, scaled_ref, scratch) = refs[:count], refs[count:]
        blocks, misfit, _ = loads_in(arrivals, scratch, stride)
        joined, scaled = combine_loads(blocks, factors_of(steps_ref))
        rows = scratch.shape[2]
        message[:rows] = joined[0]
        message[rows:2 * rows] = joined[1]
        message[2 * rows:] = misfit
        for i, value in enumerate(scaled):
            scaled_ref[i] = value

    return join


def make_top_loads(stride, count, inner):
    def top(*refs):
        arrivals = refs[:count]
        (top_steps, group_steps, group_scaled, pair_steps, pair_scaled,
         own, send, misfit_ref, scratch, edges_top, edges_group) = refs[count:]
        blocks, misfit, position = loads_in(arrivals, scratch, stride)
        misfit_ref[...] = misfit
        nothing = jnp.zeros(own.shape[1:], f32)
        factors = factors_of(top_steps)
        _, scaled = combine_loads(blocks, factors)
        faces = expand(with_scaled(factors, scaled), nothing, nothing)
        edges = own_edges(edges_top, position, nothing, faces, nothing)
        position = lax.rem(lax.axis_index("gx") // 2, inner)
        factors = factors_of(group_steps)
        steps = with_scaled(factors, [group_scaled[i] for i in range(len(factors))])
        edges = own_edges(edges_group, position, edges[0], expand(steps, *edges), edges[1])
        steps = with_scaled(factors_of(pair_steps), [pair_scaled[0]])
        hand_back(edges, expand(steps, *edges)[0], own, send)

    return top


def x_back(own, other, x_steps, scaled_x, cond, head, x_edges, terms, gradient, edges):
    cells = cond.shape[0]
    both_halves(own, other, edges)
    near_link, far_link = x_ends(cond)
    adjoint = [None] * cells
    after = edges[1]
    for i in reversed(range(cells)):
        after = scaled_x[i] + x_steps[i, 1] * edges[0] + x_steps[i, 2] * after
        adjoint[i] = after
    from_left = -near_link * (adjoint[0] - edges[0]) * (head[0] - x_edges[0])
    for i in range(cells):
        if i < cells - 1:
            to_left, to_right = face_gradient(
                cond[i], cond[i + 1], adjoint[i] - adjoint[i + 1], head[i] - head[i + 1]
            )
            gradient[i] = terms[i] + from_left + to_left
            from_left = to_right
        else:
            gradient[i] = (
                terms[i] + from_left - far_link * (adjoint[i] - edges[1]) * (head[i] - x_edges[1])
            )


def shards(log_cond, storage, head, well_east, well_north, well_depth, pump_rates,
           probe_east, probe_north, probe_depth, probe_heads):
    slab, rows, _ = log_cond.shape
    devices, columns = lax.axis_size("gx"), lax.axis_size("yz")
    inner = 4 if devices >= 16 else 2
    outer = devices // (2 * inner)
    half, chunks = rows // 2, rows // chunk
    points = probe_heads.shape[0]
    grid = (slab, rows, lanes)
    plane = (half, lanes)
    cell = (chunk, slab, chunks, lanes)
    line = (slab, lanes)

    cond, x_steps, own, send = run(
        x_reduce,
        [grid, (slab, 4, rows, lanes), (5,) + plane, (5,) + plane],
        [log_cond, storage, head]
        + [value.reshape(1, -1) for value in (well_east, well_north, well_depth, pump_rates)],
        [((5, rows, lanes), f32)],
    )
    swap = [(i, i ^ 1) for i in range(devices)]
    joined, pair_steps = run(
        make_join(1, 2),
        [(5,) + plane, (1, 4) + plane],
        [own, lax.ppermute(send, "gx", swap)],
        [((2, 5) + plane, f32)],
    )
    joined, group_steps = run(
        make_join(2, inner),
        [(5,) + plane, (inner - 1, 4) + plane],
        exchange(joined, "gx", 2, inner),
        [((inner, 5) + plane, f32)],
    )
    own, send, top_steps = run(
        make_top(2 * inner, outer, inner),
        [(2,) + plane, (2,) + plane, (outer - 1, 4) + plane],
        exchange(joined, "gx", 2 * inner, outer) + [group_steps, pair_steps],
        [((outer, 5) + plane, f32), ((outer + 1,) + plane, f32), ((inner + 1,) + plane, f32)],
    )
    head_first, x_edges, cell_steps, chunk_steps, message = run(
        y_reduce,
        [grid, (2, rows, lanes), (chunk, 4) + cell[1:], (chunks - 1, 4) + line, (5,) + line],
        [own, lax.ppermute(send, "gx", swap), x_steps, cond, storage],
        [((5, slab * chunks, lanes), f32)],
    )
    cuts = 4
    piece = (cuts, slab * rows // cuts, lanes)
    levels = lanes.bit_length() - 1
    (y_factors, head_second, y_edges, head_third, z_terms, message, scaled_cells, scaled_chunks) = run(
        make_z(columns, cuts),
        [(columns - 1, 4) + line, cell, (2,) + cell[1:], grid, grid,
         (3,) + line, cell, (chunks - 1,) + line],
        exchange(message, "yz", 1, columns)
        + [cell_steps, chunk_steps, cond, storage]
        + [value.reshape(1, -1) for value in (probe_east, probe_north, probe_depth, probe_heads)],
        [((columns, 5) + line, f32), ((columns + 1,) + line, f32), ((2, slab * chunks, lanes), f32)]
        + [((levels,) + piece, f32)] * 3 + [(piece, f32)] * 2
        + [(grid, f32), ((slab * rows, lanes), f32)],
    )
    extra = points // lanes
    note = (2 * half + extra, lanes)
    terms, scaled_x, own, send = run(
        make_y_back(columns),
        [grid, grid, note, note],
        exchange(message, "yz", 1, columns)
        + [y_factors, cell_steps, chunk_steps, scaled_cells, scaled_chunks, head_second, y_edges,
           cond, storage, z_terms, x_steps],
        [((columns, 2) + line, f32), ((columns + 1,) + line, f32), ((2, slab * chunks, lanes), f32),
         (grid, f32), ((2, rows, lanes), f32)],
    )
    message, pair_scaled = run(
        make_join_loads(1, 2),
        [note, (1,) + plane],
        [own, lax.ppermute(send, "gx", swap), pair_steps],
        [((2, 2) + plane, f32)],
    )
    message, group_scaled = run(
        make_join_loads(2, inner),
        [note, (inner - 1,) + plane],
        exchange(message, "gx", 2, inner) + [group_steps],
        [((inner, 2) + plane, f32)],
    )
    own, send, misfits = run(
        make_top_loads(2 * inner, outer, inner),
        [(2,) + plane, (2,) + plane, (extra, lanes)],
        exchange(message, "gx", 2 * inner, outer)
        + [top_steps, group_steps, group_scaled, pair_steps, pair_scaled],
        [((outer, 2) + plane, f32), ((outer + 1,) + plane, f32), ((inner + 1,) + plane, f32)],
    )
    (gradient,) = run(
        x_back,
        [grid],
        [own, lax.ppermute(send, "gx", swap), x_steps, scaled_x, cond, head_first, x_edges, terms],
        [((2, rows, lanes), f32)],
    )
    return head_third, gradient, misfits.reshape(-1)


def solution(mesh):
    cells = P("gx", "yz", None)
    return jax.shard_map(
        shards,
        mesh=mesh,
        in_specs=(cells, cells, cells) + (P(),) * 8,
        out_specs=(cells, cells, P()),
        check_vma=False,
    )
```

```python
import jax
import jax.numpy as jnp
from jax import lax
from jax.experimental import pallas as pl
from jax.experimental.pallas import tpu as pltpu
from jax.sharding import PartitionSpec as P


f32 = jnp.float32
misfit_weight = 100.0
lanes = 128
chunk = 8
field = 10
mask = (1 << field) - 1


def harmonic(left_cond, right_cond):
    return 2.0 * left_cond * right_cond / (left_cond + right_cond)


def eliminate(entry, links, grounds, loads):
    near_ground = near_load = far_ground = far_load = None
    steps = []
    for link, ground, load in zip(links, grounds, loads):
        if far_ground is not None:
            ground, load = ground + far_ground, load + far_load
        inverse = 1.0 / (entry + link + ground)
        to_near, to_far = entry * inverse, link * inverse
        far_ground, far_load = to_far * ground, to_far * load
        if near_ground is None:
            near_ground, near_load = to_near * ground, to_near * load
        else:
            near_ground, near_load = near_ground + to_near * ground, near_load + to_near * load
        steps.append((inverse, to_near, to_far, inverse * load))
        entry = to_near * link
    return (entry, near_ground, far_ground, near_load, far_load), steps


def eliminate_loads(factors, loads):
    near_load = far_load = None
    scaled = []
    for (inverse, to_near, to_far), load in zip(factors, loads):
        if far_load is not None:
            load = load + far_load
        far_load = to_far * load
        near_load = to_near * load if near_load is None else near_load + to_near * load
        scaled.append(inverse * load)
    return near_load, far_load, scaled


def expand(steps, near, far):
    values = []
    for _, to_near, to_far, scaled in reversed(steps):
        far = scaled + to_near * near + to_far * far
        values.append(far)
    return values[::-1]


def combine(blocks):
    pairs = list(zip(blocks[:-1], blocks[1:]))
    (entry, near_ground, far_ground, near_load, far_load), steps = eliminate(
        blocks[0][0],
        [after[0] for _, after in pairs],
        [before[2] + after[1] for before, after in pairs],
        [before[4] + after[3] for before, after in pairs],
    )
    joined = (
        entry,
        blocks[0][1] + near_ground,
        blocks[-1][2] + far_ground,
        blocks[0][3] + near_load,
        blocks[-1][4] + far_load,
    )
    return joined, steps


def combine_loads(blocks, factors):
    near_load, far_load, scaled = eliminate_loads(
        factors, [before[1] + after[0] for before, after in zip(blocks[:-1], blocks[1:])]
    )
    return (blocks[0][0] + near_load, blocks[-1][1] + far_load), scaled


def with_scaled(factors, scaled):
    return [factor + (value,) for factor, value in zip(factors, scaled)]


def factors_of(ref):
    return [(ref[i, 0], ref[i, 1], ref[i, 2]) for i in range(ref.shape[0])]


def steps_of(ref):
    return [(None, ref[i, 1], ref[i, 2], ref[i, 3]) for i in range(ref.shape[0])]


def keep_steps(ref, steps):
    for i, step in enumerate(steps):
        for j, value in enumerate(step):
            ref[i, j] = value


def face_gradient(left_cond, right_cond, adjoint_drop, head_drop):
    total = 1.0 / (left_cond + right_cond)
    flow = -(adjoint_drop * head_drop) * (2.0 * left_cond * right_cond * total) * total
    return flow * right_cond, flow * left_cond


def bf16_parts(values, count):
    parts = []
    for _ in range(count):
        part = values.astype(jnp.bfloat16)
        parts.append(part)
        values = values - part.astype(jnp.float32)
    return parts


def run(body, outs, ins, scratch=(), raw=0, after=(), flops=1000000, limit=24):
    shapes = [
        jax.ShapeDtypeStruct(*((out, f32) if isinstance(out[0], int) else out)) for out in outs
    ]
    size = 4 * (sum(x.size for x in ins) + sum(x.size for x in shapes))
    places = [pltpu.HBM] * raw + [pltpu.VMEM] * (len(ins) - raw) + [pl.ANY] * len(after)
    count = len(ins)

    def ordered(*refs):
        return body(*refs[:count], *refs[count + len(after):])

    return pl.pallas_call(
        ordered,
        out_shape=shapes,
        in_specs=[pl.BlockSpec(memory_space=place) for place in places],
        out_specs=[pl.BlockSpec(memory_space=pltpu.VMEM)] * len(outs),
        scratch_shapes=[
            item if not isinstance(item, tuple) else pltpu.VMEM(*item) for item in scratch
        ],
        compiler_params=pltpu.CompilerParams(vmem_limit_bytes=int(limit * 1024 * 1024)),
        cost_estimate=pl.CostEstimate(flops=flops, bytes_accessed=size, transcendentals=0),
    )(*ins, *after)


def spot_in(stride, count):
    return lax.rem(lax.axis_index("gx") // stride, count)


def place(scratch, arrivals, stride):
    position = spot_in(stride, len(arrivals))
    for turn, arrival in enumerate(arrivals):
        scratch[position ^ turn] = arrival[...]


def exchange(value, axis, stride, count):
    size = lax.axis_size(axis)
    return [value] + [
        lax.ppermute(value, axis, [(i, i ^ (turn * stride)) for i in range(size)])
        for turn in range(1, count)
    ]


def swap(value):
    return lax.ppermute(value, "gx", [(i, i ^ 1) for i in range(lax.axis_size("gx"))])


def own_edges(scratch, position, near, faces, far):
    for i, value in enumerate([near] + faces + [far]):
        scratch[i] = value
    return scratch[position], scratch[position + 1]


def x_ends(cond):
    me, count = lax.axis_index("gx"), lax.axis_size("gx")
    depth = cond.shape[0]
    near = jnp.where(me == 0, 0.0, 2.0) * cond[0]
    far = jnp.where(me == count - 1, 0.0, 2.0) * cond[depth - 1]
    return near, far


def x_eliminate(cond, storage, loads):
    cells = cond.shape[0]
    near, far = x_ends(cond)
    links = [harmonic(cond[i], cond[i + 1]) for i in range(cells - 1)] + [far]
    return eliminate(
        near, links, [storage[i] for i in range(cells)], [loads[i] for i in range(cells)]
    )


def x_factor(cond, storage, loads, steps_ref):
    keep_steps(steps_ref, x_eliminate(cond, storage, loads)[1])


def x_load(log_cond_in, storage_in, head_in, cond, storage, loads, log_cond, head, done):
    moves = [
        pltpu.make_async_copy(source, target, done.at[i])
        for i, (source, target) in enumerate(
            ((log_cond_in, log_cond), (storage_in, storage), (head_in, head))
        )
    ]
    for move in moves:
        move.start()
    moves[0].wait()
    cond[...] = jnp.exp(log_cond[...])
    moves[1].wait()
    moves[2].wait()
    loads[...] = storage[...] * head[...]


def x_reduce(cond, storage, stored, places, rates, loads, own, send, five):
    cells, rows, _ = cond.shape
    me, group = lax.axis_index("gx"), lax.axis_index("yz")
    wells = rates.shape[1]
    local_east = lax.shift_right_logical(places[...], 2 * field) - me * cells
    local_north = (lax.shift_right_logical(places[...], field) & mask) - group * rows
    depth = places[...] & mask
    inside = (
        (local_east >= 0) & (local_east < cells) & (local_north >= 0) & (local_north < rows)
    )
    spot = jnp.where(inside, local_east * rows + local_north, -1)
    at_row = jnp.where(
        lax.broadcasted_iota(jnp.int32, (cells * rows, wells), 0) == spot, 1.0, 0.0
    ).astype(jnp.bfloat16)
    at_depth = lax.broadcasted_iota(jnp.int32, (lanes, wells), 0) == depth
    sources = sum(
        lax.dot_general(
            at_row, part, (((1,), (1,)), ((), ())), preferred_element_type=f32
        )
        for part in bf16_parts(jnp.where(at_depth, rates[...], 0.0), 3)
    ).reshape(cells, rows, lanes)
    for i in range(cells):
        loads[i] = stored[i] + sources[i]
    block, _ = x_eliminate(cond, storage, loads)
    for i, value in enumerate(block):
        five[i] = value
    half = rows // 2
    mine = lax.rem(me, 2)
    own[...] = five[:, pl.ds(pl.multiple_of(mine * half, half), half), :]
    send[...] = five[:, pl.ds(pl.multiple_of((1 - mine) * half, half), half), :]


def make_join(stride, count):
    def join(*refs):
        arrivals, (joined_ref, steps_ref, scratch) = refs[:count], refs[count:]
        place(scratch, arrivals, stride)
        joined, steps = combine([[scratch[i, j] for j in range(5)] for i in range(count)])
        for i, value in enumerate(joined):
            joined_ref[i] = value
        keep_steps(steps_ref, steps)

    return join


def descend(levels, edges, scratch):
    for stride, steps in levels[:-1]:
        faces = expand(steps, *edges)
        edges = own_edges(scratch, spot_in(stride, len(steps) + 1), edges[0], faces, edges[1])
    return edges[0], expand(levels[-1][1], *edges)[0], edges[1]


def hand_back(near, middle, far, own, send):
    first = spot_in(1, 2) == 0
    own[0] = jnp.where(first, near, middle)
    own[1] = jnp.where(first, middle, far)
    send[0] = jnp.where(first, middle, near)
    send[1] = jnp.where(first, far, middle)


def make_top(strides, counts):
    below = len(strides) - 1

    def top(*refs):
        arrivals = refs[:counts[-1]]
        lower, (own, send, steps_ref, scratch, edges) = (
            refs[counts[-1]:counts[-1] + below], refs[counts[-1] + below:]
        )
        place(scratch, arrivals, strides[-1])
        nothing = jnp.zeros(own.shape[1:], f32)
        _, steps = combine([[scratch[i, j] for j in range(5)] for i in range(counts[-1])])
        keep_steps(steps_ref, steps)
        levels = [(strides[-1], steps)] + [
            (strides[i], steps_of(lower[i])) for i in reversed(range(below))
        ]
        hand_back(*descend(levels, (nothing, nothing), edges), own, send)

    return top


def both_halves(own, other, scratch):
    half = own.shape[1]
    mine = lax.rem(lax.axis_index("gx"), 2)
    scratch[:, pl.ds(pl.multiple_of(mine * half, half), half), :] = own[...]
    scratch[:, pl.ds(pl.multiple_of((1 - mine) * half, half), half), :] = other[...]


def y_cells(ref, spot):
    chunks = ref.shape[1] // chunk
    return ref[:, pl.ds(spot, chunks, stride=chunk), :]


def y_links(cond):
    me, count = lax.axis_index("yz"), lax.axis_size("yz")
    cells = [y_cells(cond, spot) for spot in range(chunk)]
    place_of = lax.broadcasted_iota(jnp.int32, cells[0].shape, 1)
    chunks = cells[0].shape[1]
    near = jnp.where((place_of == 0) & (me == 0), 0.0, 2.0 * cells[0])
    far = jnp.where((place_of == chunks - 1) & (me == count - 1), 0.0, 2.0 * cells[-1])
    return cells, near, far


def by_chunk(value, scratch):
    slab, chunks, _ = value.shape
    scratch[...] = value.reshape(slab * chunks, lanes)
    return [scratch[pl.ds(i, slab, stride=chunks), :] for i in range(chunks)]


def from_chunk(values, scratch):
    slab, chunks = values[0].shape[0], len(values)
    for i, value in enumerate(values):
        scratch[pl.ds(i, slab, stride=chunks), :] = value
    return scratch[...].reshape(slab, chunks, lanes)


def y_factor(cond, storage, cell_factors, chunk_factors, ends, turned):
    conds, near, far = y_links(cond)
    links = [harmonic(conds[i], conds[i + 1]) for i in range(chunk - 1)] + [far]
    nothing = [jnp.zeros_like(near)] * chunk
    block, steps = eliminate(near, links, [y_cells(storage, i) for i in range(chunk)], nothing)
    keep_steps(cell_factors, [step[:3] for step in steps])
    parts = [by_chunk(value, turned.at[i]) for i, value in enumerate(block[:3])]
    nothing = [jnp.zeros_like(parts[0][0])] * len(parts[0])
    joined, steps = combine(list(zip(*parts, nothing, nothing)))
    keep_steps(chunk_factors, [step[:3] for step in steps])
    for i in range(3):
        ends[i] = joined[i]


def z_links(cond):
    lane = lax.broadcasted_iota(jnp.int32, cond.shape, 1)
    after = pltpu.roll(cond, lanes - 1, 1)
    return lane == lanes - 1, after


def piece_of(ref, i, cuts):
    per = ref.shape[0] // cuts
    return ref[i * per:(i + 1) * per].reshape(per * ref.shape[1], lanes)


def make_z_factor(cuts, first, last, total):
    def z_factor(*refs):
        if first == 0:
            cond, storage, from_back, from_ahead, links, grounds = refs
            for i in range(cuts):
                here = piece_of(cond, i, cuts)
                ending, after = z_links(here)
                links[i] = jnp.where(ending, 0.0, harmonic(here, after))
                grounds[i] = piece_of(storage, i, cuts)
            links_in, grounds_in = links, grounds
        else:
            links_in, grounds_in, from_back, from_ahead, links, grounds = refs
        for level in range(first, last):
            shift = 1 << level
            for i in range(cuts):
                link, ground = links_in[i], grounds_in[i]
                link_back = pltpu.roll(link, shift, 1)
                inverse = 1.0 / (link + link_back + ground)
                passed = inverse * link
                from_back[level - first, i] = pltpu.roll(passed, shift, 1)
                from_ahead[level - first, i] = link * pltpu.roll(inverse, lanes - shift, 1)
                held = inverse * ground
                grounds[i] = (
                    ground
                    + link * pltpu.roll(held, lanes - shift, 1)
                    + link_back * pltpu.roll(held, shift, 1)
                )
                links[i] = link * pltpu.roll(passed, lanes - shift, 1)
            links_in, grounds_in = links, grounds
        if last == total:
            for i in range(cuts):
                grounds[i] = 1.0 / grounds[i]

    return z_factor


def make_points(slab, rows):
    def points(east, north, depth, at_row, at_depth, here):
        local_east = east[...] - lax.axis_index("gx") * slab
        local_north = north[...] - lax.axis_index("yz") * rows
        inside = (
            (local_east >= 0) & (local_east < slab) & (local_north >= 0) & (local_north < rows)
        )
        spot = jnp.where(inside, local_east * rows + local_north, -1)
        at_row[...] = jnp.where(
            lax.broadcasted_iota(jnp.int32, at_row.shape, 0) == spot, 1.0, 0.0
        ).astype(jnp.bfloat16)
        at_depth[...] = jnp.where(
            lax.broadcasted_iota(jnp.int32, at_depth.shape, 0) == depth[...], 1.0, 0.0
        )
        here[...] = jnp.where(inside, 1.0, 0.0)

    return points


def y_forward(own, other, x_steps, storage, cell_factors, chunk_factors, ends,
              head_first, x_edges, scaled_cells, scaled_chunks, message, loads, turned):
    cells = head_first.shape[0]
    both_halves(own, other, x_edges)
    near, far = x_edges[0], x_edges[1]
    for i in reversed(range(cells)):
        far = x_steps[i, 3] + x_steps[i, 1] * near + x_steps[i, 2] * far
        head_first[i] = far
        loads[i] = storage[i] * far
    for i in range(3):
        message[i] = ends[i]
    y_loads(loads, cell_factors, chunk_factors, scaled_cells, scaled_chunks, turned, message.at[3:5])


def y_loads(loads, cell_factors, chunk_factors, scaled_cells, scaled_chunks, turned, message):
    near, far, scaled = eliminate_loads(
        factors_of(cell_factors), [y_cells(loads, i) for i in range(chunk)]
    )
    for i, value in enumerate(scaled):
        scaled_cells[i] = value
    blocks = list(zip(by_chunk(near, turned.at[0]), by_chunk(far, turned.at[1])))
    joined, scaled = combine_loads(blocks, factors_of(chunk_factors))
    for i, value in enumerate(scaled):
        scaled_chunks[i] = value
    message[0] = joined[0]
    message[1] = joined[1]


def y_expand(near, far, cell_factors, chunk_factors, scaled_cells, scaled_chunks,
             turned, solved, edges, natural):
    factors = factors_of(chunk_factors)
    steps = with_scaled(factors, [scaled_chunks[i] for i in range(len(factors))])
    faces = [near] + expand(steps, near, far) + [far]
    near = from_chunk(faces[:-1], turned.at[0])
    far = from_chunk(faces[1:], turned.at[1])
    edges[0] = near
    edges[1] = far
    for spot in reversed(range(chunk)):
        far = scaled_cells[spot] + cell_factors[spot, 1] * near + cell_factors[spot, 2] * far
        solved[spot] = far
        natural[:, pl.ds(spot, natural.shape[1] // chunk, stride=chunk), :] = far


def z_sweep(loads, parts):
    level = 0
    for from_back, from_ahead in parts:
        for part in range(from_back.shape[0]):
            shift = 1 << level
            level = level + 1
            for i in range(from_back.shape[1]):
                load = loads[i]
                loads[i] = (
                    load
                    + from_ahead[part, i] * pltpu.roll(load, lanes - shift, 1)
                    + from_back[part, i] * pltpu.roll(load, shift, 1)
                )


def make_z(count, cuts, split):
    def z_solve(*refs):
        arrivals, tables = refs[:count], refs[count:count + 2 * split]
        sweeps = [(tables[2 * i], tables[2 * i + 1]) for i in range(split)]
        (cell_factors, chunk_factors, scaled_cells, scaled_chunks, storage,
         inverse, at_row, at_depth, here, observed,
         y_factors, head_second, y_edges, head_third, adjoint_third, message,
         next_cells, next_chunks,
         scratch, edges, turned, loads, second, third) = refs[count + 2 * split:]
        me = lax.axis_index("yz")
        for turn, arrival in enumerate(arrivals):
            scratch[me ^ turn] = arrival[...]
        nothing = jnp.zeros(arrivals[0].shape[1:], f32)
        _, steps = combine([[scratch[i, j] for j in range(5)] for i in range(count)])
        keep_steps(y_factors, [step[:3] for step in steps])
        near, far = own_edges(edges, me, nothing, expand(steps, nothing, nothing), nothing)
        y_expand(near, far, cell_factors, chunk_factors, scaled_cells, scaled_chunks,
                 turned, head_second, y_edges, second)

        slab, rows, _ = storage.shape
        per = slab // cuts
        piece = per * rows
        for i in range(cuts):
            loads[i] = piece_of(storage, i, cuts) * piece_of(second, i, cuts)
        z_sweep(loads, sweeps)
        for i in range(cuts):
            head = loads[i] * inverse[i]
            head_third[i * per:(i + 1) * per] = head.reshape(per, rows, lanes)
            for j, part in enumerate(bf16_parts(head, 2)):
                third[pl.ds(i * piece, piece), j * lanes:(j + 1) * lanes] = part
        found = lax.dot_general(
            third[...], at_row[...], (((0,), (0,)), ((), ())), preferred_element_type=f32
        )
        found = jnp.sum(
            at_depth[...] * (found[:lanes] + found[lanes:]), axis=0, keepdims=True
        )
        misfit = here[...] * (found - observed[...])
        for i in range(misfit.shape[1] // lanes):
            message[2, i:i + 1, :] = misfit[:, i * lanes:(i + 1) * lanes]
        parts = [
            (at_depth[...] * part.astype(f32)).astype(jnp.bfloat16)
            for part in bf16_parts(misfit_weight * misfit, 2)
        ]
        source = lax.dot_general(
            at_row[...], jnp.concatenate(parts, axis=0),
            (((1,), (1,)), ((), ())), preferred_element_type=f32,
        )
        for i in range(cuts):
            part = source[i * piece:(i + 1) * piece]
            loads[i] = part[:, :lanes] + part[:, lanes:]
        z_sweep(loads, sweeps)
        for i in range(cuts):
            adjoint = (loads[i] * inverse[i]).reshape(per, rows, lanes)
            adjoint_third[i * per:(i + 1) * per] = adjoint
            second[i * per:(i + 1) * per] = storage[i * per:(i + 1) * per] * adjoint
        y_loads(second, cell_factors, chunk_factors, next_cells, next_chunks, turned,
                message.at[0:2])

    return z_solve


def make_y_back(count):
    def y_back(*refs):
        arrivals = refs[:count]
        (y_factors, cell_factors, chunk_factors, scaled_cells, scaled_chunks, storage, x_steps,
         adjoint_second, y_edges, scaled_x, own, send, scratch, edges, turned, second, pair
         ) = refs[count:]
        me = lax.axis_index("yz")
        misfit = arrivals[0][2]
        for turn, arrival in enumerate(arrivals):
            scratch[me ^ turn] = arrival[:2]
            if turn:
                misfit = misfit + arrival[2]
        nothing = jnp.zeros(arrivals[0].shape[1:], f32)
        factors = factors_of(y_factors)
        _, scaled = combine_loads([[scratch[i, 0], scratch[i, 1]] for i in range(count)], factors)
        faces = expand(with_scaled(factors, scaled), nothing, nothing)
        near, far = own_edges(edges, me, nothing, faces, nothing)
        y_expand(near, far, cell_factors, chunk_factors, scaled_cells, scaled_chunks,
                 turned, adjoint_second, y_edges, second)
        near, far, scaled = eliminate_loads(
            factors_of(x_steps), [storage[i] * second[i] for i in range(second.shape[0])]
        )
        for i, value in enumerate(scaled):
            scaled_x[i] = value
        pair[0] = near
        pair[1] = far
        half = pair.shape[1] // 2
        mine = lax.rem(lax.axis_index("gx"), 2)
        for ref, side in ((own, mine), (send, 1 - mine)):
            for i in range(2):
                ref[i * half:(i + 1) * half] = pair[i, pl.ds(pl.multiple_of(side * half, half), half), :]
            ref[2 * half:] = misfit

    return y_back


def make_terms(cuts):
    def gather_terms(cond, head_third, adjoint_third, head_second, adjoint_second,
                     head_edges, adjoint_edges, terms, natural):
        conds, near_link, far_link = y_links(cond)
        from_left = (
            -near_link * (adjoint_second[0] - adjoint_edges[0]) * (head_second[0] - head_edges[0])
        )
        for spot in range(chunk):
            if spot < chunk - 1:
                to_left, to_right = face_gradient(
                    conds[spot], conds[spot + 1],
                    adjoint_second[spot] - adjoint_second[spot + 1],
                    head_second[spot] - head_second[spot + 1],
                )
            else:
                to_left = (
                    -far_link * (adjoint_second[spot] - adjoint_edges[1])
                    * (head_second[spot] - head_edges[1])
                )
            natural[:, pl.ds(spot, natural.shape[1] // chunk, stride=chunk), :] = from_left + to_left
            from_left = to_right
        slab, rows, _ = cond.shape
        per = slab // cuts
        for i in range(cuts):
            here, head, adjoint = [
                piece_of(ref, i, cuts) for ref in (cond, head_third, adjoint_third)
            ]
            last, after = z_links(here)
            to_left, to_right = face_gradient(
                here, after,
                adjoint - pltpu.roll(adjoint, lanes - 1, 1),
                head - pltpu.roll(head, lanes - 1, 1),
            )
            to_left = jnp.where(last, 0.0, to_left)
            to_right = jnp.where(last, 0.0, to_right)
            value = (to_left + pltpu.roll(to_right, 1, 1)).reshape(per, rows, lanes)
            terms[i * per:(i + 1) * per] = value + natural[i * per:(i + 1) * per]

    return gather_terms


def loads_in(arrivals, scratch, stride):
    rows, count = scratch.shape[2], len(arrivals)
    misfit = None
    for turn, arrival in enumerate(arrivals):
        position = spot_in(stride, count) ^ turn
        scratch[position, 0] = arrival[:rows]
        scratch[position, 1] = arrival[rows:2 * rows]
        part = arrival[2 * rows:]
        misfit = part if misfit is None else misfit + part
    return [[scratch[i, 0], scratch[i, 1]] for i in range(count)], misfit


def make_join_loads(stride, count):
    def join(*refs):
        arrivals, (steps_ref, message, scaled_ref, scratch) = refs[:count], refs[count:]
        blocks, misfit = loads_in(arrivals, scratch, stride)
        joined, scaled = combine_loads(blocks, factors_of(steps_ref))
        rows = scratch.shape[2]
        message[:rows] = joined[0]
        message[rows:2 * rows] = joined[1]
        message[2 * rows:] = misfit
        for i, value in enumerate(scaled):
            scaled_ref[i] = value

    return join


def make_top_loads(strides, counts):
    below = len(strides) - 1

    def top(*refs):
        arrivals, refs = refs[:counts[-1]], refs[counts[-1]:]
        top_steps, lower, lower_scaled = refs[0], refs[1:1 + below], refs[1 + below:1 + 2 * below]
        own, send, misfit_ref, scratch, edges = refs[1 + 2 * below:]
        blocks, misfit = loads_in(arrivals, scratch, strides[-1])
        nothing = jnp.zeros(scratch.shape[2:], f32)
        factors = factors_of(top_steps)
        levels = [(strides[-1], with_scaled(factors, combine_loads(blocks, factors)[1]))]
        for i in reversed(range(below)):
            factors = factors_of(lower[i])
            scaled = [lower_scaled[i][j] for j in range(len(factors))]
            levels.append((strides[i], with_scaled(factors, scaled)))
        misfit_ref[...] = misfit
        hand_back(*descend(levels, (nothing, nothing), edges), own, send)

    return top


def x_back(own, other, x_steps, scaled_x, cond, head, x_edges, terms, gradient, edges):
    cells = cond.shape[0]
    both_halves(own, other, edges)
    near_link, far_link = x_ends(cond)
    adjoint = [None] * cells
    after = edges[1]
    for i in reversed(range(cells)):
        after = scaled_x[i] + x_steps[i, 1] * edges[0] + x_steps[i, 2] * after
        adjoint[i] = after
    from_left = -near_link * (adjoint[0] - edges[0]) * (head[0] - x_edges[0])
    for i in range(cells):
        if i < cells - 1:
            to_left, to_right = face_gradient(
                cond[i], cond[i + 1], adjoint[i] - adjoint[i + 1], head[i] - head[i + 1]
            )
            gradient[i] = terms[i] + from_left + to_left
            from_left = to_right
        else:
            gradient[i] = (
                terms[i] + from_left - far_link * (adjoint[i] - edges[1]) * (head[i] - x_edges[1])
            )


def shards(log_cond, storage, head, well_east, well_north, well_depth, pump_rates,
           probe_east, probe_north, probe_depth, probe_heads):
    slab, rows, _ = log_cond.shape
    devices, columns = lax.axis_size("gx"), lax.axis_size("yz")
    inner = 4 if devices >= 16 else 2
    strides, counts = [1, 2, 2 * inner], [2, inner, devices // (2 * inner)]
    half = rows // 2
    chunks = rows // chunk
    points = probe_heads.shape[0]
    grid = (slab, rows, lanes)
    plane = (half, lanes)
    cell = (chunk, slab, chunks, lanes)
    line = (slab, lanes)

    places = ((well_east << (2 * field)) + (well_north << field) + well_depth).reshape(1, -1)
    probes = [value.reshape(1, -1) for value in (probe_east, probe_north, probe_depth, probe_heads)]
    cond, storage, stored = run(
        x_load,
        [grid, grid, grid],
        [log_cond, storage, head],
        [(grid, f32), (grid, f32), pltpu.SemaphoreType.DMA((3,))],
        raw=3,
        limit=53,
    )
    loads, own, send = run(
        x_reduce,
        [grid, (5,) + plane, (5,) + plane],
        [cond, storage, stored, places, pump_rates.reshape(1, -1)],
        [((5, rows, lanes), f32)],
    )
    (x_steps,) = run(x_factor, [(slab, 4, rows, lanes)], [cond, storage, loads], after=[send])
    cell_factors, chunk_factors, ends = run(
        y_factor,
        [(chunk, 3) + cell[1:], (chunks - 1, 3) + line, (3,) + line],
        [cond, storage],
        [((3, slab * chunks, lanes), f32)],
        after=[send],
    )
    joined, steps = run(
        make_join(1, 2),
        [(5,) + plane, (1, 4) + plane],
        [own, swap(send)],
        [((2, 5) + plane, f32)],
        after=[x_steps, ends],
    )
    x_levels = [steps]

    cuts = 4
    piece = (cuts, slab * rows // cuts, lanes)
    levels = lanes.bit_length() - 1
    bounds = [0, 4, levels]
    split = len(bounds) - 1
    carried, z_parts, waits = [cond, storage], [], []
    for i, (stride, count) in enumerate(zip(strides[1:], counts[1:])):
        arrivals = exchange(joined, "gx", stride, count)
        waits = []
        if i < split:
            first, last = bounds[i:i + 2]
            from_back, from_ahead, *carried = run(
                make_z_factor(cuts, first, last, levels),
                [(last - first,) + piece] * 2 + [piece] * 2,
                carried,
                after=[joined],
            )
            z_parts += [from_back, from_ahead]
            waits = [carried[1]]
        if i == split - 1:
            at_row, at_depth, here = run(
                make_points(slab, rows),
                [((slab * rows, points), jnp.bfloat16), (lanes, points), (1, points)],
                probes[:3],
                after=[joined],
            )
            waits.append(here)
        if i < len(strides) - 2:
            joined, steps = run(
                make_join(stride, count),
                [(5,) + plane, (count - 1, 4) + plane],
                arrivals,
                [((count, 5) + plane, f32)],
                after=waits,
            )
            x_levels.append(steps)
    own, send, steps = run(
        make_top(strides, counts),
        [(2,) + plane, (2,) + plane, (counts[-1] - 1, 4) + plane],
        arrivals + x_levels,
        [((counts[-1], 5) + plane, f32), ((max(counts) + 1,) + plane, f32)],
        after=waits,
    )
    x_levels.append(steps)
    inverse = carried[1]
    head_first, x_edges, scaled_cells, scaled_chunks, message = run(
        y_forward,
        [grid, (2, rows, lanes), cell, (chunks - 1,) + line, (5,) + line],
        [own, swap(send), x_steps, storage, cell_factors, chunk_factors, ends],
        [(grid, f32), ((2, slab * chunks, lanes), f32)],
    )
    (y_factors, head_second, head_edges, head_third, adjoint_third, message,
     scaled_cells, scaled_chunks) = run(
        make_z(columns, cuts, split),
        [(columns - 1, 3) + line, cell, (2,) + cell[1:], grid, grid,
         (3,) + line, cell, (chunks - 1,) + line],
        exchange(message, "yz", 1, columns)
        + z_parts
        + [cell_factors, chunk_factors, scaled_cells, scaled_chunks, storage,
           inverse, at_row, at_depth, here, probes[3]],
        [((columns, 5) + line, f32), ((columns + 1,) + line, f32), ((2, slab * chunks, lanes), f32),
         (piece, f32), (grid, f32), ((slab * rows, 2 * lanes), jnp.bfloat16)],
    )
    extra = points // lanes
    note = (2 * half + extra, lanes)
    adjoint_second, adjoint_edges, scaled_x, own, send = run(
        make_y_back(columns),
        [cell, (2,) + cell[1:], grid, note, note],
        exchange(message, "yz", 1, columns)
        + [y_factors, cell_factors, chunk_factors, scaled_cells, scaled_chunks, storage, x_steps],
        [((columns, 2) + line, f32), ((columns + 1,) + line, f32), ((2, slab * chunks, lanes), f32),
         (grid, f32), ((2, rows, lanes), f32)],
    )
    (terms,) = run(
        make_terms(cuts),
        [grid],
        [cond, head_third, adjoint_third, head_second, adjoint_second, head_edges, adjoint_edges],
        [(grid, f32)],
    )
    arrivals, x_scaled = [own, swap(send)], []
    for i, (stride, count) in enumerate(zip(strides[:-1], counts[:-1])):
        message, scaled = run(
            make_join_loads(stride, count),
            [note, (count - 1,) + plane],
            arrivals + [x_levels[i]],
            [((count, 2) + plane, f32)],
        )
        x_scaled.append(scaled)
        arrivals = exchange(message, "gx", strides[i + 1], counts[i + 1])
    own, send, misfits = run(
        make_top_loads(strides, counts),
        [(2,) + plane, (2,) + plane, (extra, lanes)],
        arrivals + x_levels[-1:] + x_levels[:-1] + x_scaled,
        [((counts[-1], 2) + plane, f32), ((max(counts) + 1,) + plane, f32)],
    )
    (gradient,) = run(
        x_back,
        [grid],
        [own, swap(send), x_steps, scaled_x, cond, head_first, x_edges, terms],
        [((2, rows, lanes), f32)],
    )
    return head_third, gradient, misfits.reshape(-1)


def solution(mesh):
    cells = P("gx", "yz", None)
    return jax.shard_map(
        shards,
        mesh=mesh,
        in_specs=(cells, cells, cells) + (P(),) * 8,
        out_specs=(cells, cells, P()),
        check_vma=False,
    )
```

```python
import jax
import jax.numpy as jnp
from jax import lax
from jax.experimental import pallas as pl
from jax.experimental.pallas import tpu as pltpu
from jax.sharding import PartitionSpec as P


f32 = jnp.float32
misfit_weight = 100.0
lanes = 128
chunks = 8
field = 10
mask = (1 << field) - 1


def harmonic(left_cond, right_cond):
    return 2.0 * left_cond * right_cond / (left_cond + right_cond)


def eliminate(entry, links, grounds, loads):
    near_ground = near_load = far_ground = far_load = None
    steps = []
    for link, ground, load in zip(links, grounds, loads):
        if far_ground is not None:
            ground, load = ground + far_ground, load + far_load
        inverse = 1.0 / (entry + link + ground)
        to_near, to_far = entry * inverse, link * inverse
        far_ground, far_load = to_far * ground, to_far * load
        if near_ground is None:
            near_ground, near_load = to_near * ground, to_near * load
        else:
            near_ground, near_load = near_ground + to_near * ground, near_load + to_near * load
        steps.append((inverse, to_near, to_far, inverse * load))
        entry = to_near * link
    return (entry, near_ground, far_ground, near_load, far_load), steps


def eliminate_loads(factors, loads):
    near_load = far_load = None
    scaled = []
    for (inverse, to_near, to_far), load in zip(factors, loads):
        if far_load is not None:
            load = load + far_load
        far_load = to_far * load
        near_load = to_near * load if near_load is None else near_load + to_near * load
        scaled.append(inverse * load)
    return near_load, far_load, scaled


def expand(steps, near, far):
    values = []
    for _, to_near, to_far, scaled in reversed(steps):
        far = scaled + to_near * near + to_far * far
        values.append(far)
    return values[::-1]


def combine(blocks):
    pairs = list(zip(blocks[:-1], blocks[1:]))
    (entry, near_ground, far_ground, near_load, far_load), steps = eliminate(
        blocks[0][0],
        [after[0] for _, after in pairs],
        [before[2] + after[1] for before, after in pairs],
        [before[4] + after[3] for before, after in pairs],
    )
    joined = (
        entry,
        blocks[0][1] + near_ground,
        blocks[-1][2] + far_ground,
        blocks[0][3] + near_load,
        blocks[-1][4] + far_load,
    )
    return joined, steps


def combine_loads(blocks, factors):
    near_load, far_load, scaled = eliminate_loads(
        factors, [before[1] + after[0] for before, after in zip(blocks[:-1], blocks[1:])]
    )
    return (blocks[0][0] + near_load, blocks[-1][1] + far_load), scaled


def with_scaled(factors, scaled):
    return [factor + (value,) for factor, value in zip(factors, scaled)]


def factors_of(ref):
    return [(ref[i, 0], ref[i, 1], ref[i, 2]) for i in range(ref.shape[0])]


def steps_of(ref):
    return [(None, ref[i, 1], ref[i, 2], ref[i, 3]) for i in range(ref.shape[0])]


def keep_steps(ref, steps):
    for i, step in enumerate(steps):
        for j, value in enumerate(step):
            ref[i, j] = value


def face_gradient(left_cond, right_cond, adjoint_drop, head_drop):
    total = 1.0 / (left_cond + right_cond)
    flow = -(adjoint_drop * head_drop) * (2.0 * left_cond * right_cond * total) * total
    return flow * right_cond, flow * left_cond


def bf16_parts(values, count):
    parts = []
    for _ in range(count):
        part = values.astype(jnp.bfloat16)
        parts.append(part)
        values = values - part.astype(jnp.float32)
    return parts


def run(body, outs, ins, scratch=(), raw=0, after=(), flops=1000000, limit=24):
    shapes = [
        jax.ShapeDtypeStruct(*((out, f32) if isinstance(out[0], int) else out)) for out in outs
    ]
    size = 4 * (sum(x.size for x in ins) + sum(x.size for x in shapes))
    places = [pltpu.HBM] * raw + [pltpu.VMEM] * (len(ins) - raw) + [pl.ANY] * len(after)
    count = len(ins)

    def ordered(*refs):
        return body(*refs[:count], *refs[count + len(after):])

    return pl.pallas_call(
        ordered,
        out_shape=shapes,
        in_specs=[pl.BlockSpec(memory_space=place) for place in places],
        out_specs=[pl.BlockSpec(memory_space=pltpu.VMEM)] * len(outs),
        scratch_shapes=[
            item if not isinstance(item, tuple) else pltpu.VMEM(*item) for item in scratch
        ],
        compiler_params=pltpu.CompilerParams(vmem_limit_bytes=int(limit * 1024 * 1024)),
        cost_estimate=pl.CostEstimate(flops=flops, bytes_accessed=size, transcendentals=0),
    )(*ins, *after)


def spot_in(stride, count):
    return lax.rem(lax.axis_index("gx") // stride, count)


def place(scratch, arrivals, stride):
    position = spot_in(stride, len(arrivals))
    for turn, arrival in enumerate(arrivals):
        scratch[position ^ turn] = arrival[...]


def exchange(value, stride, count):
    size = lax.axis_size("gx")
    return [value] + [
        lax.ppermute(value, "gx", [(i, i ^ (turn * stride)) for i in range(size)])
        for turn in range(1, count)
    ]


def swap(value):
    return exchange(value, 1, 2)[1]


def exchange_rows(value):
    size, columns = lax.axis_size("gx"), lax.axis_size("yz")
    return [value] + [
        lax.ppermute(
            value,
            ("gx", "yz"),
            [
                (i * columns + j, (i ^ (turn % 2)) * columns + (j ^ (turn // 2)))
                for i in range(size)
                for j in range(columns)
            ],
        )
        for turn in range(1, 2 * columns)
    ]


def side():
    return lax.rem(lax.axis_index("gx"), 2)


def row_block():
    return lax.axis_index("yz") * 2 + side()


def local_spot(east, north, slab, rows):
    local_east = east - lax.axis_index("gx") // 2 * slab
    local_north = north - row_block() * rows
    inside = (
        (local_east >= 0) & (local_east < slab) & (local_north >= 0) & (local_north < rows)
    )
    return inside, jnp.where(inside, local_east * rows + local_north, -1)


def own_edges(scratch, position, near, faces, far):
    for i, value in enumerate([near] + faces + [far]):
        scratch[i] = value
    return scratch[position], scratch[position + 1]


def pair_cells(ref, i):
    cells = ref.shape[0] // 2
    return jnp.stack([ref[i], ref[cells + i]])


def x_ends(cond):
    pair, count = lax.axis_index("gx") // 2, lax.axis_size("gx") // 2
    cells = cond.shape[0]
    near = [jnp.where(pair == 0, 0.0, 2.0) * cond[0], 2.0 * cond[cells // 2]]
    far = [2.0 * cond[cells // 2 - 1], jnp.where(pair == count - 1, 0.0, 2.0) * cond[cells - 1]]
    return jnp.stack(near), jnp.stack(far)


def x_load(log_cond, storage, head, *refs):
    targets, done = refs[:6], refs[6]
    half = targets[0].shape[1]
    moves = []
    for part, some in ((1 - side(), targets[3:]), (side(), targets[:3])):
        rows = pl.ds(pl.multiple_of(part * half, half), half)
        for source, target in zip((log_cond, storage, head), some):
            moves.append(
                pltpu.make_async_copy(source.at[:, rows, :], target, done.at[len(moves)])
            )
    for move in moves:
        move.start()
    for move in moves:
        move.wait()


def make_wells(slab, rows):
    def wells(places, rates, sources):
        _, spot = local_spot(
            lax.shift_right_logical(places[...], 2 * field),
            lax.shift_right_logical(places[...], field) & mask,
            slab,
            rows,
        )
        count = rates.shape[1]
        at_row = jnp.where(
            lax.broadcasted_iota(jnp.int32, (slab * rows, count), 0) == spot, 1.0, 0.0
        ).astype(jnp.bfloat16)
        at_depth = (
            lax.broadcasted_iota(jnp.int32, (lanes, count), 0) == (places[...] & mask)
        )
        sources[...] = sum(
            lax.dot_general(
                at_row, part, (((1,), (1,)), ((), ())), preferred_element_type=f32
            )
            for part in bf16_parts(jnp.where(at_depth, rates[...], 0.0), 3)
        ).reshape(slab, rows, lanes)

    return wells


def x_reduce(*refs):
    parts, (sources, cond, storage, steps_ref, pair_steps, block_ref, raw, loads) = (
        refs[:6], refs[6:]
    )
    cells = cond.shape[0] // 2
    for i in range(3):
        raw[side(), i] = parts[i][...]
        raw[1 - side(), i] = parts[3 + i][...]
    for i in range(2):
        part = slice(i * cells, (i + 1) * cells)
        cond[part] = jnp.exp(raw[i, 0])
        storage[part] = raw[i, 1]
        loads[part] = raw[i, 1] * raw[i, 2] + sources[part]
    near, far = x_ends(cond)
    conds = [pair_cells(cond, i) for i in range(cells)]
    links = [harmonic(conds[i], conds[i + 1]) for i in range(cells - 1)] + [far]
    block, steps = eliminate(
        near,
        links,
        [pair_cells(storage, i) for i in range(cells)],
        [pair_cells(loads, i) for i in range(cells)],
    )
    keep_steps(steps_ref, steps)
    joined, steps = combine([[value[i] for value in block] for i in range(2)])
    keep_steps(pair_steps, steps)
    for i, value in enumerate(joined):
        block_ref[i] = value


def make_join(stride, count):
    def join(*refs):
        arrivals, (joined_ref, steps_ref, scratch) = refs[:count], refs[count:]
        place(scratch, arrivals, stride)
        joined, steps = combine([[scratch[i, j] for j in range(5)] for i in range(count)])
        for i, value in enumerate(joined):
            joined_ref[i] = value
        keep_steps(steps_ref, steps)

    return join


def descend(levels, edges, scratch):
    for stride, steps in levels[:-1]:
        faces = expand(steps, *edges)
        edges = own_edges(scratch, spot_in(stride, len(steps) + 1), edges[0], faces, edges[1])
    return edges[0], expand(levels[-1][1], *edges)[0], edges[1]


def make_top(strides, counts):
    below = len(strides) - 1

    def top(*refs):
        arrivals = refs[:counts[-1]]
        lower, (faces_ref, steps_ref, scratch, edges) = (
            refs[counts[-1]:counts[-1] + below], refs[counts[-1] + below:]
        )
        place(scratch, arrivals, strides[-1])
        nothing = jnp.zeros(faces_ref.shape[1:], f32)
        _, steps = combine([[scratch[i, j] for j in range(5)] for i in range(counts[-1])])
        keep_steps(steps_ref, steps)
        levels = [(strides[-1], steps)] + [
            (strides[i], steps_of(lower[i])) for i in reversed(range(below))
        ]
        for i, value in enumerate(descend(levels, (nothing, nothing), edges)):
            faces_ref[i] = value

    return top


def both_edges(faces):
    return jnp.stack([faces[0], faces[1]]), jnp.stack([faces[1], faces[2]])


def y_spots(ref):
    return ref.shape[1] // chunks


def y_rows(ref, spot):
    return (slice(None), pl.ds(spot, chunks, stride=y_spots(ref)), slice(None))


def y_cells(ref):
    return [ref[y_rows(ref, spot)] for spot in range(y_spots(ref))]


def y_links(cond):
    me, count = row_block(), 2 * lax.axis_size("yz")
    cells = y_cells(cond)
    place_of = lax.broadcasted_iota(jnp.int32, cells[0].shape, 1)
    near = jnp.where((place_of == 0) & (me == 0), 0.0, 2.0 * cells[0])
    far = jnp.where((place_of == chunks - 1) & (me == count - 1), 0.0, 2.0 * cells[-1])
    return cells, near, far


def by_chunk(value, scratch):
    slab = value.shape[0]
    scratch[...] = value.reshape(slab * chunks, lanes)
    return [scratch[pl.ds(i, slab, stride=chunks), :] for i in range(chunks)]


def from_chunk(values, scratch):
    slab = values[0].shape[0]
    for i, value in enumerate(values):
        scratch[pl.ds(i, slab, stride=chunks), :] = value
    return scratch[...].reshape(slab, chunks, lanes)


def y_factor(cond, storage, cell_factors, chunk_factors, ends, turned):
    conds, near, far = y_links(cond)
    links = [harmonic(before, after) for before, after in zip(conds[:-1], conds[1:])] + [far]
    nothing = [jnp.zeros_like(near)] * len(conds)
    block, steps = eliminate(near, links, y_cells(storage), nothing)
    keep_steps(cell_factors, [step[:3] for step in steps])
    parts = [by_chunk(value, turned.at[i]) for i, value in enumerate(block[:3])]
    nothing = [jnp.zeros_like(parts[0][0])] * len(parts[0])
    joined, steps = combine(list(zip(*parts, nothing, nothing)))
    keep_steps(chunk_factors, [step[:3] for step in steps])
    for i in range(3):
        ends[i] = joined[i]


def z_links(cond):
    lane = lax.broadcasted_iota(jnp.int32, cond.shape, 1)
    after = pltpu.roll(cond, lanes - 1, 1)
    return lane == lanes - 1, after


def piece_of(ref, i, cuts):
    per = ref.shape[0] // cuts
    return ref[i * per:(i + 1) * per].reshape(per * ref.shape[1], lanes)


def make_z_factor(cuts, first, last, total):
    def z_factor(*refs):
        if first == 0:
            cond, storage, from_back, from_ahead, links, grounds = refs
            for i in range(cuts):
                here = piece_of(cond, i, cuts)
                ending, after = z_links(here)
                links[i] = jnp.where(ending, 0.0, harmonic(here, after))
                grounds[i] = piece_of(storage, i, cuts)
            links_in, grounds_in = links, grounds
        else:
            links_in, grounds_in, from_back, from_ahead, links, grounds = refs
        for level in range(first, last):
            shift = 1 << level
            for i in range(cuts):
                link, ground = links_in[i], grounds_in[i]
                link_back = pltpu.roll(link, shift, 1)
                inverse = 1.0 / (link + link_back + ground)
                passed = inverse * link
                from_back[level - first, i] = pltpu.roll(passed, shift, 1)
                from_ahead[level - first, i] = link * pltpu.roll(inverse, lanes - shift, 1)
                held = inverse * ground
                grounds[i] = (
                    ground
                    + link * pltpu.roll(held, lanes - shift, 1)
                    + link_back * pltpu.roll(held, shift, 1)
                )
                links[i] = link * pltpu.roll(passed, lanes - shift, 1)
            links_in, grounds_in = links, grounds
        if last == total:
            for i in range(cuts):
                grounds[i] = 1.0 / grounds[i]

    return z_factor


def make_points(slab, rows):
    def points(east, north, depth, heads, at_row, at_depth, here, observed):
        inside, spot = local_spot(east[...], north[...], slab, rows)
        at_row[...] = jnp.where(
            lax.broadcasted_iota(jnp.int32, at_row.shape, 0) == spot, 1.0, 0.0
        ).astype(jnp.bfloat16)
        at_depth[...] = jnp.where(
            lax.broadcasted_iota(jnp.int32, at_depth.shape, 0) == depth[...], 1.0, 0.0
        )
        here[...] = jnp.where(inside, 1.0, 0.0)
        observed[...] = heads[...]

    return points


def y_forward(x_faces, x_steps, storage, cell_factors, chunk_factors, ends,
              head_first, scaled_cells, scaled_chunks, message, loads, turned):
    cells = head_first.shape[0] // 2
    near, far = both_edges(x_faces)
    for i in reversed(range(cells)):
        far = x_steps[i, 3] + x_steps[i, 1] * near + x_steps[i, 2] * far
        for j in range(2):
            head_first[j * cells + i] = far[j]
            loads[j * cells + i] = storage[j * cells + i] * far[j]
    for i in range(3):
        message[i] = ends[i]
    near, far = y_loads(loads, cell_factors, chunk_factors, scaled_cells, scaled_chunks, turned)
    message[3] = near
    message[4] = far


def y_loads(loads, cell_factors, chunk_factors, scaled_cells, scaled_chunks, turned):
    near, far, scaled = eliminate_loads(
        factors_of(cell_factors), y_cells(loads)
    )
    for i, value in enumerate(scaled):
        scaled_cells[i] = value
    blocks = list(zip(by_chunk(near, turned.at[0]), by_chunk(far, turned.at[1])))
    joined, scaled = combine_loads(blocks, factors_of(chunk_factors))
    for i, value in enumerate(scaled):
        scaled_chunks[i] = value
    return joined


def y_expand(near, far, cell_factors, chunk_factors, scaled_cells, scaled_chunks,
             turned, solved, edges, natural):
    factors = factors_of(chunk_factors)
    steps = with_scaled(factors, [scaled_chunks[i] for i in range(len(factors))])
    faces = [near] + expand(steps, near, far) + [far]
    near = from_chunk(faces[:-1], turned.at[0])
    far = from_chunk(faces[1:], turned.at[1])
    edges[0] = near
    edges[1] = far
    for spot in reversed(range(y_spots(natural))):
        far = scaled_cells[spot] + cell_factors[spot, 1] * near + cell_factors[spot, 2] * far
        solved[spot] = far
        natural[y_rows(natural, spot)] = far


def z_sweep(loads, parts):
    level = 0
    for from_back, from_ahead in parts:
        for part in range(from_back.shape[0]):
            shift = 1 << level
            level = level + 1
            for i in range(from_back.shape[1]):
                load = loads[i]
                loads[i] = (
                    load
                    + from_ahead[part, i] * pltpu.roll(load, lanes - shift, 1)
                    + from_back[part, i] * pltpu.roll(load, shift, 1)
                )


def make_z(count, cuts, split):
    def z_solve(*refs):
        arrivals, tables = refs[:count], refs[count:count + 2 * split]
        sweeps = [(tables[2 * i], tables[2 * i + 1]) for i in range(split)]
        (cell_factors, chunk_factors, scaled_cells, scaled_chunks, storage,
         inverse, at_row, at_depth, here, observed,
         y_factors, head_second, y_edges, head_third, head_send, adjoint_third, message,
         next_cells, next_chunks,
         scratch, edges, turned, loads, second, third) = refs[count + 2 * split:]
        me = row_block()
        for turn, arrival in enumerate(arrivals):
            scratch[me ^ turn] = arrival[...]
        nothing = jnp.zeros(arrivals[0].shape[1:], f32)
        _, steps = combine([[scratch[i, j] for j in range(5)] for i in range(count)])
        keep_steps(y_factors, [step[:3] for step in steps])
        near, far = own_edges(edges, me, nothing, expand(steps, nothing, nothing), nothing)
        y_expand(near, far, cell_factors, chunk_factors, scaled_cells, scaled_chunks,
                 turned, head_second, y_edges, second)

        slab, rows, _ = storage.shape
        per = slab // cuts
        piece = per * rows
        for i in range(cuts):
            loads[i] = piece_of(storage, i, cuts) * piece_of(second, i, cuts)
        z_sweep(loads, sweeps)
        for i in range(cuts):
            head = loads[i] * inverse[i]
            head_third[i * per:(i + 1) * per] = head.reshape(per, rows, lanes)
            for j, part in enumerate(bf16_parts(head, 2)):
                third[pl.ds(i * piece, piece), j * lanes:(j + 1) * lanes] = part
        found = lax.dot_general(
            third[...], at_row[...], (((0,), (0,)), ((), ())), preferred_element_type=f32
        )
        found = jnp.sum(
            at_depth[...] * (found[:lanes] + found[lanes:]), axis=0, keepdims=True
        )
        misfit = here[...] * (found - observed[...])
        for i in range(misfit.shape[1] // lanes):
            row = 2 * slab + i
            message[row:row + 1, :] = misfit[:, i * lanes:(i + 1) * lanes]
        cells = slab // 2
        head_send[...] = head_third[pl.ds((1 - side()) * cells, cells)]
        parts = [
            (at_depth[...] * part.astype(f32)).astype(jnp.bfloat16)
            for part in bf16_parts(misfit_weight * misfit, 2)
        ]
        source = lax.dot_general(
            at_row[...], jnp.concatenate(parts, axis=0),
            (((1,), (1,)), ((), ())), preferred_element_type=f32,
        )
        for i in range(cuts):
            part = source[i * piece:(i + 1) * piece]
            loads[i] = part[:, :lanes] + part[:, lanes:]
        z_sweep(loads, sweeps)
        for i in range(cuts):
            adjoint = (loads[i] * inverse[i]).reshape(per, rows, lanes)
            adjoint_third[i * per:(i + 1) * per] = adjoint
            second[i * per:(i + 1) * per] = storage[i * per:(i + 1) * per] * adjoint
        near, far = y_loads(second, cell_factors, chunk_factors, next_cells, next_chunks, turned)
        message[:slab] = near
        message[slab:2 * slab] = far

    return z_solve


def make_y_back(count):
    def y_back(*refs):
        arrivals = refs[:count]
        (y_factors, cell_factors, chunk_factors, scaled_cells, scaled_chunks, storage, x_steps,
         pair_steps, adjoint_second, y_edges, scaled_x, pair_scaled, note,
         scratch, edges, turned, second) = refs[count:]
        me, slab = row_block(), storage.shape[0]
        misfit = None
        for turn, arrival in enumerate(arrivals):
            scratch[me ^ turn, 0] = arrival[:slab]
            scratch[me ^ turn, 1] = arrival[slab:2 * slab]
            part = arrival[2 * slab:]
            misfit = part if misfit is None else misfit + part
        nothing = jnp.zeros(scratch.shape[2:], f32)
        factors = factors_of(y_factors)
        _, scaled = combine_loads([[scratch[i, 0], scratch[i, 1]] for i in range(count)], factors)
        faces = expand(with_scaled(factors, scaled), nothing, nothing)
        near, far = own_edges(edges, me, nothing, faces, nothing)
        y_expand(near, far, cell_factors, chunk_factors, scaled_cells, scaled_chunks,
                 turned, adjoint_second, y_edges, second)
        for i in range(slab):
            second[i] = storage[i] * second[i]
        near, far, scaled = eliminate_loads(
            factors_of(x_steps), [pair_cells(second, i) for i in range(slab // 2)]
        )
        for i, value in enumerate(scaled):
            scaled_x[i] = value
        (near, far), scaled = combine_loads(
            [[near[i], far[i]] for i in range(2)], factors_of(pair_steps)
        )
        pair_scaled[0] = scaled[0]
        rows = near.shape[0]
        note[:rows] = near
        note[rows:2 * rows] = far
        note[2 * rows:] = misfit

    return y_back


def make_terms(cuts):
    def gather_terms(cond, head_third, adjoint_third, head_second, adjoint_second,
                     head_edges, adjoint_edges, terms, natural):
        conds, near_link, far_link = y_links(cond)
        from_left = (
            -near_link * (adjoint_second[0] - adjoint_edges[0]) * (head_second[0] - head_edges[0])
        )
        spots = len(conds)
        for spot in range(spots):
            if spot < spots - 1:
                to_left, to_right = face_gradient(
                    conds[spot], conds[spot + 1],
                    adjoint_second[spot] - adjoint_second[spot + 1],
                    head_second[spot] - head_second[spot + 1],
                )
            else:
                to_left = (
                    -far_link * (adjoint_second[spot] - adjoint_edges[1])
                    * (head_second[spot] - head_edges[1])
                )
            natural[y_rows(natural, spot)] = from_left + to_left
            from_left = to_right
        slab, rows, _ = cond.shape
        per = slab // cuts
        for i in range(cuts):
            here, head, adjoint = [
                piece_of(ref, i, cuts) for ref in (cond, head_third, adjoint_third)
            ]
            last, after = z_links(here)
            to_left, to_right = face_gradient(
                here, after,
                adjoint - pltpu.roll(adjoint, lanes - 1, 1),
                head - pltpu.roll(head, lanes - 1, 1),
            )
            to_left = jnp.where(last, 0.0, to_left)
            to_right = jnp.where(last, 0.0, to_right)
            value = (to_left + pltpu.roll(to_right, 1, 1)).reshape(per, rows, lanes)
            terms[i * per:(i + 1) * per] = value + natural[i * per:(i + 1) * per]

    return gather_terms


def loads_in(arrivals, scratch, stride):
    rows, count = scratch.shape[2], len(arrivals)
    misfit = None
    for turn, arrival in enumerate(arrivals):
        position = spot_in(stride, count) ^ turn
        scratch[position, 0] = arrival[:rows]
        scratch[position, 1] = arrival[rows:2 * rows]
        part = arrival[2 * rows:]
        misfit = part if misfit is None else misfit + part
    return [[scratch[i, 0], scratch[i, 1]] for i in range(count)], misfit


def make_join_loads(stride, count):
    def join(*refs):
        arrivals, (steps_ref, message, scaled_ref, scratch) = refs[:count], refs[count:]
        blocks, misfit = loads_in(arrivals, scratch, stride)
        joined, scaled = combine_loads(blocks, factors_of(steps_ref))
        rows = scratch.shape[2]
        message[:rows] = joined[0]
        message[rows:2 * rows] = joined[1]
        message[2 * rows:] = misfit
        for i, value in enumerate(scaled):
            scaled_ref[i] = value

    return join


def make_top_loads(strides, counts):
    below = len(strides) - 1

    def top(*refs):
        arrivals, refs = refs[:counts[-1]], refs[counts[-1]:]
        top_steps, lower, lower_scaled = refs[0], refs[1:1 + below], refs[1 + below:1 + 2 * below]
        faces_ref, misfit_ref, scratch, edges = refs[1 + 2 * below:]
        blocks, misfit = loads_in(arrivals, scratch, strides[-1])
        nothing = jnp.zeros(scratch.shape[2:], f32)
        factors = factors_of(top_steps)
        levels = [(strides[-1], with_scaled(factors, combine_loads(blocks, factors)[1]))]
        for i in reversed(range(below)):
            factors = factors_of(lower[i])
            scaled = [lower_scaled[i][j] for j in range(len(factors))]
            levels.append((strides[i], with_scaled(factors, scaled)))
        misfit_ref[...] = misfit
        for i, value in enumerate(descend(levels, (nothing, nothing), edges)):
            faces_ref[i] = value

    return top


def x_back(faces, head_faces, x_steps, scaled_x, cond, head, terms, own, send, gradient):
    cells = cond.shape[0] // 2
    near, far = both_edges(faces)
    head_near, head_far = both_edges(head_faces)
    near_link, far_link = x_ends(cond)
    conds = [pair_cells(cond, i) for i in range(cells)]
    heads = [pair_cells(head, i) for i in range(cells)]
    adjoint = [None] * cells
    after = far
    for i in reversed(range(cells)):
        after = scaled_x[i] + x_steps[i, 1] * near + x_steps[i, 2] * after
        adjoint[i] = after
    from_left = -near_link * (adjoint[0] - near) * (heads[0] - head_near)
    for i in range(cells):
        if i < cells - 1:
            to_left, to_right = face_gradient(
                conds[i], conds[i + 1], adjoint[i] - adjoint[i + 1], heads[i] - heads[i + 1]
            )
        else:
            to_left = -far_link * (adjoint[i] - far) * (heads[i] - head_far)
        value = from_left + to_left
        for j in range(2):
            gradient[j * cells + i] = terms[j * cells + i] + value[j]
        from_left = to_right
    own[...] = gradient[pl.ds(side() * cells, cells)]
    send[...] = gradient[pl.ds((1 - side()) * cells, cells)]


def settle(own, other, whole, full):
    cells, half, _ = other.shape
    start = (own.shape[0] - cells) // cells * side() * cells
    full[:, pl.ds(pl.multiple_of(side() * half, half), half), :] = own[pl.ds(start, cells)]
    full[:, pl.ds(pl.multiple_of((1 - side()) * half, half), half), :] = other[...]
    whole[...] = full[...]


def settle_last(own, other, misfits, whole, misfits_out, full):
    misfits_out[...] = misfits[...]
    settle(own, other, whole, full)


def shards(log_cond, storage, head, well_east, well_north, well_depth, pump_rates,
           probe_east, probe_north, probe_depth, probe_heads):
    cells, rows, _ = log_cond.shape
    devices, columns = lax.axis_size("gx"), lax.axis_size("yz")
    inner = 4 if devices >= 16 else 2
    strides, counts = [1, 2, 2 * inner], [2, inner, devices // (2 * inner)]
    slab, half = 2 * cells, rows // 2
    points = probe_heads.shape[0]
    grid = (slab, half, lanes)
    plane = (half, lanes)
    spots = half // chunks
    cell = (spots, slab, chunks, lanes)
    line = (slab, lanes)
    turned = (slab * chunks, lanes)

    places = ((well_east << (2 * field)) + (well_north << field) + well_depth).reshape(1, -1)
    probes = [value.reshape(1, -1) for value in (probe_east, probe_north, probe_depth, probe_heads)]
    parts = run(
        x_load,
        [(cells,) + plane] * 6,
        [log_cond, storage, head],
        [pltpu.SemaphoreType.DMA((6,))],
        raw=3,
        limit=53,
    )
    (sources,) = run(
        make_wells(slab, half), [grid], [places, jnp.where(places >= 0, pump_rates.reshape(1, -1), 0.0)], after=[parts[3]]
    )
    cond, storage, x_steps, pair_steps, joined = run(
        x_reduce,
        [grid, grid, (cells, 4, 2) + plane, (1, 4) + plane, (5,) + plane],
        list(parts[:3]) + [swap(part) for part in parts[3:]] + [sources],
        [((2, 3, cells) + plane, f32), (grid, f32)],
    )
    x_levels = [pair_steps]
    cell_factors, chunk_factors, ends = run(
        y_factor,
        [(spots, 3) + cell[1:], (chunks - 1, 3) + line, (3,) + line],
        [cond, storage],
        [((3,) + turned, f32)],
        after=[joined],
    )

    cuts = 4
    piece = (cuts, slab * half // cuts, lanes)
    levels = lanes.bit_length() - 1
    bounds = [0, 4, levels]
    split = len(bounds) - 1
    carried, z_parts, waits = [cond, storage], [], []
    for i, (stride, count) in enumerate(zip(strides[1:], counts[1:])):
        arrivals = exchange(joined, stride, count)
        waits = [ends]
        if i < split:
            first, last = bounds[i:i + 2]
            from_back, from_ahead, *carried = run(
                make_z_factor(cuts, first, last, levels),
                [(last - first,) + piece] * 2 + [piece] * 2,
                carried,
                after=[joined],
            )
            z_parts += [from_back, from_ahead]
            waits.append(carried[1])
        if i < len(strides) - 2:
            joined, steps = run(
                make_join(stride, count),
                [(5,) + plane, (count - 1, 4) + plane],
                arrivals,
                [((count, 5) + plane, f32)],
                after=waits,
            )
            x_levels.append(steps)
    x_faces, steps = run(
        make_top(strides, counts),
        [(3,) + plane, (counts[-1] - 1, 4) + plane],
        arrivals + x_levels,
        [((counts[-1], 5) + plane, f32), ((max(counts) + 1,) + plane, f32)],
        after=waits,
    )
    x_levels.append(steps)
    inverse = carried[1]
    head_first, scaled_cells, scaled_chunks, message = run(
        y_forward,
        [grid, cell, (chunks - 1,) + line, (5,) + line],
        [x_faces, x_steps, storage, cell_factors, chunk_factors, ends],
        [(grid, f32), ((2,) + turned, f32)],
    )
    at_row, at_depth, here, observed = run(
        make_points(slab, half),
        [((slab * half, points), jnp.bfloat16), (lanes, points), (1, points), (1, points)],
        probes,
        after=[message],
    )
    extra, blocks = points // lanes, 2 * columns
    (y_factors, head_second, head_edges, head_third, head_send, adjoint_third, message,
     scaled_cells, scaled_chunks) = run(
        make_z(blocks, cuts, split),
        [(blocks - 1, 3) + line, cell, (2,) + cell[1:], grid, (cells,) + plane, grid,
         (2 * slab + extra, lanes), cell, (chunks - 1,) + line],
        exchange_rows(message)
        + z_parts
        + [cell_factors, chunk_factors, scaled_cells, scaled_chunks, storage,
           inverse, at_row, at_depth, here, observed],
        [((blocks, 5) + line, f32), ((blocks + 1,) + line, f32), ((2,) + turned, f32),
         (piece, f32), (grid, f32), ((slab * half, 2 * lanes), jnp.bfloat16)],
    )
    note = (2 * half + extra, lanes)
    adjoint_second, adjoint_edges, scaled_x, scaled, message = run(
        make_y_back(blocks),
        [cell, (2,) + cell[1:], (cells, 2) + plane, (1,) + plane, note],
        exchange_rows(message)
        + [y_factors, cell_factors, chunk_factors, scaled_cells, scaled_chunks, storage, x_steps,
           pair_steps],
        [((blocks, 2) + line, f32), ((blocks + 1,) + line, f32), ((2,) + turned, f32),
         (grid, f32)],
    )
    x_scaled = [scaled]
    (terms,) = run(
        make_terms(cuts),
        [grid],
        [cond, head_third, adjoint_third, head_second, adjoint_second, head_edges, adjoint_edges],
        [(grid, f32)],
    )
    for i in range(1, len(strides) - 1):
        arrivals = exchange(message, strides[i], counts[i])
        message, scaled = run(
            make_join_loads(strides[i], counts[i]),
            [note, (counts[i] - 1,) + plane],
            arrivals + [x_levels[i]],
            [((counts[i], 2) + plane, f32)],
        )
        x_scaled.append(scaled)
    faces, misfits = run(
        make_top_loads(strides, counts),
        [(3,) + plane, (extra, lanes)],
        exchange(message, strides[-1], counts[-1]) + x_levels[-1:] + x_levels[:-1] + x_scaled,
        [((counts[-1], 2) + plane, f32), ((max(counts) + 1,) + plane, f32)],
        after=[terms],
    )
    whole = (cells, rows, lanes)
    (head_next,) = run(settle, [whole], [head_third, swap(head_send)], [(whole, f32)])
    own, send = run(
        x_back,
        [(cells,) + plane, (cells,) + plane],
        [faces, x_faces, x_steps, scaled_x, cond, head_first, terms],
        [(grid, f32)],
    )
    gradient, misfits = run(
        settle_last, [whole, (extra, lanes)], [own, swap(send), misfits], [(whole, f32)]
    )
    return head_next, gradient, misfits.reshape(-1)


def solution(mesh):
    cells = P("gx", "yz", None)
    return jax.shard_map(
        shards,
        mesh=mesh,
        in_specs=(cells, cells, cells) + (P(),) * 8,
        out_specs=(cells, cells, P()),
        check_vma=False,
    )
```

```python
import jax
import jax.numpy as jnp
from jax import lax
from jax.experimental import pallas as pl
from jax.experimental.pallas import tpu as pltpu
from jax.sharding import PartitionSpec as P


f32 = jnp.float32
misfit_weight = 100.0
lanes = 128
chunks = 8
field = 10
mask = (1 << field) - 1


def harmonic(left_cond, right_cond):
    return 2.0 * left_cond * right_cond / (left_cond + right_cond)


def eliminate(entry, links, grounds, loads):
    near_ground = near_load = far_ground = far_load = None
    steps = []
    for link, ground, load in zip(links, grounds, loads):
        if far_ground is not None:
            ground, load = ground + far_ground, load + far_load
        inverse = 1.0 / (entry + link + ground)
        to_near, to_far = entry * inverse, link * inverse
        far_ground, far_load = to_far * ground, to_far * load
        if near_ground is None:
            near_ground, near_load = to_near * ground, to_near * load
        else:
            near_ground, near_load = near_ground + to_near * ground, near_load + to_near * load
        steps.append((inverse, to_near, to_far, inverse * load))
        entry = to_near * link
    return (entry, near_ground, far_ground, near_load, far_load), steps


def eliminate_loads(factors, loads):
    near_load = far_load = None
    scaled = []
    for (inverse, to_near, to_far), load in zip(factors, loads):
        if far_load is not None:
            load = load + far_load
        far_load = to_far * load
        near_load = to_near * load if near_load is None else near_load + to_near * load
        scaled.append(inverse * load)
    return near_load, far_load, scaled


def expand(steps, near, far):
    values = []
    for _, to_near, to_far, scaled in reversed(steps):
        far = scaled + to_near * near + to_far * far
        values.append(far)
    return values[::-1]


def combine(blocks):
    pairs = list(zip(blocks[:-1], blocks[1:]))
    (entry, near_ground, far_ground, near_load, far_load), steps = eliminate(
        blocks[0][0],
        [after[0] for _, after in pairs],
        [before[2] + after[1] for before, after in pairs],
        [before[4] + after[3] for before, after in pairs],
    )
    joined = (
        entry,
        blocks[0][1] + near_ground,
        blocks[-1][2] + far_ground,
        blocks[0][3] + near_load,
        blocks[-1][4] + far_load,
    )
    return joined, steps


def combine_loads(blocks, factors):
    near_load, far_load, scaled = eliminate_loads(
        factors, [before[1] + after[0] for before, after in zip(blocks[:-1], blocks[1:])]
    )
    return (blocks[0][0] + near_load, blocks[-1][1] + far_load), scaled


def with_scaled(factors, scaled):
    return [factor + (value,) for factor, value in zip(factors, scaled)]


def factors_of(ref):
    return [(ref[i, 0], ref[i, 1], ref[i, 2]) for i in range(ref.shape[0])]


def steps_of(ref):
    return [(None, ref[i, 1], ref[i, 2], ref[i, 3]) for i in range(ref.shape[0])]


def keep_steps(ref, steps):
    for i, step in enumerate(steps):
        for j, value in enumerate(step):
            ref[i, j] = value


def face_gradient(left_cond, right_cond, adjoint_drop, head_drop):
    total = 1.0 / (left_cond + right_cond)
    flow = -(adjoint_drop * head_drop) * (2.0 * left_cond * right_cond * total) * total
    return flow * right_cond, flow * left_cond


def bf16_parts(values, count):
    parts = []
    for _ in range(count):
        part = values.astype(jnp.bfloat16)
        parts.append(part)
        values = values - part.astype(jnp.float32)
    return parts


def run(body, outs, ins, scratch=(), raw=0, after=(), flops=1000000, limit=24):
    shapes = [
        jax.ShapeDtypeStruct(*((out, f32) if isinstance(out[0], int) else out)) for out in outs
    ]
    size = 4 * (sum(x.size for x in ins) + sum(x.size for x in shapes))
    places = [pltpu.HBM] * raw + [pltpu.VMEM] * (len(ins) - raw) + [pl.ANY] * len(after)
    count = len(ins)

    def ordered(*refs):
        return body(*refs[:count], *refs[count + len(after):])

    return pl.pallas_call(
        ordered,
        out_shape=shapes,
        in_specs=[pl.BlockSpec(memory_space=place) for place in places],
        out_specs=[pl.BlockSpec(memory_space=pltpu.VMEM)] * len(outs),
        scratch_shapes=[
            item if not isinstance(item, tuple) else pltpu.VMEM(*item) for item in scratch
        ],
        compiler_params=pltpu.CompilerParams(vmem_limit_bytes=int(limit * 1024 * 1024)),
        cost_estimate=pl.CostEstimate(flops=flops, bytes_accessed=size, transcendentals=0),
    )(*ins, *after)


def spot_in(stride, count):
    return lax.rem(lax.axis_index("gx") // stride, count)


def place(scratch, arrivals, stride):
    position = spot_in(stride, len(arrivals))
    for turn, arrival in enumerate(arrivals):
        scratch[position ^ turn] = arrival[...]


def exchange(value, stride, count):
    size = lax.axis_size("gx")
    return [value] + [
        lax.ppermute(value, "gx", [(i, i ^ (turn * stride)) for i in range(size)])
        for turn in range(1, count)
    ]


def swap(value):
    return exchange(value, 1, 2)[1]


def exchange_rows(value):
    size, columns = lax.axis_size("gx"), lax.axis_size("yz")
    return [value] + [
        lax.ppermute(
            value,
            ("gx", "yz"),
            [
                (i * columns + j, (i ^ (turn % 2)) * columns + (j ^ (turn // 2)))
                for i in range(size)
                for j in range(columns)
            ],
        )
        for turn in range(1, 2 * columns)
    ]


def side():
    return lax.rem(lax.axis_index("gx"), 2)


def row_block():
    return lax.axis_index("yz") * 2 + side()


def local_spot(east, north, slab, rows):
    local_east = east - lax.axis_index("gx") // 2 * slab
    local_north = north - row_block() * rows
    inside = (
        (local_east >= 0) & (local_east < slab) & (local_north >= 0) & (local_north < rows)
    )
    return inside, jnp.where(inside, local_east * rows + local_north, -1)


def own_edges(scratch, position, near, faces, far):
    for i, value in enumerate([near] + faces + [far]):
        scratch[i] = value
    return scratch[position], scratch[position + 1]


def pair_cells(ref, i):
    cells = ref.shape[0] // 2
    return jnp.stack([ref[i], ref[cells + i]])


def x_ends(cond):
    pair, count = lax.axis_index("gx") // 2, lax.axis_size("gx") // 2
    cells = cond.shape[0]
    near = [jnp.where(pair == 0, 0.0, 2.0) * cond[0], 2.0 * cond[cells // 2]]
    far = [2.0 * cond[cells // 2 - 1], jnp.where(pair == count - 1, 0.0, 2.0) * cond[cells - 1]]
    return jnp.stack(near), jnp.stack(far)


def x_load(log_cond, storage, head, *refs):
    targets, done = refs[:6], refs[6]
    half = targets[0].shape[1]
    moves = []
    for part, some in ((1 - side(), targets[3:]), (side(), targets[:3])):
        rows = pl.ds(pl.multiple_of(part * half, half), half)
        for source, target in zip((log_cond, storage, head), some):
            moves.append(
                pltpu.make_async_copy(source.at[:, rows, :], target, done.at[len(moves)])
            )
    for move in moves:
        move.start()
    for move in moves:
        move.wait()


def make_wells(slab, rows):
    def wells(places, rates, sources):
        _, spot = local_spot(
            lax.shift_right_logical(places[...], 2 * field),
            lax.shift_right_logical(places[...], field) & mask,
            slab,
            rows,
        )
        count = rates.shape[1]
        at_row = jnp.where(
            lax.broadcasted_iota(jnp.int32, (slab * rows, count), 0) == spot, 1.0, 0.0
        ).astype(jnp.bfloat16)
        at_depth = (
            lax.broadcasted_iota(jnp.int32, (lanes, count), 0) == (places[...] & mask)
        )
        sources[...] = sum(
            lax.dot_general(
                at_row, part, (((1,), (1,)), ((), ())), preferred_element_type=f32
            )
            for part in bf16_parts(jnp.where(at_depth, rates[...], 0.0), 3)
        ).reshape(slab, rows, lanes)

    return wells


def x_reduce(*refs):
    parts, (sources, cond, storage, steps_ref, pair_steps, block_ref, raw, loads) = (
        refs[:6], refs[6:]
    )
    cells = cond.shape[0] // 2
    for i in range(3):
        raw[side(), i] = parts[i][...]
        raw[1 - side(), i] = parts[3 + i][...]
    for i in range(2):
        part = slice(i * cells, (i + 1) * cells)
        cond[part] = jnp.exp(raw[i, 0])
        storage[part] = raw[i, 1]
        loads[part] = raw[i, 1] * raw[i, 2] + sources[part]
    near, far = x_ends(cond)
    conds = [pair_cells(cond, i) for i in range(cells)]
    links = [harmonic(conds[i], conds[i + 1]) for i in range(cells - 1)] + [far]
    block, steps = eliminate(
        near,
        links,
        [pair_cells(storage, i) for i in range(cells)],
        [pair_cells(loads, i) for i in range(cells)],
    )
    keep_steps(steps_ref, steps)
    joined, steps = combine([[value[i] for value in block] for i in range(2)])
    keep_steps(pair_steps, steps)
    for i, value in enumerate(joined):
        block_ref[i] = value


def facing(near, far, stride):
    return jnp.where(spot_in(stride, 2) == 0, far, near)


def make_join(stride, count, two_left):
    def join(*refs):
        arrivals, (joined_ref, steps_ref, scratch) = refs[:count], refs[count:]
        place(scratch, arrivals, stride)
        joined, steps = combine([[scratch[i, j] for j in range(5)] for i in range(count)])
        if two_left:
            _, near_ground, far_ground, near_load, far_load = joined
            joined = [
                facing(near_ground, far_ground, stride * count),
                facing(near_load, far_load, stride * count),
            ]
        for i, value in enumerate(joined):
            joined_ref[i] = value
        keep_steps(steps_ref, steps)

    return join


def descend(levels, edges, scratch):
    for stride, steps in levels[:-1]:
        faces = expand(steps, *edges)
        edges = own_edges(scratch, spot_in(stride, len(steps) + 1), edges[0], faces, edges[1])
    return edges[0], expand(levels[-1][1], *edges)[0], edges[1]


def make_top(strides, counts):
    below = len(strides) - 1

    def top(*refs):
        arrivals = refs[:counts[-1]]
        lower, (faces_ref, steps_ref, scratch, edges) = (
            refs[counts[-1]:counts[-1] + below], refs[counts[-1] + below:]
        )
        nothing = jnp.zeros(faces_ref.shape[1:], f32)
        if counts[-1] == 2:
            ground, load = [arrivals[0][i] + arrivals[1][i] for i in range(2)]
            inverse = 1.0 / ground
            steps = [(inverse, nothing, nothing, inverse * load)]
        else:
            place(scratch, arrivals, strides[-1])
            _, steps = combine([[scratch[i, j] for j in range(5)] for i in range(counts[-1])])
        keep_steps(steps_ref, steps)
        levels = [(strides[-1], steps)] + [
            (strides[i], steps_of(lower[i])) for i in reversed(range(below))
        ]
        for i, value in enumerate(descend(levels, (nothing, nothing), edges)):
            faces_ref[i] = value

    return top


def both_edges(faces):
    return jnp.stack([faces[0], faces[1]]), jnp.stack([faces[1], faces[2]])


def y_spots(ref):
    return ref.shape[1] // chunks


def y_rows(ref, spot):
    return (slice(None), pl.ds(spot, chunks, stride=y_spots(ref)), slice(None))


def y_cells(ref):
    return [ref[y_rows(ref, spot)] for spot in range(y_spots(ref))]


def y_links(cond):
    me, count = row_block(), 2 * lax.axis_size("yz")
    cells = y_cells(cond)
    place_of = lax.broadcasted_iota(jnp.int32, cells[0].shape, 1)
    near = jnp.where((place_of == 0) & (me == 0), 0.0, 2.0 * cells[0])
    far = jnp.where((place_of == chunks - 1) & (me == count - 1), 0.0, 2.0 * cells[-1])
    return cells, near, far


def by_chunk(value, scratch):
    slab = value.shape[0]
    scratch[...] = value.reshape(slab * chunks, lanes)
    return [scratch[pl.ds(i, slab, stride=chunks), :] for i in range(chunks)]


def from_chunk(values, scratch):
    slab = values[0].shape[0]
    for i, value in enumerate(values):
        scratch[pl.ds(i, slab, stride=chunks), :] = value
    return scratch[...].reshape(slab, chunks, lanes)


def y_factor(cond, storage, cell_factors, chunk_factors, ends, turned):
    conds, near, far = y_links(cond)
    links = [harmonic(before, after) for before, after in zip(conds[:-1], conds[1:])] + [far]
    nothing = [jnp.zeros_like(near)] * len(conds)
    block, steps = eliminate(near, links, y_cells(storage), nothing)
    keep_steps(cell_factors, [step[:3] for step in steps])
    parts = [by_chunk(value, turned.at[i]) for i, value in enumerate(block[:3])]
    nothing = [jnp.zeros_like(parts[0][0])] * len(parts[0])
    joined, steps = combine(list(zip(*parts, nothing, nothing)))
    keep_steps(chunk_factors, [step[:3] for step in steps])
    for i in range(3):
        ends[i] = joined[i]


def z_links(cond):
    lane = lax.broadcasted_iota(jnp.int32, cond.shape, 1)
    after = pltpu.roll(cond, lanes - 1, 1)
    return lane == lanes - 1, after


def piece_of(ref, i, cuts):
    per = ref.shape[0] // cuts
    return ref[i * per:(i + 1) * per].reshape(per * ref.shape[1], lanes)


def turn_tiles(values, target):
    values = values.reshape(target.shape)
    for i in range(target.shape[0]):
        target[i] = values[i].T


def z_factor(cond, storage, cell_factors, joints, inverse_ref, cond_up, storage_up):
    turn_tiles(cond[...], cond_up)
    turn_tiles(storage[...], storage_up)
    conds = y_cells(cond_up)
    place_of = lax.broadcasted_iota(jnp.int32, conds[0].shape, 1)
    near = jnp.where(place_of == 0, 0.0, 2.0 * conds[0])
    far = jnp.where(place_of == chunks - 1, 0.0, 2.0 * conds[-1])
    links = [harmonic(before, after) for before, after in zip(conds[:-1], conds[1:])] + [far]
    nothing = [jnp.zeros_like(near)] * len(conds)
    block, steps = eliminate(near, links, y_cells(storage_up), nothing)
    keep_steps(cell_factors, [step[:3] for step in steps])
    link = pltpu.roll(block[0], chunks - 1, 1)
    ground = block[2] + pltpu.roll(block[1], chunks - 1, 1)
    ground = jnp.where(place_of == chunks - 1, 1.0, ground)
    for level in range(chunks.bit_length() - 1):
        shift = 1 << level
        link_back = pltpu.roll(link, shift, 1)
        inverse = 1.0 / (link + link_back + ground)
        passed, held = inverse * link, inverse * ground
        joints[level, 0] = pltpu.roll(passed, shift, 1)
        joints[level, 1] = link * pltpu.roll(inverse, chunks - shift, 1)
        ground = (
            ground
            + link * pltpu.roll(held, chunks - shift, 1)
            + link_back * pltpu.roll(held, shift, 1)
        )
        link = link * pltpu.roll(passed, chunks - shift, 1)
    inverse_ref[...] = 1.0 / ground


def z_sweep(loads, cell_factors, joints, inverse, solved):
    factors = factors_of(cell_factors)
    near, far, scaled = eliminate_loads(factors, y_cells(loads))
    load = far + pltpu.roll(near, chunks - 1, 1)
    for level in range(joints.shape[0]):
        shift = 1 << level
        load = (
            load
            + joints[level, 1] * pltpu.roll(load, chunks - shift, 1)
            + joints[level, 0] * pltpu.roll(load, shift, 1)
        )
    far = load * inverse[...]
    near = pltpu.roll(far, 1, 1)
    for spot, value in enumerate(expand(with_scaled(factors, scaled), near, far)):
        solved[y_rows(solved, spot)] = value


def make_points(slab, rows):
    def points(east, north, depth, heads, at_row, at_depth, here, observed):
        inside, spot = local_spot(east[...], north[...], slab, rows)
        at_row[...] = jnp.where(
            lax.broadcasted_iota(jnp.int32, at_row.shape, 0) == spot, 1.0, 0.0
        ).astype(jnp.bfloat16)
        at_depth[...] = jnp.where(
            lax.broadcasted_iota(jnp.int32, at_depth.shape, 0) == depth[...], 1.0, 0.0
        )
        here[...] = jnp.where(inside, 1.0, 0.0)
        observed[...] = heads[...]

    return points


def y_forward(x_faces, x_steps, storage, cell_factors, chunk_factors, ends,
              head_first, scaled_cells, scaled_chunks, message, loads, turned):
    cells = head_first.shape[0] // 2
    near, far = both_edges(x_faces)
    for i in reversed(range(cells)):
        far = x_steps[i, 3] + x_steps[i, 1] * near + x_steps[i, 2] * far
        for j in range(2):
            head_first[j * cells + i] = far[j]
            loads[j * cells + i] = storage[j * cells + i] * far[j]
    for i in range(3):
        message[i] = ends[i]
    near, far = y_loads(loads, cell_factors, chunk_factors, scaled_cells, scaled_chunks, turned)
    message[3] = near
    message[4] = far


def y_loads(loads, cell_factors, chunk_factors, scaled_cells, scaled_chunks, turned):
    near, far, scaled = eliminate_loads(
        factors_of(cell_factors), y_cells(loads)
    )
    for i, value in enumerate(scaled):
        scaled_cells[i] = value
    blocks = list(zip(by_chunk(near, turned.at[0]), by_chunk(far, turned.at[1])))
    joined, scaled = combine_loads(blocks, factors_of(chunk_factors))
    for i, value in enumerate(scaled):
        scaled_chunks[i] = value
    return joined


def y_expand(near, far, cell_factors, chunk_factors, scaled_cells, scaled_chunks,
             turned, solved, edges, natural):
    factors = factors_of(chunk_factors)
    steps = with_scaled(factors, [scaled_chunks[i] for i in range(len(factors))])
    faces = [near] + expand(steps, near, far) + [far]
    near = from_chunk(faces[:-1], turned.at[0])
    far = from_chunk(faces[1:], turned.at[1])
    edges[0] = near
    edges[1] = far
    for spot in reversed(range(y_spots(natural))):
        far = scaled_cells[spot] + cell_factors[spot, 1] * near + cell_factors[spot, 2] * far
        solved[spot] = far
        natural[y_rows(natural, spot)] = far


def make_z(count):
    def z_solve(*refs):
        arrivals = refs[:count]
        (cell_factors, chunk_factors, scaled_cells, scaled_chunks, storage,
         z_factors, joints, inverse, at_row, at_depth, here, observed,
         y_factors, head_second, y_edges, head_up, adjoint_third, message,
         next_cells, next_chunks,
         scratch, edges, turned, loads, second) = refs[count:]
        me = row_block()
        for turn, arrival in enumerate(arrivals):
            scratch[me ^ turn] = arrival[...]
        nothing = jnp.zeros(arrivals[0].shape[1:], f32)
        _, steps = combine([[scratch[i, j] for j in range(5)] for i in range(count)])
        keep_steps(y_factors, [step[:3] for step in steps])
        near, far = own_edges(edges, me, nothing, expand(steps, nothing, nothing), nothing)
        y_expand(near, far, cell_factors, chunk_factors, scaled_cells, scaled_chunks,
                 turned, head_second, y_edges, second)

        slab = storage.shape[0]
        turn_tiles(storage[...] * second[...], loads)
        tiles = loads.shape[0]
        z_sweep(loads, z_factors, joints, inverse, head_up)
        found = jnp.dot(
            jnp.concatenate(
                bf16_parts(jnp.concatenate([head_up[i] for i in range(tiles)], axis=1), 2), axis=0
            ),
            at_row[...],
            preferred_element_type=f32,
        )
        found = jnp.sum(
            at_depth[...] * (found[:lanes] + found[lanes:]), axis=0, keepdims=True
        )
        misfit = here[...] * (found - observed[...])
        for i in range(misfit.shape[1] // lanes):
            row = 2 * slab + i
            message[row:row + 1, :] = misfit[:, i * lanes:(i + 1) * lanes]
        parts = [
            (at_depth[...] * part.astype(f32)).astype(jnp.bfloat16)
            for part in bf16_parts(misfit_weight * misfit, 2)
        ]
        source = lax.dot_general(
            jnp.concatenate(parts, axis=0), at_row[...],
            (((1,), (1,)), ((), ())), preferred_element_type=f32,
        )
        for i in range(tiles):
            tile = slice(i * lanes, (i + 1) * lanes)
            loads[i] = source[:lanes, tile] + source[lanes:, tile]
        z_sweep(loads, z_factors, joints, inverse, loads)
        adjoint_third[...] = jnp.stack([loads[i].T for i in range(tiles)]).reshape(second.shape)
        second[...] = storage[...] * adjoint_third[...]
        near, far = y_loads(second, cell_factors, chunk_factors, next_cells, next_chunks, turned)
        message[:slab] = near
        message[slab:2 * slab] = far

    return z_solve


def lay_head(head_up, head_third, head_send):
    cells = head_send.shape[0]
    tiles = head_up.shape[0]
    head_third[...] = jnp.stack([head_up[i].T for i in range(tiles)]).reshape(head_third.shape)
    head_send[...] = head_third[pl.ds((1 - side()) * cells, cells)]


def make_y_back(count):
    def y_back(*refs):
        arrivals = refs[:count]
        (y_factors, cell_factors, chunk_factors, scaled_cells, scaled_chunks, storage, x_steps,
         pair_steps, adjoint_second, y_edges, scaled_x, pair_scaled, note,
         scratch, edges, turned, second) = refs[count:]
        me, slab = row_block(), storage.shape[0]
        misfit = None
        for turn, arrival in enumerate(arrivals):
            scratch[me ^ turn, 0] = arrival[:slab]
            scratch[me ^ turn, 1] = arrival[slab:2 * slab]
            part = arrival[2 * slab:]
            misfit = part if misfit is None else misfit + part
        nothing = jnp.zeros(scratch.shape[2:], f32)
        factors = factors_of(y_factors)
        _, scaled = combine_loads([[scratch[i, 0], scratch[i, 1]] for i in range(count)], factors)
        faces = expand(with_scaled(factors, scaled), nothing, nothing)
        near, far = own_edges(edges, me, nothing, faces, nothing)
        y_expand(near, far, cell_factors, chunk_factors, scaled_cells, scaled_chunks,
                 turned, adjoint_second, y_edges, second)
        for i in range(slab):
            second[i] = storage[i] * second[i]
        near, far, scaled = eliminate_loads(
            factors_of(x_steps), [pair_cells(second, i) for i in range(slab // 2)]
        )
        for i, value in enumerate(scaled):
            scaled_x[i] = value
        (near, far), scaled = combine_loads(
            [[near[i], far[i]] for i in range(2)], factors_of(pair_steps)
        )
        pair_scaled[0] = scaled[0]
        rows = near.shape[0]
        note[:rows] = near
        note[rows:2 * rows] = far
        note[2 * rows:] = misfit

    return y_back


def make_terms(cuts):
    def gather_terms(cond, head_third, adjoint_third, head_second, adjoint_second,
                     head_edges, adjoint_edges, terms, natural):
        conds, near_link, far_link = y_links(cond)
        from_left = (
            -near_link * (adjoint_second[0] - adjoint_edges[0]) * (head_second[0] - head_edges[0])
        )
        spots = len(conds)
        for spot in range(spots):
            if spot < spots - 1:
                to_left, to_right = face_gradient(
                    conds[spot], conds[spot + 1],
                    adjoint_second[spot] - adjoint_second[spot + 1],
                    head_second[spot] - head_second[spot + 1],
                )
            else:
                to_left = (
                    -far_link * (adjoint_second[spot] - adjoint_edges[1])
                    * (head_second[spot] - head_edges[1])
                )
            natural[y_rows(natural, spot)] = from_left + to_left
            from_left = to_right
        slab, rows, _ = cond.shape
        per = slab // cuts
        for i in range(cuts):
            here, head, adjoint = [
                piece_of(ref, i, cuts) for ref in (cond, head_third, adjoint_third)
            ]
            last, after = z_links(here)
            to_left, to_right = face_gradient(
                here, after,
                adjoint - pltpu.roll(adjoint, lanes - 1, 1),
                head - pltpu.roll(head, lanes - 1, 1),
            )
            to_left = jnp.where(last, 0.0, to_left)
            to_right = jnp.where(last, 0.0, to_right)
            value = (to_left + pltpu.roll(to_right, 1, 1)).reshape(per, rows, lanes)
            terms[i * per:(i + 1) * per] = value + natural[i * per:(i + 1) * per]

    return gather_terms


def loads_in(arrivals, scratch, stride):
    rows, count = scratch.shape[2], len(arrivals)
    misfit = None
    for turn, arrival in enumerate(arrivals):
        position = spot_in(stride, count) ^ turn
        scratch[position, 0] = arrival[:rows]
        scratch[position, 1] = arrival[rows:2 * rows]
        part = arrival[2 * rows:]
        misfit = part if misfit is None else misfit + part
    return [[scratch[i, 0], scratch[i, 1]] for i in range(count)], misfit


def make_join_loads(stride, count, two_left):
    def join(*refs):
        arrivals, (steps_ref, message, scaled_ref, scratch) = refs[:count], refs[count:]
        blocks, misfit = loads_in(arrivals, scratch, stride)
        joined, scaled = combine_loads(blocks, factors_of(steps_ref))
        rows = scratch.shape[2]
        if two_left:
            message[:rows] = facing(*joined, stride * count)
            message[rows:] = misfit
        else:
            message[:rows] = joined[0]
            message[rows:2 * rows] = joined[1]
            message[2 * rows:] = misfit
        for i, value in enumerate(scaled):
            scaled_ref[i] = value

    return join


def make_top_loads(strides, counts):
    below = len(strides) - 1

    def top(*refs):
        arrivals, refs = refs[:counts[-1]], refs[counts[-1]:]
        top_steps, lower, lower_scaled = refs[0], refs[1:1 + below], refs[1 + below:1 + 2 * below]
        faces_ref, misfit_ref, scratch, edges = refs[1 + 2 * below:]
        nothing = jnp.zeros(scratch.shape[2:], f32)
        factors = factors_of(top_steps)
        if counts[-1] == 2:
            rows = nothing.shape[0]
            total = arrivals[0][...] + arrivals[1][...]
            scaled, misfit = [factors[0][0] * total[:rows]], total[rows:]
        else:
            blocks, misfit = loads_in(arrivals, scratch, strides[-1])
            scaled = combine_loads(blocks, factors)[1]
        levels = [(strides[-1], with_scaled(factors, scaled))]
        for i in reversed(range(below)):
            factors = factors_of(lower[i])
            scaled = [lower_scaled[i][j] for j in range(len(factors))]
            levels.append((strides[i], with_scaled(factors, scaled)))
        misfit_ref[...] = misfit
        for i, value in enumerate(descend(levels, (nothing, nothing), edges)):
            faces_ref[i] = value

    return top


def x_back(faces, head_faces, x_steps, scaled_x, cond, head, terms, own, send, gradient):
    cells = cond.shape[0] // 2
    near, far = both_edges(faces)
    head_near, head_far = both_edges(head_faces)
    near_link, far_link = x_ends(cond)
    conds = [pair_cells(cond, i) for i in range(cells)]
    heads = [pair_cells(head, i) for i in range(cells)]
    adjoint = [None] * cells
    after = far
    for i in reversed(range(cells)):
        after = scaled_x[i] + x_steps[i, 1] * near + x_steps[i, 2] * after
        adjoint[i] = after
    from_left = -near_link * (adjoint[0] - near) * (heads[0] - head_near)
    for i in range(cells):
        if i < cells - 1:
            to_left, to_right = face_gradient(
                conds[i], conds[i + 1], adjoint[i] - adjoint[i + 1], heads[i] - heads[i + 1]
            )
        else:
            to_left = -far_link * (adjoint[i] - far) * (heads[i] - head_far)
        value = from_left + to_left
        for j in range(2):
            gradient[j * cells + i] = terms[j * cells + i] + value[j]
        from_left = to_right
    own[...] = gradient[pl.ds(side() * cells, cells)]
    send[...] = gradient[pl.ds((1 - side()) * cells, cells)]


def settle(own, other, whole, full):
    cells, half, _ = other.shape
    start = (own.shape[0] - cells) // cells * side() * cells
    full[:, pl.ds(pl.multiple_of(side() * half, half), half), :] = own[pl.ds(start, cells)]
    full[:, pl.ds(pl.multiple_of((1 - side()) * half, half), half), :] = other[...]
    whole[...] = full[...]


def settle_last(own, other, misfits, whole, misfits_out, full):
    misfits_out[...] = misfits[...]
    settle(own, other, whole, full)


def shards(log_cond, storage, head, well_east, well_north, well_depth, pump_rates,
           probe_east, probe_north, probe_depth, probe_heads):
    cells, rows, _ = log_cond.shape
    devices, columns = lax.axis_size("gx"), lax.axis_size("yz")
    inner = 4 if devices >= 16 else 2
    strides, counts = [1, 2, 2 * inner], [2, inner, devices // (2 * inner)]
    two_left = counts[-1] == 2
    slab, half = 2 * cells, rows // 2
    points = probe_heads.shape[0]
    grid = (slab, half, lanes)
    plane = (half, lanes)
    spots = half // chunks
    cell = (spots, slab, chunks, lanes)
    line = (slab, lanes)
    turned = (slab * chunks, lanes)

    places = ((well_east << (2 * field)) + (well_north << field) + well_depth).reshape(1, -1)
    probes = [value.reshape(1, -1) for value in (probe_east, probe_north, probe_depth, probe_heads)]
    parts = run(
        x_load,
        [(cells,) + plane] * 6,
        [log_cond, storage, head],
        [pltpu.SemaphoreType.DMA((6,))],
        raw=3,
        limit=53,
    )
    (sources,) = run(
        make_wells(slab, half), [grid], [places, jnp.where(places >= 0, pump_rates.reshape(1, -1), 0.0)], after=[parts[3]]
    )
    cond, storage, x_steps, pair_steps, joined = run(
        x_reduce,
        [grid, grid, (cells, 4, 2) + plane, (1, 4) + plane, (5,) + plane],
        list(parts[:3]) + [swap(part) for part in parts[3:]] + [sources],
        [((2, 3, cells) + plane, f32), (grid, f32)],
    )
    x_levels = [pair_steps]
    cell_factors, chunk_factors, ends = run(
        y_factor,
        [(spots, 3) + cell[1:], (chunks - 1, 3) + line, (3,) + line],
        [cond, storage],
        [((3,) + turned, f32)],
        after=[joined],
    )

    cuts = 4
    tiles = slab * half // lanes
    upright = (tiles, lanes, lanes)
    z_cell = (tiles, chunks, lanes)
    for i, (stride, count) in enumerate(zip(strides[1:], counts[1:])):
        arrivals = exchange(joined, stride, count)
        waits = []
        if i == 0:
            z_factors, joints, inverse = run(
                z_factor,
                [(lanes // chunks, 3) + z_cell, (chunks.bit_length() - 1, 2) + z_cell, z_cell],
                [cond, storage],
                [(upright, f32), (upright, f32)],
                after=[joined],
            )
            waits = [ends, inverse]
        if i < len(strides) - 2:
            joined, steps = run(
                make_join(stride, count, i == len(strides) - 3 and two_left),
                [(2 if i == len(strides) - 3 and two_left else 5,) + plane,
                 (count - 1, 4) + plane],
                arrivals,
                [((count, 5) + plane, f32)],
                after=waits,
            )
            x_levels.append(steps)
    x_faces, steps = run(
        make_top(strides, counts),
        [(3,) + plane, (counts[-1] - 1, 4) + plane],
        arrivals + x_levels,
        [((counts[-1], 5) + plane, f32), ((max(counts) + 1,) + plane, f32)],
        after=waits,
    )
    x_levels.append(steps)
    head_first, scaled_cells, scaled_chunks, message = run(
        y_forward,
        [grid, cell, (chunks - 1,) + line, (5,) + line],
        [x_faces, x_steps, storage, cell_factors, chunk_factors, ends],
        [(grid, f32), ((2,) + turned, f32)],
    )
    at_row, at_depth, here, observed = run(
        make_points(slab, half),
        [((slab * half, points), jnp.bfloat16), (lanes, points), (1, points), (1, points)],
        probes,
        after=[message],
    )
    extra, blocks = points // lanes, 2 * columns
    (y_factors, head_second, head_edges, head_up, adjoint_third, message,
     scaled_cells, scaled_chunks) = run(
        make_z(blocks),
        [(blocks - 1, 3) + line, cell, (2,) + cell[1:], upright, grid,
         (2 * slab + extra, lanes), cell, (chunks - 1,) + line],
        exchange_rows(message)
        + [cell_factors, chunk_factors, scaled_cells, scaled_chunks, storage,
           z_factors, joints, inverse, at_row, at_depth, here, observed],
        [((blocks, 5) + line, f32), ((blocks + 1,) + line, f32), ((2,) + turned, f32),
         (upright, f32), (grid, f32)],
    )
    head_third, head_send = run(
        lay_head, [grid, (cells,) + plane], [head_up], after=[message]
    )
    note = (2 * half + extra, lanes)
    adjoint_second, adjoint_edges, scaled_x, scaled, message = run(
        make_y_back(blocks),
        [cell, (2,) + cell[1:], (cells, 2) + plane, (1,) + plane, note],
        exchange_rows(message)
        + [y_factors, cell_factors, chunk_factors, scaled_cells, scaled_chunks, storage, x_steps,
           pair_steps],
        [((blocks, 2) + line, f32), ((blocks + 1,) + line, f32), ((2,) + turned, f32),
         (grid, f32)],
    )
    x_scaled = [scaled]
    (terms,) = run(
        make_terms(cuts),
        [grid],
        [cond, head_third, adjoint_third, head_second, adjoint_second, head_edges, adjoint_edges],
        [(grid, f32)],
    )
    for i in range(1, len(strides) - 1):
        arrivals = exchange(message, strides[i], counts[i])
        message, scaled = run(
            make_join_loads(strides[i], counts[i], i == len(strides) - 2 and two_left),
            [(half + extra, lanes) if i == len(strides) - 2 and two_left else note,
             (counts[i] - 1,) + plane],
            arrivals + [x_levels[i]],
            [((counts[i], 2) + plane, f32)],
        )
        x_scaled.append(scaled)
    faces, misfits = run(
        make_top_loads(strides, counts),
        [(3,) + plane, (extra, lanes)],
        exchange(message, strides[-1], counts[-1]) + x_levels[-1:] + x_levels[:-1] + x_scaled,
        [((counts[-1], 2) + plane, f32), ((max(counts) + 1,) + plane, f32)],
        after=[terms],
    )
    whole = (cells, rows, lanes)
    (head_next,) = run(settle, [whole], [head_third, swap(head_send)], [(whole, f32)])
    own, send = run(
        x_back,
        [(cells,) + plane, (cells,) + plane],
        [faces, x_faces, x_steps, scaled_x, cond, head_first, terms],
        [(grid, f32)],
    )
    gradient, misfits = run(
        settle_last, [whole, (extra, lanes)], [own, swap(send), misfits], [(whole, f32)]
    )
    return head_next, gradient, misfits.reshape(-1)


def solution(mesh):
    cells = P("gx", "yz", None)
    return jax.shard_map(
        shards,
        mesh=mesh,
        in_specs=(cells, cells, cells) + (P(),) * 8,
        out_specs=(cells, cells, P()),
        check_vma=False,
    )
```

```python
import jax
import jax.numpy as jnp
from jax import lax
from jax.experimental import pallas as pl
from jax.experimental.pallas import tpu as pltpu
from jax.sharding import PartitionSpec as P


f32 = jnp.float32
misfit_weight = 100.0
lanes = 128
chunks = 8
field = 10
mask = (1 << field) - 1


def harmonic(left_cond, right_cond):
    return 2.0 * left_cond * right_cond / (left_cond + right_cond)


def eliminate(entry, links, grounds, loads):
    near_ground = near_load = far_ground = far_load = None
    steps = []
    for link, ground, load in zip(links, grounds, loads):
        if far_ground is not None:
            ground, load = ground + far_ground, load + far_load
        inverse = 1.0 / (entry + link + ground)
        to_near, to_far = entry * inverse, link * inverse
        far_ground, far_load = to_far * ground, to_far * load
        if near_ground is None:
            near_ground, near_load = to_near * ground, to_near * load
        else:
            near_ground, near_load = near_ground + to_near * ground, near_load + to_near * load
        steps.append((inverse, to_near, to_far, inverse * load))
        entry = to_near * link
    return (entry, near_ground, far_ground, near_load, far_load), steps


def eliminate_loads(factors, loads):
    near_load = far_load = None
    scaled = []
    for (inverse, to_near, to_far), load in zip(factors, loads):
        if far_load is not None:
            load = load + far_load
        far_load = to_far * load
        near_load = to_near * load if near_load is None else near_load + to_near * load
        scaled.append(inverse * load)
    return near_load, far_load, scaled


def expand(steps, near, far):
    values = []
    for _, to_near, to_far, scaled in reversed(steps):
        far = scaled + to_near * near + to_far * far
        values.append(far)
    return values[::-1]


def combine(blocks):
    pairs = list(zip(blocks[:-1], blocks[1:]))
    (entry, near_ground, far_ground, near_load, far_load), steps = eliminate(
        blocks[0][0],
        [after[0] for _, after in pairs],
        [before[2] + after[1] for before, after in pairs],
        [before[4] + after[3] for before, after in pairs],
    )
    joined = (
        entry,
        blocks[0][1] + near_ground,
        blocks[-1][2] + far_ground,
        blocks[0][3] + near_load,
        blocks[-1][4] + far_load,
    )
    return joined, steps


def combine_loads(blocks, factors):
    near_load, far_load, scaled = eliminate_loads(
        factors, [before[1] + after[0] for before, after in zip(blocks[:-1], blocks[1:])]
    )
    return (blocks[0][0] + near_load, blocks[-1][1] + far_load), scaled


def with_scaled(factors, scaled):
    return [factor + (value,) for factor, value in zip(factors, scaled)]


def factors_of(ref):
    return [(ref[i, 0], ref[i, 1], ref[i, 2]) for i in range(ref.shape[0])]


def steps_of(ref):
    return [(None, ref[i, 1], ref[i, 2], ref[i, 3]) for i in range(ref.shape[0])]


def keep_steps(ref, steps):
    for i, step in enumerate(steps):
        for j, value in enumerate(step):
            ref[i, j] = value


def face_gradient(left_cond, right_cond, adjoint_drop, head_drop):
    total = 1.0 / (left_cond + right_cond)
    flow = -(adjoint_drop * head_drop) * (2.0 * left_cond * right_cond * total) * total
    return flow * right_cond, flow * left_cond


def bf16_parts(values, count):
    parts = []
    for _ in range(count):
        part = values.astype(jnp.bfloat16)
        parts.append(part)
        values = values - part.astype(jnp.float32)
    return parts


def run(body, outs, ins, scratch=(), raw=0, after=(), flops=1000000, limit=24):
    shapes = [
        jax.ShapeDtypeStruct(*((out, f32) if isinstance(out[0], int) else out)) for out in outs
    ]
    size = 4 * (sum(x.size for x in ins) + sum(x.size for x in shapes))
    places = [pltpu.HBM] * raw + [pltpu.VMEM] * (len(ins) - raw) + [pl.ANY] * len(after)
    count = len(ins)

    def ordered(*refs):
        return body(*refs[:count], *refs[count + len(after):])

    return pl.pallas_call(
        ordered,
        out_shape=shapes,
        in_specs=[pl.BlockSpec(memory_space=place) for place in places],
        out_specs=[pl.BlockSpec(memory_space=pltpu.VMEM)] * len(outs),
        scratch_shapes=[
            item if not isinstance(item, tuple) else pltpu.VMEM(*item) for item in scratch
        ],
        compiler_params=pltpu.CompilerParams(vmem_limit_bytes=int(limit * 1024 * 1024)),
        cost_estimate=pl.CostEstimate(flops=flops, bytes_accessed=size, transcendentals=0),
    )(*ins, *after)


def spot_in(stride, count):
    return lax.rem(lax.axis_index("gx") // stride, count)


def place(scratch, arrivals, stride):
    position = spot_in(stride, len(arrivals))
    for turn, arrival in enumerate(arrivals):
        scratch[position ^ turn] = arrival[...]


def exchange(value, stride, count):
    size = lax.axis_size("gx")
    return [value] + [
        lax.ppermute(value, "gx", [(i, i ^ (turn * stride)) for i in range(size)])
        for turn in range(1, count)
    ]


def swap(value):
    return exchange(value, 1, 2)[1]


def exchange_rows(value):
    size, columns = lax.axis_size("gx"), lax.axis_size("yz")
    return [value] + [
        lax.ppermute(
            value,
            ("gx", "yz"),
            [
                (i * columns + j, (i ^ (turn % 2)) * columns + (j ^ (turn // 2)))
                for i in range(size)
                for j in range(columns)
            ],
        )
        for turn in range(1, 2 * columns)
    ]


def side():
    return lax.rem(lax.axis_index("gx"), 2)


def row_block():
    return lax.axis_index("yz") * 2 + side()


def local_spot(east, north, slab, rows):
    local_east = east - lax.axis_index("gx") // 2 * slab
    local_north = north - row_block() * rows
    inside = (
        (local_east >= 0) & (local_east < slab) & (local_north >= 0) & (local_north < rows)
    )
    return inside, jnp.where(inside, local_east * rows + local_north, -1)


def own_edges(scratch, position, near, faces, far):
    for i, value in enumerate([near] + faces + [far]):
        scratch[i] = value
    return scratch[position], scratch[position + 1]


def pair_cells(ref, i):
    cells = ref.shape[0] // 2
    return jnp.stack([ref[i], ref[cells + i]])


def x_ends(cond):
    pair, count = lax.axis_index("gx") // 2, lax.axis_size("gx") // 2
    cells = cond.shape[0]
    near = [jnp.where(pair == 0, 0.0, 2.0) * cond[0], 2.0 * cond[cells // 2]]
    far = [2.0 * cond[cells // 2 - 1], jnp.where(pair == count - 1, 0.0, 2.0) * cond[cells - 1]]
    return jnp.stack(near), jnp.stack(far)


def x_load(log_cond, storage, head, *refs):
    targets, done = refs[:6], refs[6]
    half = targets[0].shape[1]
    moves = []
    for part, some in ((1 - side(), targets[3:]), (side(), targets[:3])):
        rows = pl.ds(pl.multiple_of(part * half, half), half)
        for source, target in zip((log_cond, storage, head), some):
            moves.append(
                pltpu.make_async_copy(source.at[:, rows, :], target, done.at[len(moves)])
            )
    for move in moves:
        move.start()
    for move in moves:
        move.wait()


def make_wells(slab, rows):
    def wells(places, rates, sources):
        _, spot = local_spot(
            lax.shift_right_logical(places[...], 2 * field),
            lax.shift_right_logical(places[...], field) & mask,
            slab,
            rows,
        )
        count = rates.shape[1]
        at_row = jnp.where(
            lax.broadcasted_iota(jnp.int32, (slab * rows, count), 0) == spot, 1.0, 0.0
        ).astype(jnp.bfloat16)
        at_depth = (
            lax.broadcasted_iota(jnp.int32, (lanes, count), 0) == (places[...] & mask)
        )
        sources[...] = sum(
            lax.dot_general(
                at_row, part, (((1,), (1,)), ((), ())), preferred_element_type=f32
            )
            for part in bf16_parts(jnp.where(at_depth, rates[...], 0.0), 3)
        ).reshape(slab, rows, lanes)

    return wells


def x_prepare(log_cond, storage, head, sources, cond_own, load_own):
    cells = log_cond.shape[0]
    cond_own[...] = jnp.exp(log_cond[...])
    load_own[...] = storage[...] * head[...] + sources[pl.ds(side() * cells, cells)]


def x_reduce(cond_own, storage_own, load_own, log_cond_other, storage_other, head_other, sources,
             cond, storage, steps_ref, pair_steps, block_ref, loads):
    cells = cond_own.shape[0]
    mine, rest = pl.ds(side() * cells, cells), pl.ds((1 - side()) * cells, cells)
    cond[mine] = cond_own[...]
    storage[mine] = storage_own[...]
    loads[mine] = load_own[...]
    cond[rest] = jnp.exp(log_cond_other[...])
    storage[rest] = storage_other[...]
    loads[rest] = storage_other[...] * head_other[...] + sources[rest]
    near, far = x_ends(cond)
    conds = [pair_cells(cond, i) for i in range(cells)]
    links = [harmonic(conds[i], conds[i + 1]) for i in range(cells - 1)] + [far]
    block, steps = eliminate(
        near,
        links,
        [pair_cells(storage, i) for i in range(cells)],
        [pair_cells(loads, i) for i in range(cells)],
    )
    keep_steps(steps_ref, steps)
    joined, steps = combine([[value[i] for value in block] for i in range(2)])
    keep_steps(pair_steps, steps)
    for i, value in enumerate(joined):
        block_ref[i] = value


def facing(near, far, stride):
    return jnp.where(spot_in(stride, 2) == 0, far, near)


def make_join(stride, count, two_left):
    def join(*refs):
        arrivals, (joined_ref, steps_ref, scratch) = refs[:count], refs[count:]
        place(scratch, arrivals, stride)
        joined, steps = combine([[scratch[i, j] for j in range(5)] for i in range(count)])
        if two_left:
            _, near_ground, far_ground, near_load, far_load = joined
            joined = [
                facing(near_ground, far_ground, stride * count),
                facing(near_load, far_load, stride * count),
            ]
        for i, value in enumerate(joined):
            joined_ref[i] = value
        keep_steps(steps_ref, steps)

    return join


def descend(levels, edges, scratch):
    for stride, steps in levels[:-1]:
        faces = expand(steps, *edges)
        edges = own_edges(scratch, spot_in(stride, len(steps) + 1), edges[0], faces, edges[1])
    return edges[0], expand(levels[-1][1], *edges)[0], edges[1]


def make_top(strides, counts):
    below = len(strides) - 1

    def top(*refs):
        arrivals = refs[:counts[-1]]
        lower, (faces_ref, steps_ref, scratch, edges) = (
            refs[counts[-1]:counts[-1] + below], refs[counts[-1] + below:]
        )
        nothing = jnp.zeros(faces_ref.shape[1:], f32)
        if counts[-1] == 2:
            ground, load = [arrivals[0][i] + arrivals[1][i] for i in range(2)]
            inverse = 1.0 / ground
            steps = [(inverse, nothing, nothing, inverse * load)]
        else:
            place(scratch, arrivals, strides[-1])
            _, steps = combine([[scratch[i, j] for j in range(5)] for i in range(counts[-1])])
        keep_steps(steps_ref, steps)
        levels = [(strides[-1], steps)] + [
            (strides[i], steps_of(lower[i])) for i in reversed(range(below))
        ]
        for i, value in enumerate(descend(levels, (nothing, nothing), edges)):
            faces_ref[i] = value

    return top


def both_edges(faces):
    return jnp.stack([faces[0], faces[1]]), jnp.stack([faces[1], faces[2]])


def y_spots(ref):
    return ref.shape[1] // chunks


def y_rows(ref, spot):
    return (slice(None), pl.ds(spot, chunks, stride=y_spots(ref)), slice(None))


def y_cells(ref):
    return [ref[y_rows(ref, spot)] for spot in range(y_spots(ref))]


def y_links(cond):
    me, count = row_block(), 2 * lax.axis_size("yz")
    cells = y_cells(cond)
    place_of = lax.broadcasted_iota(jnp.int32, cells[0].shape, 1)
    near = jnp.where((place_of == 0) & (me == 0), 0.0, 2.0 * cells[0])
    far = jnp.where((place_of == chunks - 1) & (me == count - 1), 0.0, 2.0 * cells[-1])
    return cells, near, far


def by_chunk(value, scratch):
    slab = value.shape[0]
    scratch[...] = value.reshape(slab * chunks, lanes)
    return [scratch[pl.ds(i, slab, stride=chunks), :] for i in range(chunks)]


def from_chunk(values, scratch):
    slab = values[0].shape[0]
    for i, value in enumerate(values):
        scratch[pl.ds(i, slab, stride=chunks), :] = value
    return scratch[...].reshape(slab, chunks, lanes)


def y_factor(cond, storage, cell_factors, chunk_factors, ends, turned):
    conds, near, far = y_links(cond)
    links = [harmonic(before, after) for before, after in zip(conds[:-1], conds[1:])] + [far]
    nothing = [jnp.zeros_like(near)] * len(conds)
    block, steps = eliminate(near, links, y_cells(storage), nothing)
    keep_steps(cell_factors, [step[:3] for step in steps])
    parts = [by_chunk(value, turned.at[i]) for i, value in enumerate(block[:3])]
    nothing = [jnp.zeros_like(parts[0][0])] * len(parts[0])
    joined, steps = combine(list(zip(*parts, nothing, nothing)))
    keep_steps(chunk_factors, [step[:3] for step in steps])
    for i in range(3):
        ends[i] = joined[i]


def z_links(cond):
    lane = lax.broadcasted_iota(jnp.int32, cond.shape, 1)
    after = pltpu.roll(cond, lanes - 1, 1)
    return lane == lanes - 1, after


def piece_of(ref, i, cuts):
    per = ref.shape[0] // cuts
    return ref[i * per:(i + 1) * per].reshape(per * ref.shape[1], lanes)


def turn_tiles(values, target):
    values = values.reshape(target.shape)
    for i in range(target.shape[0]):
        target[i] = values[i].T


def z_factor(cond, storage, cell_factors, joints, inverse_ref, cond_up, storage_up):
    turn_tiles(cond[...], cond_up)
    turn_tiles(storage[...], storage_up)
    conds = y_cells(cond_up)
    place_of = lax.broadcasted_iota(jnp.int32, conds[0].shape, 1)
    near = jnp.where(place_of == 0, 0.0, 2.0 * conds[0])
    far = jnp.where(place_of == chunks - 1, 0.0, 2.0 * conds[-1])
    links = [harmonic(before, after) for before, after in zip(conds[:-1], conds[1:])] + [far]
    nothing = [jnp.zeros_like(near)] * len(conds)
    block, steps = eliminate(near, links, y_cells(storage_up), nothing)
    keep_steps(cell_factors, [step[:3] for step in steps])
    link = pltpu.roll(block[0], chunks - 1, 1)
    ground = block[2] + pltpu.roll(block[1], chunks - 1, 1)
    ground = jnp.where(place_of == chunks - 1, 1.0, ground)
    for level in range(chunks.bit_length() - 1):
        shift = 1 << level
        link_back = pltpu.roll(link, shift, 1)
        inverse = 1.0 / (link + link_back + ground)
        passed, held = inverse * link, inverse * ground
        joints[level, 0] = pltpu.roll(passed, shift, 1)
        joints[level, 1] = link * pltpu.roll(inverse, chunks - shift, 1)
        ground = (
            ground
            + link * pltpu.roll(held, chunks - shift, 1)
            + link_back * pltpu.roll(held, shift, 1)
        )
        link = link * pltpu.roll(passed, chunks - shift, 1)
    inverse_ref[...] = 1.0 / ground


def z_sweep(loads, cell_factors, joints, inverse, solved):
    factors = factors_of(cell_factors)
    near, far, scaled = eliminate_loads(factors, y_cells(loads))
    load = far + pltpu.roll(near, chunks - 1, 1)
    for level in range(joints.shape[0]):
        shift = 1 << level
        load = (
            load
            + joints[level, 1] * pltpu.roll(load, chunks - shift, 1)
            + joints[level, 0] * pltpu.roll(load, shift, 1)
        )
    far = load * inverse[...]
    near = pltpu.roll(far, 1, 1)
    for spot, value in enumerate(expand(with_scaled(factors, scaled), near, far)):
        solved[y_rows(solved, spot)] = value


def make_points(slab, rows):
    def points(east, north, depth, heads, at_row, at_depth, here, observed):
        inside, spot = local_spot(east[...], north[...], slab, rows)
        at_row[...] = jnp.where(
            lax.broadcasted_iota(jnp.int32, at_row.shape, 0) == spot, 1.0, 0.0
        ).astype(jnp.bfloat16)
        at_depth[...] = jnp.where(
            lax.broadcasted_iota(jnp.int32, at_depth.shape, 0) == depth[...], 1.0, 0.0
        )
        here[...] = jnp.where(inside, 1.0, 0.0)
        observed[...] = heads[...]

    return points


def y_forward(x_faces, x_steps, storage, cell_factors, chunk_factors, ends,
              head_first, scaled_cells, scaled_chunks, message, loads, turned):
    cells = head_first.shape[0] // 2
    near, far = both_edges(x_faces)
    for i in reversed(range(cells)):
        far = x_steps[i, 3] + x_steps[i, 1] * near + x_steps[i, 2] * far
        for j in range(2):
            head_first[j * cells + i] = far[j]
            loads[j * cells + i] = storage[j * cells + i] * far[j]
    for i in range(3):
        message[i] = ends[i]
    near, far = y_loads(loads, cell_factors, chunk_factors, scaled_cells, scaled_chunks, turned)
    message[3] = near
    message[4] = far


def y_loads(loads, cell_factors, chunk_factors, scaled_cells, scaled_chunks, turned):
    near, far, scaled = eliminate_loads(
        factors_of(cell_factors), y_cells(loads)
    )
    for i, value in enumerate(scaled):
        scaled_cells[i] = value
    blocks = list(zip(by_chunk(near, turned.at[0]), by_chunk(far, turned.at[1])))
    joined, scaled = combine_loads(blocks, factors_of(chunk_factors))
    for i, value in enumerate(scaled):
        scaled_chunks[i] = value
    return joined


def y_expand(near, far, cell_factors, chunk_factors, scaled_cells, scaled_chunks,
             turned, solved, edges, natural):
    factors = factors_of(chunk_factors)
    steps = with_scaled(factors, [scaled_chunks[i] for i in range(len(factors))])
    faces = [near] + expand(steps, near, far) + [far]
    near = from_chunk(faces[:-1], turned.at[0])
    far = from_chunk(faces[1:], turned.at[1])
    edges[0] = near
    edges[1] = far
    for spot in reversed(range(y_spots(natural))):
        far = scaled_cells[spot] + cell_factors[spot, 1] * near + cell_factors[spot, 2] * far
        solved[spot] = far
        natural[y_rows(natural, spot)] = far


def make_z(count):
    def z_solve(*refs):
        arrivals = refs[:count]
        (cell_factors, chunk_factors, scaled_cells, scaled_chunks, storage,
         z_factors, joints, inverse, at_row, at_depth, here, observed,
         y_factors, head_second, y_edges, head_up, adjoint_third, message,
         next_cells, next_chunks,
         scratch, edges, turned, loads, second) = refs[count:]
        me = row_block()
        for turn, arrival in enumerate(arrivals):
            scratch[me ^ turn] = arrival[...]
        nothing = jnp.zeros(arrivals[0].shape[1:], f32)
        _, steps = combine([[scratch[i, j] for j in range(5)] for i in range(count)])
        keep_steps(y_factors, [step[:3] for step in steps])
        near, far = own_edges(edges, me, nothing, expand(steps, nothing, nothing), nothing)
        y_expand(near, far, cell_factors, chunk_factors, scaled_cells, scaled_chunks,
                 turned, head_second, y_edges, second)

        slab = storage.shape[0]
        turn_tiles(storage[...] * second[...], loads)
        tiles = loads.shape[0]
        z_sweep(loads, z_factors, joints, inverse, head_up)
        found = jnp.dot(
            jnp.concatenate(
                bf16_parts(jnp.concatenate([head_up[i] for i in range(tiles)], axis=1), 2), axis=0
            ),
            at_row[...],
            preferred_element_type=f32,
        )
        found = jnp.sum(
            at_depth[...] * (found[:lanes] + found[lanes:]), axis=0, keepdims=True
        )
        misfit = here[...] * (found - observed[...])
        for i in range(misfit.shape[1] // lanes):
            row = 2 * slab + i
            message[row:row + 1, :] = misfit[:, i * lanes:(i + 1) * lanes]
        parts = [
            (at_depth[...] * part.astype(f32)).astype(jnp.bfloat16)
            for part in bf16_parts(misfit_weight * misfit, 2)
        ]
        source = lax.dot_general(
            jnp.concatenate(parts, axis=0), at_row[...],
            (((1,), (1,)), ((), ())), preferred_element_type=f32,
        )
        for i in range(tiles):
            tile = slice(i * lanes, (i + 1) * lanes)
            loads[i] = source[:lanes, tile] + source[lanes:, tile]
        z_sweep(loads, z_factors, joints, inverse, loads)
        adjoint_third[...] = jnp.stack([loads[i].T for i in range(tiles)]).reshape(second.shape)
        second[...] = storage[...] * adjoint_third[...]
        near, far = y_loads(second, cell_factors, chunk_factors, next_cells, next_chunks, turned)
        message[:slab] = near
        message[slab:2 * slab] = far

    return z_solve


def lay_head(head_up, head_third, head_send):
    cells = head_send.shape[0]
    tiles = head_up.shape[0]
    head_third[...] = jnp.stack([head_up[i].T for i in range(tiles)]).reshape(head_third.shape)
    head_send[...] = head_third[pl.ds((1 - side()) * cells, cells)]


def make_y_back(count):
    def y_back(*refs):
        arrivals = refs[:count]
        (y_factors, cell_factors, chunk_factors, scaled_cells, scaled_chunks, storage, x_steps,
         pair_steps, adjoint_second, y_edges, scaled_x, pair_scaled, note,
         scratch, edges, turned, second) = refs[count:]
        me, slab = row_block(), storage.shape[0]
        misfit = None
        for turn, arrival in enumerate(arrivals):
            scratch[me ^ turn, 0] = arrival[:slab]
            scratch[me ^ turn, 1] = arrival[slab:2 * slab]
            part = arrival[2 * slab:]
            misfit = part if misfit is None else misfit + part
        nothing = jnp.zeros(scratch.shape[2:], f32)
        factors = factors_of(y_factors)
        _, scaled = combine_loads([[scratch[i, 0], scratch[i, 1]] for i in range(count)], factors)
        faces = expand(with_scaled(factors, scaled), nothing, nothing)
        near, far = own_edges(edges, me, nothing, faces, nothing)
        y_expand(near, far, cell_factors, chunk_factors, scaled_cells, scaled_chunks,
                 turned, adjoint_second, y_edges, second)
        for i in range(slab):
            second[i] = storage[i] * second[i]
        near, far, scaled = eliminate_loads(
            factors_of(x_steps), [pair_cells(second, i) for i in range(slab // 2)]
        )
        for i, value in enumerate(scaled):
            scaled_x[i] = value
        (near, far), scaled = combine_loads(
            [[near[i], far[i]] for i in range(2)], factors_of(pair_steps)
        )
        pair_scaled[0] = scaled[0]
        rows = near.shape[0]
        note[:rows] = near
        note[rows:2 * rows] = far
        note[2 * rows:] = misfit

    return y_back


def make_terms(cuts):
    def gather_terms(cond, head_third, adjoint_third, head_second, adjoint_second,
                     head_edges, adjoint_edges, terms, natural):
        conds, near_link, far_link = y_links(cond)
        from_left = (
            -near_link * (adjoint_second[0] - adjoint_edges[0]) * (head_second[0] - head_edges[0])
        )
        spots = len(conds)
        for spot in range(spots):
            if spot < spots - 1:
                to_left, to_right = face_gradient(
                    conds[spot], conds[spot + 1],
                    adjoint_second[spot] - adjoint_second[spot + 1],
                    head_second[spot] - head_second[spot + 1],
                )
            else:
                to_left = (
                    -far_link * (adjoint_second[spot] - adjoint_edges[1])
                    * (head_second[spot] - head_edges[1])
                )
            natural[y_rows(natural, spot)] = from_left + to_left
            from_left = to_right
        slab, rows, _ = cond.shape
        per = slab // cuts
        for i in range(cuts):
            here, head, adjoint = [
                piece_of(ref, i, cuts) for ref in (cond, head_third, adjoint_third)
            ]
            last, after = z_links(here)
            to_left, to_right = face_gradient(
                here, after,
                adjoint - pltpu.roll(adjoint, lanes - 1, 1),
                head - pltpu.roll(head, lanes - 1, 1),
            )
            to_left = jnp.where(last, 0.0, to_left)
            to_right = jnp.where(last, 0.0, to_right)
            value = (to_left + pltpu.roll(to_right, 1, 1)).reshape(per, rows, lanes)
            terms[i * per:(i + 1) * per] = value + natural[i * per:(i + 1) * per]

    return gather_terms


def loads_in(arrivals, scratch, stride):
    rows, count = scratch.shape[2], len(arrivals)
    misfit = None
    for turn, arrival in enumerate(arrivals):
        position = spot_in(stride, count) ^ turn
        scratch[position, 0] = arrival[:rows]
        scratch[position, 1] = arrival[rows:2 * rows]
        part = arrival[2 * rows:]
        misfit = part if misfit is None else misfit + part
    return [[scratch[i, 0], scratch[i, 1]] for i in range(count)], misfit


def make_join_loads(stride, count, two_left):
    def join(*refs):
        arrivals, (steps_ref, message, scaled_ref, scratch) = refs[:count], refs[count:]
        blocks, misfit = loads_in(arrivals, scratch, stride)
        joined, scaled = combine_loads(blocks, factors_of(steps_ref))
        rows = scratch.shape[2]
        if two_left:
            message[:rows] = facing(*joined, stride * count)
            message[rows:] = misfit
        else:
            message[:rows] = joined[0]
            message[rows:2 * rows] = joined[1]
            message[2 * rows:] = misfit
        for i, value in enumerate(scaled):
            scaled_ref[i] = value

    return join


def make_top_loads(strides, counts):
    below = len(strides) - 1

    def top(*refs):
        arrivals, refs = refs[:counts[-1]], refs[counts[-1]:]
        top_steps, lower, lower_scaled = refs[0], refs[1:1 + below], refs[1 + below:1 + 2 * below]
        faces_ref, misfit_ref, scratch, edges = refs[1 + 2 * below:]
        nothing = jnp.zeros(scratch.shape[2:], f32)
        factors = factors_of(top_steps)
        if counts[-1] == 2:
            rows = nothing.shape[0]
            total = arrivals[0][...] + arrivals[1][...]
            scaled, misfit = [factors[0][0] * total[:rows]], total[rows:]
        else:
            blocks, misfit = loads_in(arrivals, scratch, strides[-1])
            scaled = combine_loads(blocks, factors)[1]
        levels = [(strides[-1], with_scaled(factors, scaled))]
        for i in reversed(range(below)):
            factors = factors_of(lower[i])
            scaled = [lower_scaled[i][j] for j in range(len(factors))]
            levels.append((strides[i], with_scaled(factors, scaled)))
        misfit_ref[...] = misfit
        for i, value in enumerate(descend(levels, (nothing, nothing), edges)):
            faces_ref[i] = value

    return top


def x_back(faces, head_faces, x_steps, scaled_x, cond, head, terms, own, send, gradient):
    cells = cond.shape[0] // 2
    near, far = both_edges(faces)
    head_near, head_far = both_edges(head_faces)
    near_link, far_link = x_ends(cond)
    conds = [pair_cells(cond, i) for i in range(cells)]
    heads = [pair_cells(head, i) for i in range(cells)]
    adjoint = [None] * cells
    after = far
    for i in reversed(range(cells)):
        after = scaled_x[i] + x_steps[i, 1] * near + x_steps[i, 2] * after
        adjoint[i] = after
    from_left = -near_link * (adjoint[0] - near) * (heads[0] - head_near)
    for i in range(cells):
        if i < cells - 1:
            to_left, to_right = face_gradient(
                conds[i], conds[i + 1], adjoint[i] - adjoint[i + 1], heads[i] - heads[i + 1]
            )
        else:
            to_left = -far_link * (adjoint[i] - far) * (heads[i] - head_far)
        value = from_left + to_left
        for j in range(2):
            gradient[j * cells + i] = terms[j * cells + i] + value[j]
        from_left = to_right
    own[...] = gradient[pl.ds(side() * cells, cells)]
    send[...] = gradient[pl.ds((1 - side()) * cells, cells)]


def settle(own, other, whole):
    cells, half, _ = other.shape
    start = (own.shape[0] - cells) // cells * side() * cells
    whole[:, pl.ds(pl.multiple_of(side() * half, half), half), :] = own[pl.ds(start, cells)]
    whole[:, pl.ds(pl.multiple_of((1 - side()) * half, half), half), :] = other[...]


def settle_last(own, other, misfits, whole, misfits_out):
    misfits_out[...] = misfits[...]
    settle(own, other, whole)


def shards(log_cond, storage, head, well_east, well_north, well_depth, pump_rates,
           probe_east, probe_north, probe_depth, probe_heads):
    cells, rows, _ = log_cond.shape
    devices, columns = lax.axis_size("gx"), lax.axis_size("yz")
    inner = 4 if devices >= 16 else 2
    strides, counts = [1, 2, 2 * inner], [2, inner, devices // (2 * inner)]
    two_left = counts[-1] == 2
    slab, half = 2 * cells, rows // 2
    points = probe_heads.shape[0]
    grid = (slab, half, lanes)
    plane = (half, lanes)
    spots = half // chunks
    cell = (spots, slab, chunks, lanes)
    line = (slab, lanes)
    turned = (slab * chunks, lanes)

    places = ((well_east << (2 * field)) + (well_north << field) + well_depth).reshape(1, -1)
    probes = [value.reshape(1, -1) for value in (probe_east, probe_north, probe_depth, probe_heads)]
    parts = run(
        x_load,
        [(cells,) + plane] * 6,
        [log_cond, storage, head],
        [pltpu.SemaphoreType.DMA((6,))],
        raw=3,
        limit=53,
    )
    (sources,) = run(
        make_wells(slab, half), [grid], [places, jnp.where(places >= 0, pump_rates.reshape(1, -1), 0.0)], after=[parts[3]]
    )
    cond_own, load_own = run(
        x_prepare, [(cells,) + plane] * 2, list(parts[:3]) + [sources], after=[parts[3]]
    )
    cond, storage, x_steps, pair_steps, joined = run(
        x_reduce,
        [grid, grid, (cells, 4, 2) + plane, (1, 4) + plane, (5,) + plane],
        [cond_own, parts[1], load_own] + [swap(part) for part in parts[3:]] + [sources],
        [(grid, f32)],
    )
    x_levels = [pair_steps]
    cell_factors, chunk_factors, ends = run(
        y_factor,
        [(spots, 3) + cell[1:], (chunks - 1, 3) + line, (3,) + line],
        [cond, storage],
        [((3,) + turned, f32)],
        after=[joined],
    )

    cuts = 4
    tiles = slab * half // lanes
    upright = (tiles, lanes, lanes)
    z_cell = (tiles, chunks, lanes)
    for i, (stride, count) in enumerate(zip(strides[1:], counts[1:])):
        arrivals = exchange(joined, stride, count)
        waits = []
        if i == 0:
            z_factors, joints, inverse = run(
                z_factor,
                [(lanes // chunks, 3) + z_cell, (chunks.bit_length() - 1, 2) + z_cell, z_cell],
                [cond, storage],
                [(upright, f32), (upright, f32)],
                after=[joined],
            )
            waits = [ends, inverse]
        if i < len(strides) - 2:
            joined, steps = run(
                make_join(stride, count, i == len(strides) - 3 and two_left),
                [(2 if i == len(strides) - 3 and two_left else 5,) + plane,
                 (count - 1, 4) + plane],
                arrivals,
                [((count, 5) + plane, f32)],
                after=waits,
            )
            x_levels.append(steps)
    x_faces, steps = run(
        make_top(strides, counts),
        [(3,) + plane, (counts[-1] - 1, 4) + plane],
        arrivals + x_levels,
        [((counts[-1], 5) + plane, f32), ((max(counts) + 1,) + plane, f32)],
        after=waits,
    )
    x_levels.append(steps)
    head_first, scaled_cells, scaled_chunks, message = run(
        y_forward,
        [grid, cell, (chunks - 1,) + line, (5,) + line],
        [x_faces, x_steps, storage, cell_factors, chunk_factors, ends],
        [(grid, f32), ((2,) + turned, f32)],
    )
    at_row, at_depth, here, observed = run(
        make_points(slab, half),
        [((slab * half, points), jnp.bfloat16), (lanes, points), (1, points), (1, points)],
        probes,
        after=[message],
    )
    extra, blocks = points // lanes, 2 * columns
    (y_factors, head_second, head_edges, head_up, adjoint_third, message,
     scaled_cells, scaled_chunks) = run(
        make_z(blocks),
        [(blocks - 1, 3) + line, cell, (2,) + cell[1:], upright, grid,
         (2 * slab + extra, lanes), cell, (chunks - 1,) + line],
        exchange_rows(message)
        + [cell_factors, chunk_factors, scaled_cells, scaled_chunks, storage,
           z_factors, joints, inverse, at_row, at_depth, here, observed],
        [((blocks, 5) + line, f32), ((blocks + 1,) + line, f32), ((2,) + turned, f32),
         (upright, f32), (grid, f32)],
    )
    head_third, head_send = run(
        lay_head, [grid, (cells,) + plane], [head_up], after=[message]
    )
    note = (2 * half + extra, lanes)
    adjoint_second, adjoint_edges, scaled_x, scaled, message = run(
        make_y_back(blocks),
        [cell, (2,) + cell[1:], (cells, 2) + plane, (1,) + plane, note],
        exchange_rows(message)
        + [y_factors, cell_factors, chunk_factors, scaled_cells, scaled_chunks, storage, x_steps,
           pair_steps],
        [((blocks, 2) + line, f32), ((blocks + 1,) + line, f32), ((2,) + turned, f32),
         (grid, f32)],
    )
    x_scaled = [scaled]
    (terms,) = run(
        make_terms(cuts),
        [grid],
        [cond, head_third, adjoint_third, head_second, adjoint_second, head_edges, adjoint_edges],
        [(grid, f32)],
    )
    for i in range(1, len(strides) - 1):
        arrivals = exchange(message, strides[i], counts[i])
        message, scaled = run(
            make_join_loads(strides[i], counts[i], i == len(strides) - 2 and two_left),
            [(half + extra, lanes) if i == len(strides) - 2 and two_left else note,
             (counts[i] - 1,) + plane],
            arrivals + [x_levels[i]],
            [((counts[i], 2) + plane, f32)],
        )
        x_scaled.append(scaled)
    faces, misfits = run(
        make_top_loads(strides, counts),
        [(3,) + plane, (extra, lanes)],
        exchange(message, strides[-1], counts[-1]) + x_levels[-1:] + x_levels[:-1] + x_scaled,
        [((counts[-1], 2) + plane, f32), ((max(counts) + 1,) + plane, f32)],
        after=[terms],
    )
    whole = (cells, rows, lanes)
    (head_next,) = run(settle, [whole], [head_third, swap(head_send)])
    own, send = run(
        x_back,
        [(cells,) + plane, (cells,) + plane],
        [faces, x_faces, x_steps, scaled_x, cond, head_first, terms],
        [(grid, f32)],
    )
    gradient, misfits = run(
        settle_last, [whole, (extra, lanes)], [own, swap(send), misfits]
    )
    return head_next, gradient, misfits.reshape(-1)


def solution(mesh):
    cells = P("gx", "yz", None)
    return jax.shard_map(
        shards,
        mesh=mesh,
        in_specs=(cells, cells, cells) + (P(),) * 8,
        out_specs=(cells, cells, P()),
        check_vma=False,
    )
```

```python
import jax
import jax.numpy as jnp
from jax import lax
from jax.experimental import pallas as pl
from jax.experimental.pallas import tpu as pltpu
from jax.sharding import PartitionSpec as P


f32 = jnp.float32
misfit_weight = 100.0
lanes = 128
chunks = 8
field = 10
mask = (1 << field) - 1


def harmonic(left_cond, right_cond):
    return 2.0 * left_cond * right_cond / (left_cond + right_cond)


def eliminate(entry, links, grounds, loads):
    near_ground = near_load = far_ground = far_load = None
    steps = []
    for link, ground, load in zip(links, grounds, loads):
        if far_ground is not None:
            ground, load = ground + far_ground, load + far_load
        inverse = 1.0 / (entry + link + ground)
        to_near, to_far = entry * inverse, link * inverse
        far_ground, far_load = to_far * ground, to_far * load
        if near_ground is None:
            near_ground, near_load = to_near * ground, to_near * load
        else:
            near_ground, near_load = near_ground + to_near * ground, near_load + to_near * load
        steps.append((inverse, to_near, to_far, inverse * load))
        entry = to_near * link
    return (entry, near_ground, far_ground, near_load, far_load), steps


def eliminate_loads(factors, loads):
    near_load = far_load = None
    scaled = []
    for (inverse, to_near, to_far), load in zip(factors, loads):
        if far_load is not None:
            load = load + far_load
        far_load = to_far * load
        near_load = to_near * load if near_load is None else near_load + to_near * load
        scaled.append(inverse * load)
    return near_load, far_load, scaled


def expand(steps, near, far):
    values = []
    for _, to_near, to_far, scaled in reversed(steps):
        far = scaled + to_near * near + to_far * far
        values.append(far)
    return values[::-1]


def combine(blocks):
    pairs = list(zip(blocks[:-1], blocks[1:]))
    (entry, near_ground, far_ground, near_load, far_load), steps = eliminate(
        blocks[0][0],
        [after[0] for _, after in pairs],
        [before[2] + after[1] for before, after in pairs],
        [before[4] + after[3] for before, after in pairs],
    )
    joined = (
        entry,
        blocks[0][1] + near_ground,
        blocks[-1][2] + far_ground,
        blocks[0][3] + near_load,
        blocks[-1][4] + far_load,
    )
    return joined, steps


def combine_loads(blocks, factors):
    near_load, far_load, scaled = eliminate_loads(
        factors, [before[1] + after[0] for before, after in zip(blocks[:-1], blocks[1:])]
    )
    return (blocks[0][0] + near_load, blocks[-1][1] + far_load), scaled


def with_scaled(factors, scaled):
    return [factor + (value,) for factor, value in zip(factors, scaled)]


def factors_of(ref):
    return [(ref[i, 0], ref[i, 1], ref[i, 2]) for i in range(ref.shape[0])]


def steps_of(ref):
    return [(None, ref[i, 1], ref[i, 2], ref[i, 3]) for i in range(ref.shape[0])]


def keep_steps(ref, steps):
    for i, step in enumerate(steps):
        for j, value in enumerate(step):
            ref[i, j] = value


def face_gradient(left_cond, right_cond, adjoint_drop, head_drop):
    total = 1.0 / (left_cond + right_cond)
    flow = -(adjoint_drop * head_drop) * (2.0 * left_cond * right_cond * total) * total
    return flow * right_cond, flow * left_cond


def bf16_parts(values, count):
    parts = []
    for _ in range(count):
        part = values.astype(jnp.bfloat16)
        parts.append(part)
        values = values - part.astype(jnp.float32)
    return parts


def run(body, outs, ins, scratch=(), raw=0, after=(), flops=1000000, limit=24):
    shapes = [
        jax.ShapeDtypeStruct(*((out, f32) if isinstance(out[0], int) else out)) for out in outs
    ]
    size = 4 * (sum(x.size for x in ins) + sum(x.size for x in shapes))
    places = [pltpu.HBM] * raw + [pltpu.VMEM] * (len(ins) - raw) + [pl.ANY] * len(after)
    count = len(ins)

    def ordered(*refs):
        return body(*refs[:count], *refs[count + len(after):])

    return pl.pallas_call(
        ordered,
        out_shape=shapes,
        in_specs=[pl.BlockSpec(memory_space=place) for place in places],
        out_specs=[pl.BlockSpec(memory_space=pltpu.VMEM)] * len(outs),
        scratch_shapes=[
            item if not isinstance(item, tuple) else pltpu.VMEM(*item) for item in scratch
        ],
        compiler_params=pltpu.CompilerParams(vmem_limit_bytes=int(limit * 1024 * 1024)),
        cost_estimate=pl.CostEstimate(flops=flops, bytes_accessed=size, transcendentals=0),
    )(*ins, *after)


def spot_in(stride, count):
    return lax.rem(lax.axis_index("gx") // stride, count)


def place(scratch, arrivals, stride):
    position = spot_in(stride, len(arrivals))
    for turn, arrival in enumerate(arrivals):
        scratch[position ^ turn] = arrival[...]


def exchange(value, stride, count):
    size = lax.axis_size("gx")
    return [value] + [
        lax.ppermute(value, "gx", [(i, i ^ (turn * stride)) for i in range(size)])
        for turn in range(1, count)
    ]


def swap(value):
    return exchange(value, 1, 2)[1]


def exchange_rows(value):
    size, columns = lax.axis_size("gx"), lax.axis_size("yz")
    return [value] + [
        lax.ppermute(
            value,
            ("gx", "yz"),
            [
                (i * columns + j, (i ^ (turn % 2)) * columns + (j ^ (turn // 2)))
                for i in range(size)
                for j in range(columns)
            ],
        )
        for turn in range(1, 2 * columns)
    ]


def side():
    return lax.rem(lax.axis_index("gx"), 2)


def row_block():
    return lax.axis_index("yz") * 2 + side()


def local_spot(east, north, slab, rows):
    local_east = east - lax.axis_index("gx") // 2 * slab
    local_north = north - row_block() * rows
    inside = (
        (local_east >= 0) & (local_east < slab) & (local_north >= 0) & (local_north < rows)
    )
    return inside, jnp.where(inside, local_east * rows + local_north, -1)


def own_edges(scratch, position, near, faces, far):
    for i, value in enumerate([near] + faces + [far]):
        scratch[i] = value
    return scratch[position], scratch[position + 1]


def pair_cells(ref, i):
    cells = ref.shape[0] // 2
    return jnp.stack([ref[i], ref[cells + i]])


def x_ends(cond):
    pair, count = lax.axis_index("gx") // 2, lax.axis_size("gx") // 2
    cells = cond.shape[0]
    near = [jnp.where(pair == 0, 0.0, 2.0) * cond[0], 2.0 * cond[cells // 2]]
    far = [2.0 * cond[cells // 2 - 1], jnp.where(pair == count - 1, 0.0, 2.0) * cond[cells - 1]]
    return jnp.stack(near), jnp.stack(far)


def x_load(log_cond, storage, head, *refs):
    targets, done = refs[:6], refs[6]
    half = targets[0].shape[1]
    moves = []
    for part, some in ((1 - side(), targets[3:]), (side(), targets[:3])):
        rows = pl.ds(pl.multiple_of(part * half, half), half)
        for source, target in zip((log_cond, storage, head), some):
            moves.append(
                pltpu.make_async_copy(source.at[:, rows, :], target, done.at[len(moves)])
            )
    for move in moves:
        move.start()
    for move in moves:
        move.wait()


def make_wells(slab, rows):
    def wells(places, rates, sources):
        _, spot = local_spot(
            lax.shift_right_logical(places[...], 2 * field),
            lax.shift_right_logical(places[...], field) & mask,
            slab,
            rows,
        )
        count = rates.shape[1]
        at_row = jnp.where(
            lax.broadcasted_iota(jnp.int32, (slab * rows, count), 0) == spot, 1.0, 0.0
        ).astype(jnp.bfloat16)
        at_depth = (
            lax.broadcasted_iota(jnp.int32, (lanes, count), 0) == (places[...] & mask)
        )
        sources[...] = sum(
            lax.dot_general(
                at_row, part, (((1,), (1,)), ((), ())), preferred_element_type=f32
            )
            for part in bf16_parts(jnp.where(at_depth, rates[...], 0.0), 3)
        ).reshape(slab, rows, lanes)

    return wells


def x_prepare(log_cond, storage, head, sources, cond_own, load_own):
    cells = log_cond.shape[0]
    cond_own[...] = jnp.exp(log_cond[...])
    load_own[...] = storage[...] * head[...] + sources[pl.ds(side() * cells, cells)]


def x_reduce(cond_own, storage_own, load_own, log_cond_other, storage_other, head_other, sources,
             cond, storage, steps_ref, pair_steps, block_ref, loads):
    cells = cond_own.shape[0]
    mine, rest = pl.ds(side() * cells, cells), pl.ds((1 - side()) * cells, cells)
    cond[mine] = cond_own[...]
    storage[mine] = storage_own[...]
    loads[mine] = load_own[...]
    cond[rest] = jnp.exp(log_cond_other[...])
    storage[rest] = storage_other[...]
    loads[rest] = storage_other[...] * head_other[...] + sources[rest]
    near, far = x_ends(cond)
    conds = [pair_cells(cond, i) for i in range(cells)]
    links = [harmonic(conds[i], conds[i + 1]) for i in range(cells - 1)] + [far]
    block, steps = eliminate(
        near,
        links,
        [pair_cells(storage, i) for i in range(cells)],
        [pair_cells(loads, i) for i in range(cells)],
    )
    keep_steps(steps_ref, steps)
    joined, steps = combine([[value[i] for value in block] for i in range(2)])
    keep_steps(pair_steps, steps)
    for i, value in enumerate(joined):
        block_ref[i] = value


def facing(near, far, stride):
    return jnp.where(spot_in(stride, 2) == 0, far, near)


def make_join(stride, count, two_left):
    def join(*refs):
        arrivals, (joined_ref, steps_ref, scratch) = refs[:count], refs[count:]
        place(scratch, arrivals, stride)
        joined, steps = combine([[scratch[i, j] for j in range(5)] for i in range(count)])
        if two_left:
            _, near_ground, far_ground, near_load, far_load = joined
            joined = [
                facing(near_ground, far_ground, stride * count),
                facing(near_load, far_load, stride * count),
            ]
        for i, value in enumerate(joined):
            joined_ref[i] = value
        keep_steps(steps_ref, steps)

    return join


def descend(levels, edges, scratch):
    for stride, steps in levels[:-1]:
        faces = expand(steps, *edges)
        edges = own_edges(scratch, spot_in(stride, len(steps) + 1), edges[0], faces, edges[1])
    return edges[0], expand(levels[-1][1], *edges)[0], edges[1]


def make_top(strides, counts):
    below = len(strides) - 1

    def top(*refs):
        arrivals = refs[:counts[-1]]
        lower, (faces_ref, steps_ref, scratch, edges) = (
            refs[counts[-1]:counts[-1] + below], refs[counts[-1] + below:]
        )
        nothing = jnp.zeros(faces_ref.shape[1:], f32)
        if counts[-1] == 2:
            ground, load = [arrivals[0][i] + arrivals[1][i] for i in range(2)]
            inverse = 1.0 / ground
            steps = [(inverse, nothing, nothing, inverse * load)]
        else:
            place(scratch, arrivals, strides[-1])
            _, steps = combine([[scratch[i, j] for j in range(5)] for i in range(counts[-1])])
        keep_steps(steps_ref, steps)
        levels = [(strides[-1], steps)] + [
            (strides[i], steps_of(lower[i])) for i in reversed(range(below))
        ]
        for i, value in enumerate(descend(levels, (nothing, nothing), edges)):
            faces_ref[i] = value

    return top


def both_edges(faces):
    return jnp.stack([faces[0], faces[1]]), jnp.stack([faces[1], faces[2]])


def y_spots(ref):
    return ref.shape[1] // chunks


def y_rows(ref, spot):
    return (slice(None), pl.ds(spot, chunks, stride=y_spots(ref)), slice(None))


def y_cells(ref):
    return [ref[y_rows(ref, spot)] for spot in range(y_spots(ref))]


def y_links(cond):
    me, count = row_block(), 2 * lax.axis_size("yz")
    cells = y_cells(cond)
    place_of = lax.broadcasted_iota(jnp.int32, cells[0].shape, 1)
    near = jnp.where((place_of == 0) & (me == 0), 0.0, 2.0 * cells[0])
    far = jnp.where((place_of == chunks - 1) & (me == count - 1), 0.0, 2.0 * cells[-1])
    return cells, near, far


def by_chunk(value, scratch):
    slab = value.shape[0]
    scratch[...] = value.reshape(slab * chunks, lanes)
    return [scratch[pl.ds(i, slab, stride=chunks), :] for i in range(chunks)]


def from_chunk(values, scratch):
    slab = values[0].shape[0]
    for i, value in enumerate(values):
        scratch[pl.ds(i, slab, stride=chunks), :] = value
    return scratch[...].reshape(slab, chunks, lanes)


def y_factor(cond, storage, cell_factors, chunk_factors, ends, turned):
    conds, near, far = y_links(cond)
    links = [harmonic(before, after) for before, after in zip(conds[:-1], conds[1:])] + [far]
    nothing = [jnp.zeros_like(near)] * len(conds)
    block, steps = eliminate(near, links, y_cells(storage), nothing)
    keep_steps(cell_factors, [step[:3] for step in steps])
    parts = [by_chunk(value, turned.at[i]) for i, value in enumerate(block[:3])]
    nothing = [jnp.zeros_like(parts[0][0])] * len(parts[0])
    joined, steps = combine(list(zip(*parts, nothing, nothing)))
    keep_steps(chunk_factors, [step[:3] for step in steps])
    for i in range(3):
        ends[i] = joined[i]


def z_links(cond):
    lane = lax.broadcasted_iota(jnp.int32, cond.shape, 1)
    after = pltpu.roll(cond, lanes - 1, 1)
    return lane == lanes - 1, after


def piece_of(ref, i, cuts):
    per = ref.shape[0] // cuts
    return ref[i * per:(i + 1) * per].reshape(per * ref.shape[1], lanes)


def turn_tiles(values, target):
    values = values.reshape(target.shape)
    for i in range(target.shape[0]):
        target[i] = values[i].T


def z_factor(cond, storage, cell_factors, joints, inverse_ref, cond_up, storage_up):
    turn_tiles(cond[...], cond_up)
    turn_tiles(storage[...], storage_up)
    conds = y_cells(cond_up)
    place_of = lax.broadcasted_iota(jnp.int32, conds[0].shape, 1)
    near = jnp.where(place_of == 0, 0.0, 2.0 * conds[0])
    far = jnp.where(place_of == chunks - 1, 0.0, 2.0 * conds[-1])
    links = [harmonic(before, after) for before, after in zip(conds[:-1], conds[1:])] + [far]
    nothing = [jnp.zeros_like(near)] * len(conds)
    block, steps = eliminate(near, links, y_cells(storage_up), nothing)
    keep_steps(cell_factors, [step[:3] for step in steps])
    link = pltpu.roll(block[0], chunks - 1, 1)
    ground = block[2] + pltpu.roll(block[1], chunks - 1, 1)
    ground = jnp.where(place_of == chunks - 1, 1.0, ground)
    for level in range(chunks.bit_length() - 1):
        shift = 1 << level
        link_back = pltpu.roll(link, shift, 1)
        inverse = 1.0 / (link + link_back + ground)
        passed, held = inverse * link, inverse * ground
        joints[level, 0] = pltpu.roll(passed, shift, 1)
        joints[level, 1] = link * pltpu.roll(inverse, chunks - shift, 1)
        ground = (
            ground
            + link * pltpu.roll(held, chunks - shift, 1)
            + link_back * pltpu.roll(held, shift, 1)
        )
        link = link * pltpu.roll(passed, chunks - shift, 1)
    inverse_ref[...] = 1.0 / ground


def z_sweep(loads, cell_factors, joints, inverse, solved):
    factors = factors_of(cell_factors)
    near, far, scaled = eliminate_loads(factors, y_cells(loads))
    load = far + pltpu.roll(near, chunks - 1, 1)
    for level in range(joints.shape[0]):
        shift = 1 << level
        load = (
            load
            + joints[level, 1] * pltpu.roll(load, chunks - shift, 1)
            + joints[level, 0] * pltpu.roll(load, shift, 1)
        )
    far = load * inverse[...]
    near = pltpu.roll(far, 1, 1)
    for spot, value in enumerate(expand(with_scaled(factors, scaled), near, far)):
        solved[y_rows(solved, spot)] = value


def make_points(slab, rows):
    def points(east, north, depth, heads, at_row, at_depth, at_depth_short, here, observed):
        inside, spot = local_spot(east[...], north[...], slab, rows)
        at_row[...] = jnp.where(
            lax.broadcasted_iota(jnp.int32, at_row.shape, 0) == spot, 1.0, 0.0
        ).astype(jnp.bfloat16)
        at_depth[...] = jnp.where(
            lax.broadcasted_iota(jnp.int32, at_depth.shape, 0) == depth[...], 1.0, 0.0
        )
        at_depth_short[...] = at_depth[...].astype(jnp.bfloat16)
        here[...] = jnp.where(inside, 1.0, 0.0)
        observed[...] = heads[...]

    return points


def y_forward(x_faces, x_steps, storage, cell_factors, chunk_factors, ends,
              head_first, scaled_cells, scaled_chunks, message, loads, turned):
    cells = head_first.shape[0] // 2
    near, far = both_edges(x_faces)
    for i in reversed(range(cells)):
        far = x_steps[i, 3] + x_steps[i, 1] * near + x_steps[i, 2] * far
        for j in range(2):
            head_first[j * cells + i] = far[j]
            loads[j * cells + i] = storage[j * cells + i] * far[j]
    for i in range(3):
        message[i] = ends[i]
    near, far = y_loads(loads, cell_factors, chunk_factors, scaled_cells, scaled_chunks, turned)
    message[3] = near
    message[4] = far


def y_loads(loads, cell_factors, chunk_factors, scaled_cells, scaled_chunks, turned):
    near, far, scaled = eliminate_loads(
        factors_of(cell_factors), y_cells(loads)
    )
    for i, value in enumerate(scaled):
        scaled_cells[i] = value
    blocks = list(zip(by_chunk(near, turned.at[0]), by_chunk(far, turned.at[1])))
    joined, scaled = combine_loads(blocks, factors_of(chunk_factors))
    for i, value in enumerate(scaled):
        scaled_chunks[i] = value
    return joined


def y_expand(near, far, cell_factors, chunk_factors, scaled_cells, scaled_chunks,
             turned, solved, edges, natural):
    factors = factors_of(chunk_factors)
    steps = with_scaled(factors, [scaled_chunks[i] for i in range(len(factors))])
    faces = [near] + expand(steps, near, far) + [far]
    near = from_chunk(faces[:-1], turned.at[0])
    far = from_chunk(faces[1:], turned.at[1])
    edges[0] = near
    edges[1] = far
    for spot in reversed(range(y_spots(natural))):
        far = scaled_cells[spot] + cell_factors[spot, 1] * near + cell_factors[spot, 2] * far
        solved[spot] = far
        natural[y_rows(natural, spot)] = far


def make_z(count):
    def z_solve(*refs):
        arrivals = refs[:count]
        (cell_factors, chunk_factors, scaled_cells, scaled_chunks, storage,
         z_factors, joints, inverse, at_row, at_depth, at_depth_short, here, observed,
         y_factors, head_second, y_edges, head_up, adjoint_third, message,
         next_cells, next_chunks,
         scratch, edges, turned, loads, second) = refs[count:]
        me = row_block()
        for turn, arrival in enumerate(arrivals):
            scratch[me ^ turn] = arrival[...]
        nothing = jnp.zeros(arrivals[0].shape[1:], f32)
        _, steps = combine([[scratch[i, j] for j in range(5)] for i in range(count)])
        keep_steps(y_factors, [step[:3] for step in steps])
        near, far = own_edges(edges, me, nothing, expand(steps, nothing, nothing), nothing)
        y_expand(near, far, cell_factors, chunk_factors, scaled_cells, scaled_chunks,
                 turned, head_second, y_edges, second)

        slab = storage.shape[0]
        turn_tiles(storage[...] * second[...], loads)
        tiles = loads.shape[0]
        z_sweep(loads, z_factors, joints, inverse, head_up)
        found = jnp.dot(
            jnp.concatenate(
                bf16_parts(jnp.concatenate([head_up[i] for i in range(tiles)], axis=1), 2), axis=0
            ),
            at_row[...],
            preferred_element_type=f32,
        )
        found = jnp.sum(
            at_depth[...] * (found[:lanes] + found[lanes:]), axis=0, keepdims=True
        )
        misfit = here[...] * (found - observed[...])
        for i in range(misfit.shape[1] // lanes):
            row = 2 * slab + i
            message[row:row + 1, :] = misfit[:, i * lanes:(i + 1) * lanes]
        parts = [
            at_depth_short[...] * part
            for part in bf16_parts(misfit_weight * misfit, 2)
        ]
        source = lax.dot_general(
            jnp.concatenate(parts, axis=0), at_row[...],
            (((1,), (1,)), ((), ())), preferred_element_type=f32,
        )
        for i in range(tiles):
            tile = slice(i * lanes, (i + 1) * lanes)
            loads[i] = source[:lanes, tile] + source[lanes:, tile]
        z_sweep(loads, z_factors, joints, inverse, loads)
        adjoint_third[...] = jnp.stack([loads[i].T for i in range(tiles)]).reshape(second.shape)
        second[...] = storage[...] * adjoint_third[...]
        near, far = y_loads(second, cell_factors, chunk_factors, next_cells, next_chunks, turned)
        message[:slab] = near
        message[slab:2 * slab] = far

    return z_solve


def lay_head(head_up, head_third, head_send):
    cells = head_send.shape[0]
    tiles = head_up.shape[0]
    head_third[...] = jnp.stack([head_up[i].T for i in range(tiles)]).reshape(head_third.shape)
    head_send[...] = head_third[pl.ds((1 - side()) * cells, cells)]


def make_y_back(count):
    def y_back(*refs):
        arrivals = refs[:count]
        (y_factors, cell_factors, chunk_factors, scaled_cells, scaled_chunks, storage, x_steps,
         pair_steps, adjoint_second, y_edges, scaled_x, pair_scaled, note,
         scratch, edges, turned, second) = refs[count:]
        me, slab = row_block(), storage.shape[0]
        misfit = None
        for turn, arrival in enumerate(arrivals):
            scratch[me ^ turn, 0] = arrival[:slab]
            scratch[me ^ turn, 1] = arrival[slab:2 * slab]
            part = arrival[2 * slab:]
            misfit = part if misfit is None else misfit + part
        nothing = jnp.zeros(scratch.shape[2:], f32)
        factors = factors_of(y_factors)
        _, scaled = combine_loads([[scratch[i, 0], scratch[i, 1]] for i in range(count)], factors)
        faces = expand(with_scaled(factors, scaled), nothing, nothing)
        near, far = own_edges(edges, me, nothing, faces, nothing)
        y_expand(near, far, cell_factors, chunk_factors, scaled_cells, scaled_chunks,
                 turned, adjoint_second, y_edges, second)
        for i in range(slab):
            second[i] = storage[i] * second[i]
        near, far, scaled = eliminate_loads(
            factors_of(x_steps), [pair_cells(second, i) for i in range(slab // 2)]
        )
        for i, value in enumerate(scaled):
            scaled_x[i] = value
        (near, far), scaled = combine_loads(
            [[near[i], far[i]] for i in range(2)], factors_of(pair_steps)
        )
        pair_scaled[0] = scaled[0]
        rows = near.shape[0]
        note[:rows] = near
        note[rows:2 * rows] = far
        note[2 * rows:] = misfit

    return y_back


def make_terms(cuts):
    def gather_terms(cond, head_third, adjoint_third, head_second, adjoint_second,
                     head_edges, adjoint_edges, terms, natural):
        conds, near_link, far_link = y_links(cond)
        from_left = (
            -near_link * (adjoint_second[0] - adjoint_edges[0]) * (head_second[0] - head_edges[0])
        )
        spots = len(conds)
        for spot in range(spots):
            if spot < spots - 1:
                to_left, to_right = face_gradient(
                    conds[spot], conds[spot + 1],
                    adjoint_second[spot] - adjoint_second[spot + 1],
                    head_second[spot] - head_second[spot + 1],
                )
            else:
                to_left = (
                    -far_link * (adjoint_second[spot] - adjoint_edges[1])
                    * (head_second[spot] - head_edges[1])
                )
            natural[y_rows(natural, spot)] = from_left + to_left
            from_left = to_right
        slab, rows, _ = cond.shape
        per = slab // cuts
        for i in range(cuts):
            here, head, adjoint = [
                piece_of(ref, i, cuts) for ref in (cond, head_third, adjoint_third)
            ]
            last, after = z_links(here)
            to_left, to_right = face_gradient(
                here, after,
                adjoint - pltpu.roll(adjoint, lanes - 1, 1),
                head - pltpu.roll(head, lanes - 1, 1),
            )
            to_left = jnp.where(last, 0.0, to_left)
            to_right = jnp.where(last, 0.0, to_right)
            value = (to_left + pltpu.roll(to_right, 1, 1)).reshape(per, rows, lanes)
            terms[i * per:(i + 1) * per] = value + natural[i * per:(i + 1) * per]

    return gather_terms


def loads_in(arrivals, scratch, stride):
    rows, count = scratch.shape[2], len(arrivals)
    misfit = None
    for turn, arrival in enumerate(arrivals):
        position = spot_in(stride, count) ^ turn
        scratch[position, 0] = arrival[:rows]
        scratch[position, 1] = arrival[rows:2 * rows]
        part = arrival[2 * rows:]
        misfit = part if misfit is None else misfit + part
    return [[scratch[i, 0], scratch[i, 1]] for i in range(count)], misfit


def make_join_loads(stride, count, two_left):
    def join(*refs):
        arrivals, (steps_ref, message, scaled_ref, scratch) = refs[:count], refs[count:]
        blocks, misfit = loads_in(arrivals, scratch, stride)
        joined, scaled = combine_loads(blocks, factors_of(steps_ref))
        rows = scratch.shape[2]
        if two_left:
            message[:rows] = facing(*joined, stride * count)
            message[rows:] = misfit
        else:
            message[:rows] = joined[0]
            message[rows:2 * rows] = joined[1]
            message[2 * rows:] = misfit
        for i, value in enumerate(scaled):
            scaled_ref[i] = value

    return join


def make_top_loads(strides, counts):
    below = len(strides) - 1

    def top(*refs):
        arrivals, refs = refs[:counts[-1]], refs[counts[-1]:]
        top_steps, lower, lower_scaled = refs[0], refs[1:1 + below], refs[1 + below:1 + 2 * below]
        faces_ref, misfit_ref, scratch, edges = refs[1 + 2 * below:]
        nothing = jnp.zeros(scratch.shape[2:], f32)
        factors = factors_of(top_steps)
        if counts[-1] == 2:
            rows = nothing.shape[0]
            total = arrivals[0][...] + arrivals[1][...]
            scaled, misfit = [factors[0][0] * total[:rows]], total[rows:]
        else:
            blocks, misfit = loads_in(arrivals, scratch, strides[-1])
            scaled = combine_loads(blocks, factors)[1]
        levels = [(strides[-1], with_scaled(factors, scaled))]
        for i in reversed(range(below)):
            factors = factors_of(lower[i])
            scaled = [lower_scaled[i][j] for j in range(len(factors))]
            levels.append((strides[i], with_scaled(factors, scaled)))
        misfit_ref[...] = misfit
        for i, value in enumerate(descend(levels, (nothing, nothing), edges)):
            faces_ref[i] = value

    return top


def x_back(faces, head_faces, x_steps, scaled_x, cond, head, terms, own, send, gradient):
    cells = cond.shape[0] // 2
    near, far = both_edges(faces)
    head_near, head_far = both_edges(head_faces)
    near_link, far_link = x_ends(cond)
    conds = [pair_cells(cond, i) for i in range(cells)]
    heads = [pair_cells(head, i) for i in range(cells)]
    adjoint = [None] * cells
    after = far
    for i in reversed(range(cells)):
        after = scaled_x[i] + x_steps[i, 1] * near + x_steps[i, 2] * after
        adjoint[i] = after
    from_left = -near_link * (adjoint[0] - near) * (heads[0] - head_near)
    for i in range(cells):
        if i < cells - 1:
            to_left, to_right = face_gradient(
                conds[i], conds[i + 1], adjoint[i] - adjoint[i + 1], heads[i] - heads[i + 1]
            )
        else:
            to_left = -far_link * (adjoint[i] - far) * (heads[i] - head_far)
        value = from_left + to_left
        for j in range(2):
            gradient[j * cells + i] = terms[j * cells + i] + value[j]
        from_left = to_right
    own[...] = gradient[pl.ds(side() * cells, cells)]
    send[...] = gradient[pl.ds((1 - side()) * cells, cells)]


def settle(own, other, whole):
    cells, half, _ = other.shape
    start = (own.shape[0] - cells) // cells * side() * cells
    whole[:, pl.ds(pl.multiple_of(side() * half, half), half), :] = own[pl.ds(start, cells)]
    whole[:, pl.ds(pl.multiple_of((1 - side()) * half, half), half), :] = other[...]


def settle_last(own, other, misfits, whole, misfits_out):
    misfits_out[...] = misfits[...]
    settle(own, other, whole)


def shards(log_cond, storage, head, well_east, well_north, well_depth, pump_rates,
           probe_east, probe_north, probe_depth, probe_heads):
    cells, rows, _ = log_cond.shape
    devices, columns = lax.axis_size("gx"), lax.axis_size("yz")
    inner = 4 if devices >= 16 else 2
    strides, counts = [1, 2, 2 * inner], [2, inner, devices // (2 * inner)]
    two_left = counts[-1] == 2
    slab, half = 2 * cells, rows // 2
    points = probe_heads.shape[0]
    grid = (slab, half, lanes)
    plane = (half, lanes)
    spots = half // chunks
    cell = (spots, slab, chunks, lanes)
    line = (slab, lanes)
    turned = (slab * chunks, lanes)

    places = ((well_east << (2 * field)) + (well_north << field) + well_depth).reshape(1, -1)
    probes = [value.reshape(1, -1) for value in (probe_east, probe_north, probe_depth, probe_heads)]
    parts = run(
        x_load,
        [(cells,) + plane] * 6,
        [log_cond, storage, head],
        [pltpu.SemaphoreType.DMA((6,))],
        raw=3,
        limit=53,
    )
    (sources,) = run(
        make_wells(slab, half), [grid], [places, jnp.where(places >= 0, pump_rates.reshape(1, -1), 0.0)], after=[parts[3]]
    )
    cond_own, load_own = run(
        x_prepare, [(cells,) + plane] * 2, list(parts[:3]) + [sources], after=[parts[3]]
    )
    cond, storage, x_steps, pair_steps, joined = run(
        x_reduce,
        [grid, grid, (cells, 4, 2) + plane, (1, 4) + plane, (5,) + plane],
        [cond_own, parts[1], load_own] + [swap(part) for part in parts[3:]] + [sources],
        [(grid, f32)],
    )
    x_levels = [pair_steps]
    cell_factors, chunk_factors, ends = run(
        y_factor,
        [(spots, 3) + cell[1:], (chunks - 1, 3) + line, (3,) + line],
        [cond, storage],
        [((3,) + turned, f32)],
        after=[joined],
    )

    cuts = 4
    tiles = slab * half // lanes
    upright = (tiles, lanes, lanes)
    z_cell = (tiles, chunks, lanes)
    for i, (stride, count) in enumerate(zip(strides[1:], counts[1:])):
        arrivals = exchange(joined, stride, count)
        waits = []
        if i == 0:
            z_factors, joints, inverse = run(
                z_factor,
                [(lanes // chunks, 3) + z_cell, (chunks.bit_length() - 1, 2) + z_cell, z_cell],
                [cond, storage],
                [(upright, f32), (upright, f32)],
                after=[joined],
            )
            waits = [ends, inverse]
        if i < len(strides) - 2:
            joined, steps = run(
                make_join(stride, count, i == len(strides) - 3 and two_left),
                [(2 if i == len(strides) - 3 and two_left else 5,) + plane,
                 (count - 1, 4) + plane],
                arrivals,
                [((count, 5) + plane, f32)],
                after=waits,
            )
            x_levels.append(steps)
    x_faces, steps = run(
        make_top(strides, counts),
        [(3,) + plane, (counts[-1] - 1, 4) + plane],
        arrivals + x_levels,
        [((counts[-1], 5) + plane, f32), ((max(counts) + 1,) + plane, f32)],
        after=waits,
    )
    x_levels.append(steps)
    head_first, scaled_cells, scaled_chunks, message = run(
        y_forward,
        [grid, cell, (chunks - 1,) + line, (5,) + line],
        [x_faces, x_steps, storage, cell_factors, chunk_factors, ends],
        [(grid, f32), ((2,) + turned, f32)],
    )
    at_row, at_depth, at_depth_short, here, observed = run(
        make_points(slab, half),
        [((slab * half, points), jnp.bfloat16), (lanes, points), ((lanes, points), jnp.bfloat16),
         (1, points), (1, points)],
        probes,
        after=[message],
    )
    extra, blocks = points // lanes, 2 * columns
    (y_factors, head_second, head_edges, head_up, adjoint_third, message,
     scaled_cells, scaled_chunks) = run(
        make_z(blocks),
        [(blocks - 1, 3) + line, cell, (2,) + cell[1:], upright, grid,
         (2 * slab + extra, lanes), cell, (chunks - 1,) + line],
        exchange_rows(message)
        + [cell_factors, chunk_factors, scaled_cells, scaled_chunks, storage,
           z_factors, joints, inverse, at_row, at_depth, at_depth_short, here, observed],
        [((blocks, 5) + line, f32), ((blocks + 1,) + line, f32), ((2,) + turned, f32),
         (upright, f32), (grid, f32)],
    )
    head_third, head_send = run(
        lay_head, [grid, (cells,) + plane], [head_up], after=[message]
    )
    note = (2 * half + extra, lanes)
    adjoint_second, adjoint_edges, scaled_x, scaled, message = run(
        make_y_back(blocks),
        [cell, (2,) + cell[1:], (cells, 2) + plane, (1,) + plane, note],
        exchange_rows(message)
        + [y_factors, cell_factors, chunk_factors, scaled_cells, scaled_chunks, storage, x_steps,
           pair_steps],
        [((blocks, 2) + line, f32), ((blocks + 1,) + line, f32), ((2,) + turned, f32),
         (grid, f32)],
    )
    x_scaled = [scaled]
    (terms,) = run(
        make_terms(cuts),
        [grid],
        [cond, head_third, adjoint_third, head_second, adjoint_second, head_edges, adjoint_edges],
        [(grid, f32)],
    )
    for i in range(1, len(strides) - 1):
        arrivals = exchange(message, strides[i], counts[i])
        message, scaled = run(
            make_join_loads(strides[i], counts[i], i == len(strides) - 2 and two_left),
            [(half + extra, lanes) if i == len(strides) - 2 and two_left else note,
             (counts[i] - 1,) + plane],
            arrivals + [x_levels[i]],
            [((counts[i], 2) + plane, f32)],
        )
        x_scaled.append(scaled)
    faces, misfits = run(
        make_top_loads(strides, counts),
        [(3,) + plane, (extra, lanes)],
        exchange(message, strides[-1], counts[-1]) + x_levels[-1:] + x_levels[:-1] + x_scaled,
        [((counts[-1], 2) + plane, f32), ((max(counts) + 1,) + plane, f32)],
        after=[terms],
    )
    whole = (cells, rows, lanes)
    (head_next,) = run(settle, [whole], [head_third, swap(head_send)])
    own, send = run(
        x_back,
        [(cells,) + plane, (cells,) + plane],
        [faces, x_faces, x_steps, scaled_x, cond, head_first, terms],
        [(grid, f32)],
    )
    gradient, misfits = run(
        settle_last, [whole, (extra, lanes)], [own, swap(send), misfits]
    )
    return head_next, gradient, misfits.reshape(-1)


def solution(mesh):
    cells = P("gx", "yz", None)
    return jax.shard_map(
        shards,
        mesh=mesh,
        in_specs=(cells, cells, cells) + (P(),) * 8,
        out_specs=(cells, cells, P()),
        check_vma=False,
    )
```

```python
import jax
import jax.numpy as jnp
from jax import lax
from jax.experimental import pallas as pl
from jax.experimental.pallas import tpu as pltpu
from jax.sharding import PartitionSpec as P


f32 = jnp.float32
misfit_weight = 100.0
lanes = 128
chunks = 8
field = 10
mask = (1 << field) - 1


def harmonic(left_cond, right_cond):
    return 2.0 * left_cond * right_cond / (left_cond + right_cond)


def eliminate(entry, links, grounds, loads):
    near_ground = near_load = far_ground = far_load = None
    steps = []
    for link, ground, load in zip(links, grounds, loads):
        if far_ground is not None:
            ground, load = ground + far_ground, load + far_load
        inverse = 1.0 / (entry + link + ground)
        to_near, to_far = entry * inverse, link * inverse
        far_ground, far_load = to_far * ground, to_far * load
        if near_ground is None:
            near_ground, near_load = to_near * ground, to_near * load
        else:
            near_ground, near_load = near_ground + to_near * ground, near_load + to_near * load
        steps.append((inverse, to_near, to_far, inverse * load))
        entry = to_near * link
    return (entry, near_ground, far_ground, near_load, far_load), steps


def eliminate_loads(factors, loads):
    near_load = far_load = None
    scaled = []
    for (inverse, to_near, to_far), load in zip(factors, loads):
        if far_load is not None:
            load = load + far_load
        far_load = to_far * load
        near_load = to_near * load if near_load is None else near_load + to_near * load
        scaled.append(inverse * load)
    return near_load, far_load, scaled


def expand(steps, near, far):
    values = []
    for _, to_near, to_far, scaled in reversed(steps):
        far = scaled + to_near * near + to_far * far
        values.append(far)
    return values[::-1]


def combine(blocks):
    pairs = list(zip(blocks[:-1], blocks[1:]))
    (entry, near_ground, far_ground, near_load, far_load), steps = eliminate(
        blocks[0][0],
        [after[0] for _, after in pairs],
        [before[2] + after[1] for before, after in pairs],
        [before[4] + after[3] for before, after in pairs],
    )
    joined = (
        entry,
        blocks[0][1] + near_ground,
        blocks[-1][2] + far_ground,
        blocks[0][3] + near_load,
        blocks[-1][4] + far_load,
    )
    return joined, steps


def combine_loads(blocks, factors):
    near_load, far_load, scaled = eliminate_loads(
        factors, [before[1] + after[0] for before, after in zip(blocks[:-1], blocks[1:])]
    )
    return (blocks[0][0] + near_load, blocks[-1][1] + far_load), scaled


def with_scaled(factors, scaled):
    return [factor + (value,) for factor, value in zip(factors, scaled)]


def factors_of(ref):
    return [(ref[i, 0], ref[i, 1], ref[i, 2]) for i in range(ref.shape[0])]


def steps_of(ref):
    return [(None, ref[i, 1], ref[i, 2], ref[i, 3]) for i in range(ref.shape[0])]


def keep_steps(ref, steps):
    for i, step in enumerate(steps):
        for j, value in enumerate(step):
            ref[i, j] = value


def face_gradient(left_cond, right_cond, adjoint_drop, head_drop):
    total = 1.0 / (left_cond + right_cond)
    flow = -(adjoint_drop * head_drop) * (2.0 * left_cond * right_cond * total) * total
    return flow * right_cond, flow * left_cond


def bf16_parts(values, count):
    parts = []
    for _ in range(count):
        part = values.astype(jnp.bfloat16)
        parts.append(part)
        values = values - part.astype(jnp.float32)
    return parts


def run(body, outs, ins, scratch=(), raw=0, after=(), flops=1000000, limit=24):
    shapes = [
        jax.ShapeDtypeStruct(*((out, f32) if isinstance(out[0], int) else out)) for out in outs
    ]
    size = 4 * (sum(x.size for x in ins) + sum(x.size for x in shapes))
    places = [pltpu.HBM] * raw + [pltpu.VMEM] * (len(ins) - raw) + [pl.ANY] * len(after)
    count = len(ins)

    def ordered(*refs):
        return body(*refs[:count], *refs[count + len(after):])

    return pl.pallas_call(
        ordered,
        out_shape=shapes,
        in_specs=[pl.BlockSpec(memory_space=place) for place in places],
        out_specs=[pl.BlockSpec(memory_space=pltpu.VMEM)] * len(outs),
        scratch_shapes=[
            item if not isinstance(item, tuple) else pltpu.VMEM(*item) for item in scratch
        ],
        compiler_params=pltpu.CompilerParams(vmem_limit_bytes=int(limit * 1024 * 1024)),
        cost_estimate=pl.CostEstimate(flops=flops, bytes_accessed=size, transcendentals=0),
    )(*ins, *after)


def spot_in(stride, count):
    return lax.rem(lax.axis_index("gx") // stride, count)


def place(scratch, arrivals, stride):
    position = spot_in(stride, len(arrivals))
    for turn, arrival in enumerate(arrivals):
        scratch[position ^ turn] = arrival[...]


def exchange(value, stride, count):
    size = lax.axis_size("gx")
    return [value] + [
        lax.ppermute(value, "gx", [(i, i ^ (turn * stride)) for i in range(size)])
        for turn in range(1, count)
    ]


def swap(value):
    return exchange(value, 1, 2)[1]


def exchange_rows(value):
    size, columns = lax.axis_size("gx"), lax.axis_size("yz")
    return [value] + [
        lax.ppermute(
            value,
            ("gx", "yz"),
            [
                (i * columns + j, (i ^ (turn % 2)) * columns + (j ^ (turn // 2)))
                for i in range(size)
                for j in range(columns)
            ],
        )
        for turn in range(1, 2 * columns)
    ]


def side():
    return lax.rem(lax.axis_index("gx"), 2)


def row_block():
    return lax.axis_index("yz") * 2 + side()


def local_spot(east, north, slab, rows):
    local_east = east - lax.axis_index("gx") // 2 * slab
    local_north = north - row_block() * rows
    inside = (
        (local_east >= 0) & (local_east < slab) & (local_north >= 0) & (local_north < rows)
    )
    return inside, jnp.where(inside, local_east * rows + local_north, -1)


def own_edges(scratch, position, near, faces, far):
    for i, value in enumerate([near] + faces + [far]):
        scratch[i] = value
    return scratch[position], scratch[position + 1]


def pair_cells(ref, i):
    cells = ref.shape[0] // 2
    return jnp.stack([ref[i], ref[cells + i]])


def x_ends(cond):
    pair, count = lax.axis_index("gx") // 2, lax.axis_size("gx") // 2
    cells = cond.shape[0]
    near = [jnp.where(pair == 0, 0.0, 2.0) * cond[0], 2.0 * cond[cells // 2]]
    far = [2.0 * cond[cells // 2 - 1], jnp.where(pair == count - 1, 0.0, 2.0) * cond[cells - 1]]
    return jnp.stack(near), jnp.stack(far)


def x_load(log_cond, storage, head, *refs):
    targets, done = refs[:6], refs[6]
    half = targets[0].shape[1]
    moves = []
    for part, some in ((1 - side(), targets[3:]), (side(), targets[:3])):
        rows = pl.ds(pl.multiple_of(part * half, half), half)
        for source, target in zip((log_cond, storage, head), some):
            moves.append(
                pltpu.make_async_copy(source.at[:, rows, :], target, done.at[len(moves)])
            )
    for move in moves:
        move.start()
    for move in moves:
        move.wait()


def make_wells(slab, rows):
    def wells(places, rates, sources):
        _, spot = local_spot(
            lax.shift_right_logical(places[...], 2 * field),
            lax.shift_right_logical(places[...], field) & mask,
            slab,
            rows,
        )
        count = rates.shape[1]
        at_row = jnp.where(
            lax.broadcasted_iota(jnp.int32, (slab * rows, count), 0) == spot, 1.0, 0.0
        ).astype(jnp.bfloat16)
        at_depth = (
            lax.broadcasted_iota(jnp.int32, (lanes, count), 0) == (places[...] & mask)
        )
        sources[...] = sum(
            lax.dot_general(
                at_row, part, (((1,), (1,)), ((), ())), preferred_element_type=f32
            )
            for part in bf16_parts(jnp.where(at_depth, rates[...], 0.0), 3)
        ).reshape(slab, rows, lanes)

    return wells


def x_prepare(log_cond, storage, head, sources, cond_own, load_own):
    cells = log_cond.shape[0]
    cond_own[...] = jnp.exp(log_cond[...])
    load_own[...] = storage[...] * head[...] + sources[pl.ds(side() * cells, cells)]


def x_reduce(cond_own, storage_own, load_own, log_cond_other, storage_other, head_other, sources,
             cond, storage, steps_ref, pair_steps, block_ref, loads):
    cells = cond_own.shape[0]
    mine, rest = pl.ds(side() * cells, cells), pl.ds((1 - side()) * cells, cells)
    cond[mine] = cond_own[...]
    storage[mine] = storage_own[...]
    loads[mine] = load_own[...]
    cond[rest] = jnp.exp(log_cond_other[...])
    storage[rest] = storage_other[...]
    loads[rest] = storage_other[...] * head_other[...] + sources[rest]
    near, far = x_ends(cond)
    conds = [pair_cells(cond, i) for i in range(cells)]
    links = [harmonic(conds[i], conds[i + 1]) for i in range(cells - 1)] + [far]
    block, steps = eliminate(
        near,
        links,
        [pair_cells(storage, i) for i in range(cells)],
        [pair_cells(loads, i) for i in range(cells)],
    )
    keep_steps(steps_ref, steps)
    joined, steps = combine([[value[i] for value in block] for i in range(2)])
    keep_steps(pair_steps, steps)
    for i, value in enumerate(joined):
        block_ref[i] = value


def facing(near, far, stride):
    return jnp.where(spot_in(stride, 2) == 0, far, near)


def make_join(stride, count, two_left):
    def join(*refs):
        arrivals, (joined_ref, steps_ref, scratch) = refs[:count], refs[count:]
        place(scratch, arrivals, stride)
        joined, steps = combine([[scratch[i, j] for j in range(5)] for i in range(count)])
        if two_left:
            _, near_ground, far_ground, near_load, far_load = joined
            joined = [
                facing(near_ground, far_ground, stride * count),
                facing(near_load, far_load, stride * count),
            ]
        for i, value in enumerate(joined):
            joined_ref[i] = value
        keep_steps(steps_ref, steps)

    return join


def descend(levels, edges, scratch):
    for stride, steps in levels[:-1]:
        faces = expand(steps, *edges)
        edges = own_edges(scratch, spot_in(stride, len(steps) + 1), edges[0], faces, edges[1])
    return edges[0], expand(levels[-1][1], *edges)[0], edges[1]


def make_top(strides, counts):
    below = len(strides) - 1

    def top(*refs):
        arrivals = refs[:counts[-1]]
        lower, (faces_ref, steps_ref, scratch, edges) = (
            refs[counts[-1]:counts[-1] + below], refs[counts[-1] + below:]
        )
        nothing = jnp.zeros(faces_ref.shape[1:], f32)
        if counts[-1] == 2:
            ground, load = [arrivals[0][i] + arrivals[1][i] for i in range(2)]
            inverse = 1.0 / ground
            steps = [(inverse, nothing, nothing, inverse * load)]
        else:
            place(scratch, arrivals, strides[-1])
            _, steps = combine([[scratch[i, j] for j in range(5)] for i in range(counts[-1])])
        keep_steps(steps_ref, steps)
        levels = [(strides[-1], steps)] + [
            (strides[i], steps_of(lower[i])) for i in reversed(range(below))
        ]
        for i, value in enumerate(descend(levels, (nothing, nothing), edges)):
            faces_ref[i] = value

    return top


def both_edges(faces):
    return jnp.stack([faces[0], faces[1]]), jnp.stack([faces[1], faces[2]])


def y_spots(ref):
    return ref.shape[1] // chunks


def y_rows(ref, spot):
    return (slice(None), pl.ds(spot, chunks, stride=y_spots(ref)), slice(None))


def y_cells(ref):
    return [ref[y_rows(ref, spot)] for spot in range(y_spots(ref))]


def y_links(cond):
    me, count = row_block(), 2 * lax.axis_size("yz")
    cells = y_cells(cond)
    place_of = lax.broadcasted_iota(jnp.int32, cells[0].shape, 1)
    near = jnp.where((place_of == 0) & (me == 0), 0.0, 2.0 * cells[0])
    far = jnp.where((place_of == chunks - 1) & (me == count - 1), 0.0, 2.0 * cells[-1])
    return cells, near, far


def by_chunk(value, scratch):
    slab = value.shape[0]
    scratch[...] = value.reshape(slab * chunks, lanes)
    return [scratch[pl.ds(i, slab, stride=chunks), :] for i in range(chunks)]


def from_chunk(values, scratch):
    slab = values[0].shape[0]
    for i, value in enumerate(values):
        scratch[pl.ds(i, slab, stride=chunks), :] = value
    return scratch[...].reshape(slab, chunks, lanes)


def y_factor(cond, storage, cell_factors, chunk_factors, ends, turned):
    conds, near, far = y_links(cond)
    links = [harmonic(before, after) for before, after in zip(conds[:-1], conds[1:])] + [far]
    nothing = [jnp.zeros_like(near)] * len(conds)
    block, steps = eliminate(near, links, y_cells(storage), nothing)
    keep_steps(cell_factors, [step[:3] for step in steps])
    parts = [by_chunk(value, turned.at[i]) for i, value in enumerate(block[:3])]
    nothing = [jnp.zeros_like(parts[0][0])] * len(parts[0])
    joined, steps = combine(list(zip(*parts, nothing, nothing)))
    keep_steps(chunk_factors, [step[:3] for step in steps])
    for i in range(3):
        ends[i] = joined[i]


def z_links(cond):
    lane = lax.broadcasted_iota(jnp.int32, cond.shape, 1)
    after = pltpu.roll(cond, lanes - 1, 1)
    return lane == lanes - 1, after


def piece_of(ref, i, cuts):
    per = ref.shape[0] // cuts
    return ref[i * per:(i + 1) * per].reshape(per * ref.shape[1], lanes)


def turn_tiles(values, target):
    values = values.reshape(target.shape)
    for i in range(target.shape[0]):
        target[i] = values[i].T


def z_factor(cond, storage, cell_factors, joints, inverse_ref, cond_up, storage_up):
    turn_tiles(cond[...], cond_up)
    turn_tiles(storage[...], storage_up)
    conds = y_cells(cond_up)
    place_of = lax.broadcasted_iota(jnp.int32, conds[0].shape, 1)
    near = jnp.where(place_of == 0, 0.0, 2.0 * conds[0])
    far = jnp.where(place_of == chunks - 1, 0.0, 2.0 * conds[-1])
    links = [harmonic(before, after) for before, after in zip(conds[:-1], conds[1:])] + [far]
    nothing = [jnp.zeros_like(near)] * len(conds)
    block, steps = eliminate(near, links, y_cells(storage_up), nothing)
    keep_steps(cell_factors, [step[:3] for step in steps])
    link = pltpu.roll(block[0], chunks - 1, 1)
    ground = block[2] + pltpu.roll(block[1], chunks - 1, 1)
    ground = jnp.where(place_of == chunks - 1, 1.0, ground)
    for level in range(chunks.bit_length() - 1):
        shift = 1 << level
        link_back = pltpu.roll(link, shift, 1)
        inverse = 1.0 / (link + link_back + ground)
        passed, held = inverse * link, inverse * ground
        joints[level, 0] = pltpu.roll(passed, shift, 1)
        joints[level, 1] = link * pltpu.roll(inverse, chunks - shift, 1)
        ground = (
            ground
            + link * pltpu.roll(held, chunks - shift, 1)
            + link_back * pltpu.roll(held, shift, 1)
        )
        link = link * pltpu.roll(passed, chunks - shift, 1)
    inverse_ref[...] = 1.0 / ground


def z_sweep(loads, cell_factors, joints, inverse, solved):
    factors = factors_of(cell_factors)
    near, far, scaled = eliminate_loads(factors, y_cells(loads))
    load = far + pltpu.roll(near, chunks - 1, 1)
    for level in range(joints.shape[0]):
        shift = 1 << level
        load = (
            load
            + joints[level, 1] * pltpu.roll(load, chunks - shift, 1)
            + joints[level, 0] * pltpu.roll(load, shift, 1)
        )
    far = load * inverse[...]
    near = pltpu.roll(far, 1, 1)
    for spot, value in enumerate(expand(with_scaled(factors, scaled), near, far)):
        solved[y_rows(solved, spot)] = value


def make_points(slab, rows):
    def points(east, north, depth, heads, at_row, at_depth, here, observed):
        inside, spot = local_spot(east[...], north[...], slab, rows)
        at_row[...] = jnp.where(
            lax.broadcasted_iota(jnp.int32, at_row.shape, 0) == spot, 1.0, 0.0
        ).astype(jnp.bfloat16)
        at_depth[...] = jnp.where(
            lax.broadcasted_iota(jnp.int32, at_depth.shape, 0) == depth[...], 1.0, 0.0
        )
        here[...] = jnp.where(inside, 1.0, 0.0)
        observed[...] = heads[...]

    return points


def y_forward(x_faces, x_steps, storage, cell_factors, chunk_factors, ends,
              head_first, scaled_cells, scaled_chunks, message, loads, turned):
    cells = head_first.shape[0] // 2
    near, far = both_edges(x_faces)
    for i in reversed(range(cells)):
        far = x_steps[i, 3] + x_steps[i, 1] * near + x_steps[i, 2] * far
        for j in range(2):
            head_first[j * cells + i] = far[j]
            loads[j * cells + i] = storage[j * cells + i] * far[j]
    for i in range(3):
        message[i] = ends[i]
    near, far = y_loads(loads, cell_factors, chunk_factors, scaled_cells, scaled_chunks, turned)
    message[3] = near
    message[4] = far


def y_loads(loads, cell_factors, chunk_factors, scaled_cells, scaled_chunks, turned):
    near, far, scaled = eliminate_loads(
        factors_of(cell_factors), y_cells(loads)
    )
    for i, value in enumerate(scaled):
        scaled_cells[i] = value
    blocks = list(zip(by_chunk(near, turned.at[0]), by_chunk(far, turned.at[1])))
    joined, scaled = combine_loads(blocks, factors_of(chunk_factors))
    for i, value in enumerate(scaled):
        scaled_chunks[i] = value
    return joined


def y_expand(near, far, cell_factors, chunk_factors, scaled_cells, scaled_chunks,
             turned, solved, edges, natural):
    factors = factors_of(chunk_factors)
    steps = with_scaled(factors, [scaled_chunks[i] for i in range(len(factors))])
    faces = [near] + expand(steps, near, far) + [far]
    near = from_chunk(faces[:-1], turned.at[0])
    far = from_chunk(faces[1:], turned.at[1])
    edges[0] = near
    edges[1] = far
    for spot in reversed(range(y_spots(natural))):
        far = scaled_cells[spot] + cell_factors[spot, 1] * near + cell_factors[spot, 2] * far
        solved[spot] = far
        natural[y_rows(natural, spot)] = far


def make_z(count):
    def z_solve(*refs):
        arrivals = refs[:count]
        (cell_factors, chunk_factors, scaled_cells, scaled_chunks, storage,
         z_factors, joints, inverse, at_row, at_depth, here, observed,
         y_factors, head_second, y_edges, head_up, adjoint_third, message,
         next_cells, next_chunks,
         scratch, edges, turned, loads, second) = refs[count:]
        me = row_block()
        for turn, arrival in enumerate(arrivals):
            scratch[me ^ turn] = arrival[...]
        nothing = jnp.zeros(arrivals[0].shape[1:], f32)
        _, steps = combine([[scratch[i, j] for j in range(5)] for i in range(count)])
        keep_steps(y_factors, [step[:3] for step in steps])
        near, far = own_edges(edges, me, nothing, expand(steps, nothing, nothing), nothing)
        y_expand(near, far, cell_factors, chunk_factors, scaled_cells, scaled_chunks,
                 turned, head_second, y_edges, second)

        slab = storage.shape[0]
        turn_tiles(storage[...] * second[...], loads)
        tiles = loads.shape[0]
        z_sweep(loads, z_factors, joints, inverse, head_up)
        found = jnp.dot(
            jnp.concatenate(
                bf16_parts(jnp.concatenate([head_up[i] for i in range(tiles)], axis=1), 2), axis=0
            ),
            at_row[...],
            preferred_element_type=f32,
        )
        found = jnp.sum(
            at_depth[...] * (found[:lanes] + found[lanes:]), axis=0, keepdims=True
        )
        misfit = here[...] * (found - observed[...])
        for i in range(misfit.shape[1] // lanes):
            row = 2 * slab + i
            message[row:row + 1, :] = misfit[:, i * lanes:(i + 1) * lanes]
        parts = [
            (at_depth[...] * part.astype(f32)).astype(jnp.bfloat16)
            for part in bf16_parts(misfit_weight * misfit, 2)
        ]
        source = lax.dot_general(
            jnp.concatenate(parts, axis=0), at_row[...],
            (((1,), (1,)), ((), ())), preferred_element_type=f32,
        )
        for i in range(tiles):
            tile = slice(i * lanes, (i + 1) * lanes)
            loads[i] = source[:lanes, tile] + source[lanes:, tile]
        z_sweep(loads, z_factors, joints, inverse, loads)
        adjoint_third[...] = jnp.stack([loads[i].T for i in range(tiles)]).reshape(second.shape)
        second[...] = storage[...] * adjoint_third[...]
        near, far = y_loads(second, cell_factors, chunk_factors, next_cells, next_chunks, turned)
        message[:slab] = near
        message[slab:2 * slab] = far

    return z_solve


def lay_head(head_up, head_third, head_send):
    cells = head_send.shape[0]
    tiles = head_up.shape[0]
    head_third[...] = jnp.stack([head_up[i].T for i in range(tiles)]).reshape(head_third.shape)
    head_send[...] = head_third[pl.ds((1 - side()) * cells, cells)]


def make_y_back(count):
    def y_back(*refs):
        arrivals = refs[:count]
        (y_factors, cell_factors, chunk_factors, scaled_cells, scaled_chunks, storage, x_steps,
         pair_steps, adjoint_second, y_edges, scaled_x, pair_scaled, note,
         scratch, edges, turned, second) = refs[count:]
        me, slab = row_block(), storage.shape[0]
        misfit = None
        for turn, arrival in enumerate(arrivals):
            scratch[me ^ turn, 0] = arrival[:slab]
            scratch[me ^ turn, 1] = arrival[slab:2 * slab]
            part = arrival[2 * slab:]
            misfit = part if misfit is None else misfit + part
        nothing = jnp.zeros(scratch.shape[2:], f32)
        factors = factors_of(y_factors)
        _, scaled = combine_loads([[scratch[i, 0], scratch[i, 1]] for i in range(count)], factors)
        faces = expand(with_scaled(factors, scaled), nothing, nothing)
        near, far = own_edges(edges, me, nothing, faces, nothing)
        y_expand(near, far, cell_factors, chunk_factors, scaled_cells, scaled_chunks,
                 turned, adjoint_second, y_edges, second)
        near, far, scaled = eliminate_loads(
            factors_of(x_steps),
            [pair_cells(storage, i) * pair_cells(second, i) for i in range(slab // 2)],
        )
        for i, value in enumerate(scaled):
            scaled_x[i] = value
        (near, far), scaled = combine_loads(
            [[near[i], far[i]] for i in range(2)], factors_of(pair_steps)
        )
        pair_scaled[0] = scaled[0]
        rows = near.shape[0]
        note[:rows] = near
        note[rows:2 * rows] = far
        note[2 * rows:] = misfit

    return y_back


def make_terms(cuts):
    def gather_terms(cond, head_third, adjoint_third, head_second, adjoint_second,
                     head_edges, adjoint_edges, terms, natural):
        conds, near_link, far_link = y_links(cond)
        from_left = (
            -near_link * (adjoint_second[0] - adjoint_edges[0]) * (head_second[0] - head_edges[0])
        )
        spots = len(conds)
        for spot in range(spots):
            if spot < spots - 1:
                to_left, to_right = face_gradient(
                    conds[spot], conds[spot + 1],
                    adjoint_second[spot] - adjoint_second[spot + 1],
                    head_second[spot] - head_second[spot + 1],
                )
            else:
                to_left = (
                    -far_link * (adjoint_second[spot] - adjoint_edges[1])
                    * (head_second[spot] - head_edges[1])
                )
            natural[y_rows(natural, spot)] = from_left + to_left
            from_left = to_right
        slab, rows, _ = cond.shape
        per = slab // cuts
        for i in range(cuts):
            here, head, adjoint = [
                piece_of(ref, i, cuts) for ref in (cond, head_third, adjoint_third)
            ]
            last, after = z_links(here)
            to_left, to_right = face_gradient(
                here, after,
                adjoint - pltpu.roll(adjoint, lanes - 1, 1),
                head - pltpu.roll(head, lanes - 1, 1),
            )
            to_left = jnp.where(last, 0.0, to_left)
            to_right = jnp.where(last, 0.0, to_right)
            value = (to_left + pltpu.roll(to_right, 1, 1)).reshape(per, rows, lanes)
            terms[i * per:(i + 1) * per] = value + natural[i * per:(i + 1) * per]

    return gather_terms


def loads_in(arrivals, scratch, stride):
    rows, count = scratch.shape[2], len(arrivals)
    misfit = None
    for turn, arrival in enumerate(arrivals):
        position = spot_in(stride, count) ^ turn
        scratch[position, 0] = arrival[:rows]
        scratch[position, 1] = arrival[rows:2 * rows]
        part = arrival[2 * rows:]
        misfit = part if misfit is None else misfit + part
    return [[scratch[i, 0], scratch[i, 1]] for i in range(count)], misfit


def make_join_loads(stride, count, two_left):
    def join(*refs):
        arrivals, (steps_ref, message, scaled_ref, scratch) = refs[:count], refs[count:]
        blocks, misfit = loads_in(arrivals, scratch, stride)
        joined, scaled = combine_loads(blocks, factors_of(steps_ref))
        rows = scratch.shape[2]
        if two_left:
            message[:rows] = facing(*joined, stride * count)
            message[rows:] = misfit
        else:
            message[:rows] = joined[0]
            message[rows:2 * rows] = joined[1]
            message[2 * rows:] = misfit
        for i, value in enumerate(scaled):
            scaled_ref[i] = value

    return join


def make_top_loads(strides, counts):
    below = len(strides) - 1

    def top(*refs):
        arrivals, refs = refs[:counts[-1]], refs[counts[-1]:]
        top_steps, lower, lower_scaled = refs[0], refs[1:1 + below], refs[1 + below:1 + 2 * below]
        faces_ref, misfit_ref, scratch, edges = refs[1 + 2 * below:]
        nothing = jnp.zeros(scratch.shape[2:], f32)
        factors = factors_of(top_steps)
        if counts[-1] == 2:
            rows = nothing.shape[0]
            total = arrivals[0][...] + arrivals[1][...]
            scaled, misfit = [factors[0][0] * total[:rows]], total[rows:]
        else:
            blocks, misfit = loads_in(arrivals, scratch, strides[-1])
            scaled = combine_loads(blocks, factors)[1]
        levels = [(strides[-1], with_scaled(factors, scaled))]
        for i in reversed(range(below)):
            factors = factors_of(lower[i])
            scaled = [lower_scaled[i][j] for j in range(len(factors))]
            levels.append((strides[i], with_scaled(factors, scaled)))
        misfit_ref[...] = misfit
        for i, value in enumerate(descend(levels, (nothing, nothing), edges)):
            faces_ref[i] = value

    return top


def x_back(faces, head_faces, x_steps, scaled_x, cond, head, terms, own, send, gradient):
    cells = cond.shape[0] // 2
    near, far = both_edges(faces)
    head_near, head_far = both_edges(head_faces)
    near_link, far_link = x_ends(cond)
    conds = [pair_cells(cond, i) for i in range(cells)]
    heads = [pair_cells(head, i) for i in range(cells)]
    adjoint = [None] * cells
    after = far
    for i in reversed(range(cells)):
        after = scaled_x[i] + x_steps[i, 1] * near + x_steps[i, 2] * after
        adjoint[i] = after
    from_left = -near_link * (adjoint[0] - near) * (heads[0] - head_near)
    for i in range(cells):
        if i < cells - 1:
            to_left, to_right = face_gradient(
                conds[i], conds[i + 1], adjoint[i] - adjoint[i + 1], heads[i] - heads[i + 1]
            )
        else:
            to_left = -far_link * (adjoint[i] - far) * (heads[i] - head_far)
        value = from_left + to_left
        for j in range(2):
            gradient[j * cells + i] = terms[j * cells + i] + value[j]
        from_left = to_right
    own[...] = gradient[pl.ds(side() * cells, cells)]
    send[...] = gradient[pl.ds((1 - side()) * cells, cells)]


def settle(own, other, whole):
    cells, half, _ = other.shape
    start = (own.shape[0] - cells) // cells * side() * cells
    whole[:, pl.ds(pl.multiple_of(side() * half, half), half), :] = own[pl.ds(start, cells)]
    whole[:, pl.ds(pl.multiple_of((1 - side()) * half, half), half), :] = other[...]


def settle_last(own, other, misfits, whole, misfits_out):
    misfits_out[...] = misfits[...]
    settle(own, other, whole)


def shards(log_cond, storage, head, well_east, well_north, well_depth, pump_rates,
           probe_east, probe_north, probe_depth, probe_heads):
    cells, rows, _ = log_cond.shape
    devices, columns = lax.axis_size("gx"), lax.axis_size("yz")
    inner = 4 if devices >= 16 else 2
    strides, counts = [1, 2, 2 * inner], [2, inner, devices // (2 * inner)]
    two_left = counts[-1] == 2
    slab, half = 2 * cells, rows // 2
    points = probe_heads.shape[0]
    grid = (slab, half, lanes)
    plane = (half, lanes)
    spots = half // chunks
    cell = (spots, slab, chunks, lanes)
    line = (slab, lanes)
    turned = (slab * chunks, lanes)

    places = ((well_east << (2 * field)) + (well_north << field) + well_depth).reshape(1, -1)
    probes = [value.reshape(1, -1) for value in (probe_east, probe_north, probe_depth, probe_heads)]
    parts = run(
        x_load,
        [(cells,) + plane] * 6,
        [log_cond, storage, head],
        [pltpu.SemaphoreType.DMA((6,))],
        raw=3,
        limit=53,
    )
    (sources,) = run(
        make_wells(slab, half), [grid], [places, jnp.where(places >= 0, pump_rates.reshape(1, -1), 0.0)], after=[parts[3]]
    )
    cond_own, load_own = run(
        x_prepare, [(cells,) + plane] * 2, list(parts[:3]) + [sources], after=[parts[3]]
    )
    cond, storage, x_steps, pair_steps, joined = run(
        x_reduce,
        [grid, grid, (cells, 4, 2) + plane, (1, 4) + plane, (5,) + plane],
        [cond_own, parts[1], load_own] + [swap(part) for part in parts[3:]] + [sources],
        [(grid, f32)],
    )
    x_levels = [pair_steps]
    cell_factors, chunk_factors, ends = run(
        y_factor,
        [(spots, 3) + cell[1:], (chunks - 1, 3) + line, (3,) + line],
        [cond, storage],
        [((3,) + turned, f32)],
        after=[joined],
    )

    cuts = 4
    tiles = slab * half // lanes
    upright = (tiles, lanes, lanes)
    z_cell = (tiles, chunks, lanes)
    for i, (stride, count) in enumerate(zip(strides[1:], counts[1:])):
        arrivals = exchange(joined, stride, count)
        waits = []
        if i == 0:
            z_factors, joints, inverse = run(
                z_factor,
                [(lanes // chunks, 3) + z_cell, (chunks.bit_length() - 1, 2) + z_cell, z_cell],
                [cond, storage],
                [(upright, f32), (upright, f32)],
                after=[joined],
            )
            waits = [ends, inverse]
        if i < len(strides) - 2:
            joined, steps = run(
                make_join(stride, count, i == len(strides) - 3 and two_left),
                [(2 if i == len(strides) - 3 and two_left else 5,) + plane,
                 (count - 1, 4) + plane],
                arrivals,
                [((count, 5) + plane, f32)],
                after=waits,
            )
            x_levels.append(steps)
    x_faces, steps = run(
        make_top(strides, counts),
        [(3,) + plane, (counts[-1] - 1, 4) + plane],
        arrivals + x_levels,
        [((counts[-1], 5) + plane, f32), ((max(counts) + 1,) + plane, f32)],
        after=waits,
    )
    x_levels.append(steps)
    head_first, scaled_cells, scaled_chunks, message = run(
        y_forward,
        [grid, cell, (chunks - 1,) + line, (5,) + line],
        [x_faces, x_steps, storage, cell_factors, chunk_factors, ends],
        [(grid, f32), ((2,) + turned, f32)],
    )
    at_row, at_depth, here, observed = run(
        make_points(slab, half),
        [((slab * half, points), jnp.bfloat16), (lanes, points), (1, points), (1, points)],
        probes,
        after=[message],
    )
    extra, blocks = points // lanes, 2 * columns
    (y_factors, head_second, head_edges, head_up, adjoint_third, message,
     scaled_cells, scaled_chunks) = run(
        make_z(blocks),
        [(blocks - 1, 3) + line, cell, (2,) + cell[1:], upright, grid,
         (2 * slab + extra, lanes), cell, (chunks - 1,) + line],
        exchange_rows(message)
        + [cell_factors, chunk_factors, scaled_cells, scaled_chunks, storage,
           z_factors, joints, inverse, at_row, at_depth, here, observed],
        [((blocks, 5) + line, f32), ((blocks + 1,) + line, f32), ((2,) + turned, f32),
         (upright, f32), (grid, f32)],
    )
    head_third, head_send = run(
        lay_head, [grid, (cells,) + plane], [head_up], after=[message]
    )
    note = (2 * half + extra, lanes)
    adjoint_second, adjoint_edges, scaled_x, scaled, message = run(
        make_y_back(blocks),
        [cell, (2,) + cell[1:], (cells, 2) + plane, (1,) + plane, note],
        exchange_rows(message)
        + [y_factors, cell_factors, chunk_factors, scaled_cells, scaled_chunks, storage, x_steps,
           pair_steps],
        [((blocks, 2) + line, f32), ((blocks + 1,) + line, f32), ((2,) + turned, f32),
         (grid, f32)],
    )
    x_scaled = [scaled]
    (terms,) = run(
        make_terms(cuts),
        [grid],
        [cond, head_third, adjoint_third, head_second, adjoint_second, head_edges, adjoint_edges],
        [(grid, f32)],
    )
    for i in range(1, len(strides) - 1):
        arrivals = exchange(message, strides[i], counts[i])
        message, scaled = run(
            make_join_loads(strides[i], counts[i], i == len(strides) - 2 and two_left),
            [(half + extra, lanes) if i == len(strides) - 2 and two_left else note,
             (counts[i] - 1,) + plane],
            arrivals + [x_levels[i]],
            [((counts[i], 2) + plane, f32)],
        )
        x_scaled.append(scaled)
    faces, misfits = run(
        make_top_loads(strides, counts),
        [(3,) + plane, (extra, lanes)],
        exchange(message, strides[-1], counts[-1]) + x_levels[-1:] + x_levels[:-1] + x_scaled,
        [((counts[-1], 2) + plane, f32), ((max(counts) + 1,) + plane, f32)],
        after=[terms],
    )
    whole = (cells, rows, lanes)
    (head_next,) = run(settle, [whole], [head_third, swap(head_send)])
    own, send = run(
        x_back,
        [(cells,) + plane, (cells,) + plane],
        [faces, x_faces, x_steps, scaled_x, cond, head_first, terms],
        [(grid, f32)],
    )
    gradient, misfits = run(
        settle_last, [whole, (extra, lanes)], [own, swap(send), misfits]
    )
    return head_next, gradient, misfits.reshape(-1)


def solution(mesh):
    cells = P("gx", "yz", None)
    return jax.shard_map(
        shards,
        mesh=mesh,
        in_specs=(cells, cells, cells) + (P(),) * 8,
        out_specs=(cells, cells, P()),
        check_vma=False,
    )
```
